256 devices in a mesh: section: 4 (over z_lo), ch: 16 (over x, z_hi, core), slab: 4 (over y).
Axes of the slice: x: 4, y: 4, z: 8 (z_hi: 2, z_lo: 4; z = z_hi * 4 + z_lo), core: 2. Of those that a mesh axis runs over, the one named last changes fastest.
Arguments:
- x_in: bfloat16 [4, 384, 32, 128], P(None, 'ch', 'slab'), may hold values from -6 to 6
- cot: bfloat16 [4, 384, 32, 128], P(None, 'ch', 'slab'), may hold values from -0.125 to 0.125
- w1: bfloat16 [4, 9, 384, 384], P('section', None, 'ch'), may hold values from -0.109375 to 0.109375
- gain: float32 [4, 384], P('section'), may hold values from 0.5 to 1.5
Outputs:
- weight_grad: float32 [4, 9, 384, 384], P('section', None, 'ch')
- gain_grad: float32 [4, 384], P('section', 'ch')
The draws below stay inside these ranges and needn't reach their ends.
All inputs are finite; a program needn't handle non-finite values.
Results may differ from the reference program's by a relative error of at most 0.034.
Values may be sent and summed in bfloat16 or wider, within the bound.
No kernel may reach another device: no remote copies, remote signals or barrier semaphores. Data moves between devices by JAX's collectives and lax.ppermute only.
A program may use at most 128 MiB of HBM per device.

```python
import jax
import jax.numpy as jnp
from jax import lax

C = 384
H_DEV = 8
W = 128
MB = 4
H = 32
N_SECTION = 4


def block_levels(key, extent, shards, low, top_value):
    loudness = 1.0
    for position, blocks in shards:
        steps = jax.random.uniform(jax.random.fold_in(jax.random.fold_in(key, 6), position), (blocks,), jnp.float32, low / len(shards), top_value / len(shards))
        loudness = loudness * jnp.repeat(jnp.exp(steps), extent[position] // blocks).reshape((-1,) + (1,) * (len(extent) - 1 - position))
    return loudness


def normal_values(own_key, extent, spread, limit, cuts=(), dtype=jnp.bfloat16):
    level = block_levels(own_key, extent, cuts, -0.22, 0.18) if cuts else 1.0
    result = jax.random.normal(own_key, extent, jnp.float32) * spread * level
    return jnp.minimum(jnp.maximum(result, -limit), limit).astype(dtype)


def setup_inputs(seed: int = 0) -> dict:
    key_of = jax.random.split(jax.random.key(seed), 5)
    return {
        "x_in": normal_values(key_of[0], (MB, C, H, W), 1.0, 6.0, ((1, 16), (2, 4))),
        "cot": normal_values(key_of[1], (MB, C, H, W), ((MB * H * W) ** -0.5), 0.125, ((1, 16), (2, 4))),
        "w1": normal_values(key_of[2], (N_SECTION, 9, C, C), (9 * C) ** -0.5, 0.109375, ((0, 4), (2, 16))),
        "gain": jnp.clip(1.0 + 0.1 * jax.random.normal(key_of[3], (N_SECTION, C), jnp.float32), 0.5, 1.5),
    }


NORM_EPS = 1e-05
SLOPE_SCALE = 0.7978845608028654
CUBIC_COEF = 0.044715

def gelu_value(pre_act):
    inner_arg = SLOPE_SCALE * (pre_act + CUBIC_COEF * pre_act * pre_act * pre_act)
    return 0.5 * pre_act * (1.0 + jnp.tanh(inner_arg))

def gelu_slope(pre_act):
    inner_arg = SLOPE_SCALE * (pre_act + CUBIC_COEF * pre_act * pre_act * pre_act)
    tangent = jnp.tanh(inner_arg)
    return 0.5 * (1.0 + tangent) + 0.5 * pre_act * (1.0 - tangent * tangent) * SLOPE_SCALE * (1.0 + 3.0 * CUBIC_COEF * pre_act * pre_act)

def displaced(source, row_shift, col_shift):
    reach_cells = max(abs(row_shift), abs(col_shift))
    padded = jnp.pad(source, ((0, 0), (reach_cells, reach_cells), (reach_cells, reach_cells)))
    row_count = source.shape[1]
    col_count = source.shape[2]
    return padded[:, reach_cells + row_shift:reach_cells + row_shift + row_count, reach_cells + col_shift:reach_cells + col_shift + col_count]

def block_forward(inputs_here, weight, gain_row, dilation):
    all_chans = inputs_here.shape[0]
    pixels = inputs_here.shape[1] * inputs_here.shape[2]
    values = inputs_here.astype(jnp.float32)
    pix_mean = lax.optimization_barrier(jnp.mean(values, axis=0))
    pix_rstd = lax.rsqrt(lax.optimization_barrier(jnp.mean(values * values, axis=0)) - pix_mean * pix_mean + NORM_EPS)
    standard = (values - pix_mean) * pix_rstd
    normed = (standard * gain_row[:, None, None]).astype(jnp.bfloat16)
    running = jnp.zeros((all_chans, pixels), jnp.float32)
    for tap_index in range(9):
        row_shift = (tap_index // 3 - 1) * dilation
        col_shift = (tap_index % 3 - 1) * dilation
        tap_slab = displaced(normed, row_shift, col_shift).reshape(all_chans, pixels)
        running = running + jnp.dot(weight[tap_index], tap_slab, preferred_element_type=jnp.float32)
    pre_act = running.reshape(inputs_here.shape)
    block_out = (values + gelu_value(pre_act)).astype(jnp.bfloat16)
    return (block_out, (normed, standard, pix_rstd, pre_act))

def block_backward(grad_out, weight, gain_row, dilation, saved):
    normed, standard, pix_rstd, pre_act = saved
    all_chans = normed.shape[0]
    pixels = normed.shape[1] * normed.shape[2]
    slope_grad = (grad_out.astype(jnp.float32) * gelu_slope(pre_act)).astype(jnp.bfloat16)
    flat_grad = slope_grad.reshape(all_chans, pixels)
    tap_terms = []
    running = jnp.zeros((all_chans, pixels), jnp.float32)
    for tap_index in range(9):
        row_shift = (tap_index // 3 - 1) * dilation
        col_shift = (tap_index % 3 - 1) * dilation
        tap_slab = displaced(normed, row_shift, col_shift).reshape(all_chans, pixels)
        tap_terms.append(jnp.dot(flat_grad, tap_slab.T, preferred_element_type=jnp.float32))
        back_slab = displaced(slope_grad, -row_shift, -col_shift).reshape(all_chans, pixels)
        running = running + jnp.dot(weight[tap_index].T, back_slab, preferred_element_type=jnp.float32)
    input_grad = running.reshape(normed.shape)
    gain_term = lax.optimization_barrier(jnp.sum(input_grad * standard, axis=(1, 2)))
    scaled = input_grad * gain_row[:, None, None]
    grad_mean = lax.optimization_barrier(jnp.mean(scaled, axis=0))
    grad_cross = lax.optimization_barrier(jnp.mean(scaled * standard, axis=0))
    grad_in = (grad_out.astype(jnp.float32) + pix_rstd * (scaled - grad_mean - standard * grad_cross)).astype(jnp.bfloat16)
    return (grad_in, jnp.stack(tap_terms), gain_term)

def reference(x_in, cot, w1, gain):
    weight_grad = jnp.zeros(w1.shape, jnp.float32)
    gain_grad = jnp.zeros(gain.shape, jnp.float32)
    for batch_index in range(MB):
        inputs_here = x_in[batch_index]
        saves = []
        for section_num in range(N_SECTION):
            dilation = H_DEV // 2 ** (N_SECTION - 1 - section_num)
            inputs_here, saved = block_forward(inputs_here, w1[section_num], gain[section_num], dilation)
            saves.append(saved)
        grad_now = cot[batch_index]
        for section_num in reversed(range(N_SECTION)):
            dilation = H_DEV // 2 ** (N_SECTION - 1 - section_num)
            grad_now, weight_term, gain_term = block_backward(grad_now, w1[section_num], gain[section_num], dilation, saves[section_num])
            weight_grad = weight_grad.at[section_num].add(weight_term)
            gain_grad = gain_grad.at[section_num].add(gain_term)
    return (weight_grad, gain_grad)
```

```python
import functools

import jax
import jax.numpy as jnp
import numpy as np
from jax import lax
from jax.experimental import pallas as pl
from jax.experimental.pallas import tpu as pltpu
from jax.sharding import Mesh, PartitionSpec as P

NORM_EPS = 1e-05
SLOPE_SCALE = 0.7978845608028654
CUBIC_COEF = 0.044715
BF = jnp.bfloat16
F32 = jnp.float32

ROWS = 32
CHANS = 384
HALF = 192
TAPS = 9
DIL = (1, 2, 4, 8)
OWN = 16
XWIN = 80
CWIN = 48
PAD = 8
X_WIN = ((0, 80), (0, 80), (0, 80), (8, 64), (16, 48))
S_WIN = ((32, 16), (24, 32), (24, 32), (16, 48))
VMEM_LIMIT = 56 * 1024 * 1024
PARAMS = pltpu.CompilerParams(vmem_limit_bytes=VMEM_LIMIT)
NT = (((1,), (1,)), ((), ()))
NN = (((1,), (0,)), ((), ()))


def dot(a, b, dims):
    return lax.dot_general(a, b, dims, preferred_element_type=F32)


def call(kernel, out_shape, scratch, args, smem=()):
    vm = pl.BlockSpec(memory_space=pltpu.VMEM)
    sm = pl.BlockSpec(memory_space=pltpu.SMEM)
    return pl.pallas_call(
        kernel,
        out_shape=out_shape,
        in_specs=[sm if i in smem else vm for i in range(len(args))],
        out_specs=jax.tree.map(lambda _: vm, out_shape),
        scratch_shapes=scratch,
        compiler_params=PARAMS,
    )(*args)


def shape(dims, dtype):
    return jax.ShapeDtypeStruct(dims, dtype)


def row_loop(body, unroll=4):
    def step(i, carry):
        for k in range(unroll):
            body(i * unroll + k)
        return carry

    lax.fori_loop(0, ROWS // unroll, step, 0)


def in_image(base, first, count, width):
    cols = lax.broadcasted_iota(jnp.int32, (count, HALF), 0) + (base - 32 + first)
    return (cols >= 0) & (cols < width)


def stats(xo, xt):
    mean = (jnp.sum(xo, axis=1, keepdims=True) + jnp.sum(xt, axis=1, keepdims=True)) / CHANS
    square = (
        jnp.sum(xo * xo, axis=1, keepdims=True) + jnp.sum(xt * xt, axis=1, keepdims=True)
    ) / CHANS
    return mean, lax.rsqrt(square - mean * mean + NORM_EPS)


def gelu_parts(pre):
    tangent = jnp.tanh(SLOPE_SCALE * (pre + CUBIC_COEF * pre * pre * pre))
    value = 0.5 * pre * (1.0 + tangent)
    slope = 0.5 * (1.0 + tangent) + 0.5 * pre * (1.0 - tangent * tangent) * SLOPE_SCALE * (
        1.0 + 3.0 * CUBIC_COEF * pre * pre
    )
    return value, slope


def prep_kernel(w_ref, perm_ref, out_ref):
    for t in range(TAPS):
        out_ref[:, t * CHANS : (t + 1) * CHANS] = dot(w_ref[t], perm_ref[...], NN).astype(BF)


def assemble_kernel(slabs, rows, recv_ref, x_ref, cot_ref):
    lanes = XWIN + CWIN
    eye = (
        lax.broadcasted_iota(jnp.int32, (lanes, lanes), 0)
        == lax.broadcasted_iota(jnp.int32, (lanes, lanes), 1)
    ).astype(F32).astype(BF)

    def one(r, carry):
        for y in range(slabs):
            piece = recv_ref[:, y, pl.ds(r, 1)].astype(F32)
            piece = piece.reshape(HALF, lanes).astype(BF)
            flipped = dot(eye, piece, NT).astype(BF)
            x_ref[pl.ds(y * rows + r, 1)] = flipped[:XWIN].reshape(1, XWIN, HALF)
            cot_ref[pl.ds(y * rows + r, 1)] = flipped[XWIN:].reshape(1, CWIN, HALF)
        return carry

    lax.fori_loop(0, rows, one, 0)


def norm_phase(block, xo_ref, xt_ref, gain_ref, nbuf, nk):
    d = DIL[block]
    first_in, width_in = X_WIN[block]
    first_out, width_out = X_WIN[block + 1]
    low = first_out - first_in
    own = 32 - first_in
    for edge in (0, PAD + ROWS):
        nbuf[edge : edge + PAD] = jnp.zeros((PAD, width_out, 3 * CHANS), BF)
        nk[edge : edge + PAD] = jnp.zeros((PAD, OWN, 3 * CHANS), BF)
    gain = gain_ref[...]

    def one(r):
        xo = xo_ref[r].astype(F32)
        xt = xt_ref[r].astype(F32)
        mean, rstd = stats(xo, xt)
        both = jnp.concatenate([(xo - mean) * rstd, (xt - mean) * rstd], axis=1) * gain
        for kx in range(3):
            shift = (-(kx - 1) * d) % width_in
            moved = pltpu.roll(both, shift, 0) if shift else both
            lanes = slice(kx * CHANS, (kx + 1) * CHANS)
            nbuf[PAD + r, :, lanes] = moved[low : low + width_out].astype(BF)
            nk[PAD + r, :, lanes] = moved[own : own + OWN].astype(BF)

    row_loop(one, 2)


def conv_phase(block, nbuf, w_ref, pre):
    d = DIL[block]
    width = X_WIN[block + 1][1]
    step = 8

    def one(i, carry):
        r0 = i * step
        acc = None
        for ky in range(3):
            left = nbuf[pl.ds(PAD + r0 + (ky - 1) * d, step)].reshape(step * width, 3 * CHANS)
            term = dot(left, w_ref[:, ky * 3 * CHANS : (ky + 1) * 3 * CHANS], NT)
            acc = term if acc is None else acc + term
        pre[pl.ds(r0, step)] = acc.reshape(step, width, HALF)
        return carry

    lax.fori_loop(0, ROWS // step, one, 0)


def forward_kernel(block, image, idx_ref, xo_ref, xt_ref, w_ref, gain_ref, y_ref, d_ref, nk, nbuf, pre):
    first_in = X_WIN[block][0]
    first_out, width_out = X_WIN[block + 1]
    first_s, width_s = S_WIN[block]
    norm_phase(block, xo_ref, xt_ref, gain_ref, nbuf, nk)
    conv_phase(block, nbuf, w_ref, pre)
    live = in_image(idx_ref[0], first_out, width_out, image)
    low, at = first_out - first_in, first_s - first_out

    def one(r):
        value, slope = gelu_parts(pre[r])
        out = xo_ref[r].astype(F32)[low : low + width_out] + value
        y_ref[r] = jnp.where(live, out, 0.0).astype(BF)
        d_ref[r] = slope[at : at + width_s]

    row_loop(one, 2)


def scatter_s(block, s, r, sbuf, sown):
    first, width = S_WIN[block]
    sown[r] = s[32 - first : 32 - first + OWN].astype(BF)
    if sbuf is None:
        return
    d = DIL[block]
    first_q, width_q = S_WIN[block - 1]
    low = first_q - first
    gap = jnp.zeros((width_q, 256 - HALF), F32)
    for kx in range(3):
        shift = ((kx - 1) * d) % width
        moved = (pltpu.roll(s, shift, 0) if shift else s)[low : low + width_q]
        sbuf[PAD + r, :, kx * 256 : (kx + 1) * 256] = jnp.concatenate([moved, gap], axis=1).astype(BF)


def q_phase(block, sbuf, w_ref, wq, q_ref):
    d = DIL[block]
    width = S_WIN[block - 1][1]
    for ky in range(3):
        for kx in range(3):
            t = 3 * ky + kx
            wq[ky, kx * 256 : kx * 256 + HALF] = w_ref[:, t * CHANS : (t + 1) * CHANS]
            wq[ky, kx * 256 + HALF : (kx + 1) * 256] = jnp.zeros((256 - HALF, CHANS), BF)
    for edge in (0, PAD + ROWS):
        sbuf[edge : edge + PAD] = jnp.zeros((PAD, width, 768), BF)
    step = 512 // width

    def one(i, carry):
        r0 = i * step
        acc = None
        for ky in range(3):
            left = sbuf[pl.ds(PAD + r0 - (ky - 1) * d, step)].reshape(step * width, 768)
            term = dot(left, wq[ky], NN)
            acc = term if acc is None else acc + term
        q_ref[0, pl.ds(r0, step)] = acc[:, HALF:].reshape(step, width, HALF).astype(BF)
        q_ref[1, pl.ds(r0, step)] = acc[:, :HALF].reshape(step, width, HALF).astype(BF)
        return carry

    lax.fori_loop(0, ROWS // step, one, 0)


def weight_phase(block, dims, idx_ref, sown, nk, w_ref, gain_ref, wg_ref):
    own_chans, share, lines = dims
    d = DIL[block]
    count = (HALF // own_chans) * lines
    bits = lines.bit_length() - 1
    line = lax.broadcasted_iota(jnp.int32, (count, HALF), 0)
    place = jnp.bitwise_and(line, lines - 1)
    want = jnp.right_shift(line, bits) * own_chans + share * idx_ref[1] + place
    pick = (lax.broadcasted_iota(jnp.int32, (count, HALF), 1) == want) & (place < share)
    pick = jnp.where(pick, 1.0, 0.0).astype(BF)
    left = dot(pick, sown[...].reshape(ROWS * OWN, HALF), NT).astype(BF)
    total = jnp.zeros((1, CHANS), F32)
    first = None
    for ky in range(3):
        lanes = slice(ky * 3 * CHANS, (ky + 1) * 3 * CHANS)
        start = PAD + (ky - 1) * d
        right = nk[start : start + ROWS].reshape(ROWS * OWN, 3 * CHANS)
        grads = dot(left, right, NN)
        wg_ref[:, lanes] = grads.astype(BF)
        part = jnp.sum(grads * dot(pick, w_ref[:, lanes], NN), axis=0, keepdims=True)
        for kx in range(3):
            total = total + part[:, kx * CHANS : (kx + 1) * CHANS]
        if ky == 0:
            first = grads[:, :CHANS]
    total = total / gain_ref[...]
    high = total.astype(BF).astype(F32)
    spot = jnp.bitwise_and(lax.broadcasted_iota(jnp.int32, (count, CHANS), 0), lines - 1)
    first = jnp.where(spot == share, high, jnp.where(spot == share + 1, total - high, first))
    wg_ref[:, :CHANS] = first.astype(BF)


def turn_kernel(dims, idx_ref, xo_ref, xt_ref, cot_ref, w_ref, gain_ref, q_ref, wg_ref,
                nbuf, nk, pre, sbuf, sown, wq):
    norm_phase(3, xo_ref, xt_ref, gain_ref, nbuf, nk)
    conv_phase(3, nbuf, w_ref, pre)

    def one(r):
        _, slope = gelu_parts(pre[r])
        s = cot_ref[r].astype(F32) * slope
        scatter_s(3, s.astype(BF).astype(F32), r, sbuf, sown)

    row_loop(one, 2)
    q_phase(3, sbuf, w_ref, wq, q_ref)
    weight_phase(3, dims, idx_ref, sown, nk, w_ref, gain_ref, wg_ref)


def backward_kernel(block, dims, image, first_g, idx_ref, qm_ref, qr_ref, xo_ref, xt_ref, g_ref,
                    gain_up_ref, d_ref, w_ref, nk_ref, gain_ref, *rest):
    if block:
        q_ref, gn_ref, wg_ref, sown, sbuf, wq = rest
    else:
        wg_ref, sown = rest
        q_ref = gn_ref = sbuf = wq = None
    first, width = S_WIN[block]
    at = first - X_WIN[block + 1][0]
    cut = first - first_g
    live = in_image(idx_ref[0], first, width, image)
    gain_own, gain_oth = gain_up_ref[:, :HALF], gain_up_ref[:, HALF:]

    def one(r):
        xo = xo_ref[r].astype(F32)[at : at + width]
        xt = xt_ref[r].astype(F32)[at : at + width]
        mean, rstd = stats(xo, xt)
        uo, ut = (xo - mean) * rstd, (xt - mean) * rstd
        po = (qm_ref[1, r].astype(F32) + qr_ref[0, r].astype(F32)) * gain_own
        pt = (qm_ref[0, r].astype(F32) + qr_ref[1, r].astype(F32)) * gain_oth
        level = (jnp.sum(po, axis=1, keepdims=True) + jnp.sum(pt, axis=1, keepdims=True)) / CHANS
        cross = (
            jnp.sum(po * uo, axis=1, keepdims=True) + jnp.sum(pt * ut, axis=1, keepdims=True)
        ) / CHANS
        g = g_ref[r].astype(F32)[cut : cut + width] + rstd * (po - level - uo * cross)
        g = jnp.where(live, g, 0.0).astype(BF)
        if gn_ref is not None:
            gn_ref[r] = g
        s = (g.astype(F32) * d_ref[r]).astype(BF).astype(F32)
        scatter_s(block, s, r, sbuf, sown)

    row_loop(one, 2)
    if block:
        q_phase(block, sbuf, w_ref, wq, q_ref)
    weight_phase(block, dims, idx_ref, sown, nk_ref, w_ref, gain_ref, wg_ref)


def finish_kernel(dims, slabs, all_ref, perm_ref, out_ref):
    own_chans, share, lines = dims
    bits = lines.bit_length() - 1
    col = lax.broadcasted_iota(jnp.int32, (own_chans, slabs * lines), 1)
    place = jnp.bitwise_and(col, lines - 1)
    row = jnp.right_shift(col, bits) * share + place
    pick = (lax.broadcasted_iota(jnp.int32, (own_chans, slabs * lines), 0) == row) & (place < share)
    pick = jnp.where(pick, 1.0, 0.0).astype(BF)
    for t in range(TAPS):
        grads = dot(pick, all_ref[:, t * CHANS : (t + 1) * CHANS], NN).astype(BF)
        out_ref[t] = dot(grads, perm_ref[...], NT)


def local(sizes, x_in, cot, w1, gain):
    nx, nz, ny, ns = sizes
    own_chans, rows = x_in.shape[1], x_in.shape[2]
    image = x_in.shape[3]
    shards = nx * nz
    share = own_chans // ny
    lines = 8
    while lines < share + 2:
        lines *= 2
    dims = (own_chans, share, lines)
    sec, ax, az = lax.axis_index("section"), lax.axis_index("x"), lax.axis_index("zh")
    core, slab = lax.axis_index("core"), lax.axis_index("slab")
    patch = ax * nz + az
    idx = jnp.stack([patch * OWN, slab]).astype(jnp.int32)

    def other(value):
        return lax.ppermute(value, "core", [(0, 1), (1, 0)])

    order = np.arange(CHANS).reshape(shards, 2, own_chans)
    orders = [np.concatenate([order[:, h].ravel(), order[:, 1 - h].ravel()]) for h in (0, 1)]
    perms = np.stack([np.eye(CHANS, dtype=np.float32)[:, o] for o in orders])
    perm = lax.dynamic_index_in_dim(jnp.asarray(perms, BF), core, 0, keepdims=False)

    packed = call(prep_kernel, shape((own_chans, TAPS * CHANS), BF), [], (w1[0], perm))
    wide = jnp.broadcast_to(packed[None], (ns * nz, own_chans, TAPS * CHANS))
    wide = lax.all_to_all(wide, ("section", "zh"), 0, 0, tiled=True)
    wide = wide.reshape(ns, nz * own_chans, TAPS * CHANS)
    weights = [lax.all_gather(wide[b], "x", axis=0, tiled=True) for b in range(ns)]
    gains = lax.all_gather(gain[0], "section", axis=0)
    gains = gains.reshape(ns, shards, 2, own_chans)
    gains = jnp.concatenate(
        [
            lax.dynamic_index_in_dim(gains, core, 2, keepdims=False).reshape(ns, HALF),
            lax.dynamic_index_in_dim(gains, 1 - core, 2, keepdims=False).reshape(ns, HALF),
        ],
        axis=1,
    )
    gains = [gains[b : b + 1] for b in range(ns)]

    def mine(value, edge):
        value = lax.dynamic_index_in_dim(value, sec, 0, keepdims=False).transpose(1, 0, 2)
        return jnp.pad(value, ((0, 0), (0, 0), (edge, edge)))

    wide_x, wide_c = mine(x_in, 32), mine(cot, 16)
    windows = jnp.stack(
        [
            jnp.concatenate(
                [wide_x[:, :, OWN * p : OWN * p + XWIN], wide_c[:, :, OWN * p : OWN * p + CWIN]], axis=2
            )
            for p in range(shards)
        ]
    )
    windows = jnp.broadcast_to(windows[:, None], (shards, ny) + windows.shape[1:])
    windows = windows.reshape((shards * ny,) + windows.shape[2:])
    recv = lax.all_to_all(windows, ("x", "zh", "slab"), 0, 0, tiled=True)
    recv = recv.reshape(shards, ny, rows, own_chans, XWIN + CWIN)
    x_own, cot_own = call(
        functools.partial(assemble_kernel, ny, rows),
        (shape((ROWS, XWIN, HALF), BF), shape((ROWS, CWIN, HALF), BF)),
        [],
        (recv,),
    )

    taps3 = 3 * CHANS
    nk_shape = (ROWS + 2 * PAD, OWN, taps3)
    halves, slopes, shifted = [(x_own, other(x_own))], [], []
    for b in range(ns - 1):
        width = X_WIN[b + 1][1]
        y, slope, nk = call(
            functools.partial(forward_kernel, b, image),
            (
                shape((ROWS, width, HALF), BF),
                shape((ROWS, S_WIN[b][1], HALF), F32),
                shape(nk_shape, BF),
            ),
            [
                pltpu.VMEM((ROWS + 2 * PAD, width, taps3), BF),
                pltpu.VMEM((ROWS, width, HALF), F32),
            ],
            (idx, *halves[b], weights[b], gains[b]),
            (0,),
        )
        halves.append((y, other(y)))
        slopes.append(slope)
        shifted.append(nk)

    def back_scratch(b):
        width = S_WIN[b - 1][1]
        return [
            pltpu.VMEM((ROWS + 2 * PAD, width, 768), BF),
            pltpu.VMEM((ROWS, OWN, HALF), BF),
            pltpu.VMEM((3, 768, CHANS), BF),
        ]

    count = shards * lines
    wg_shape = shape((count, TAPS * CHANS), BF)
    width = X_WIN[4][1]
    sbuf_s, sown_s, wq_s = back_scratch(3)
    q, grads = call(
        functools.partial(turn_kernel, dims),
        (shape((2, ROWS, S_WIN[2][1], HALF), BF), wg_shape),
        [
            pltpu.VMEM((ROWS + 2 * PAD, width, taps3), BF),
            pltpu.VMEM(nk_shape, BF),
            pltpu.VMEM((ROWS, width, HALF), F32),
            sbuf_s,
            sown_s,
            wq_s,
        ],
        (idx, *halves[3], cot_own, weights[3], gains[3]),
        (0,),
    )
    weight_parts = [None] * 3 + [grads]
    g, first_g = cot_own, S_WIN[3][0]
    for b in (2, 1, 0):
        args = (
            idx, q, other(q), *halves[b + 1], g, gains[b + 1], slopes[b], weights[b], shifted[b], gains[b],
        )
        kernel = functools.partial(backward_kernel, b, dims, image, first_g)
        if b:
            sbuf_s, sown_s, wq_s = back_scratch(b)
            q, g, grads = call(
                kernel,
                (
                    shape((2, ROWS, S_WIN[b - 1][1], HALF), BF),
                    shape((ROWS, S_WIN[b][1], HALF), BF),
                    wg_shape,
                ),
                [sown_s, sbuf_s, wq_s],
                args,
                (0,),
            )
        else:
            (grads,) = call(kernel, (wg_shape,), [pltpu.VMEM((ROWS, OWN, HALF), BF)], args, (0,))
        first_g = S_WIN[b][0]
        weight_parts[b] = grads

    parts = jnp.stack(weight_parts).reshape(ns * shards, lines, TAPS * CHANS)
    parts = lax.all_to_all(parts, ("section", "x", "zh"), 0, 0, tiled=True)
    total = jnp.sum(parts.astype(F32), axis=0)
    gain_sum = total[share, :CHANS] + total[share + 1, :CHANS]
    high = gain_sum.astype(BF)
    low = (gain_sum - high.astype(F32)).astype(BF)
    total = total.astype(BF)
    total = total.at[share, :CHANS].set(high).at[share + 1, :CHANS].set(low)
    every = lax.all_gather(total, "slab", axis=0, tiled=True)
    weight_grad = call(
        functools.partial(finish_kernel, dims, ny),
        shape((TAPS, own_chans, CHANS), F32),
        [],
        (every, perm),
    )
    gain_rows = every.reshape(ny, lines, TAPS * CHANS)[:, share : share + 2, :CHANS]
    gain_all = jnp.sum(gain_rows.astype(F32), axis=(0, 1))
    here = lax.dynamic_slice_in_dim(gain_all, patch * own_chans, own_chans)
    there = lax.dynamic_slice_in_dim(gain_all, HALF + patch * own_chans, own_chans)
    gain_grad = here + other(there)
    return weight_grad[None], gain_grad[None]


def solution(mesh):
    ns, chans, ny = mesh.shape["section"], mesh.shape["ch"], mesh.shape["slab"]
    nz = 2 if chans % 4 == 0 else 1
    nx = chans // (2 * nz)
    axes = ("section", "x", "zh", "core", "slab")
    fine = Mesh(mesh.devices.reshape(ns, nx, nz, 2, ny), axes)
    ch = ("x", "zh", "core")
    return jax.shard_map(
        functools.partial(local, (nx, nz, ny, ns)),
        mesh=fine,
        in_specs=(
            P(None, ch, "slab", None),
            P(None, ch, "slab", None),
            P("section", None, ch, None),
            P("section", None),
        ),
        out_specs=(P("section", None, ch, None), P("section", ch)),
        check_vma=False,
    )
```

```python
import functools

import jax
import jax.numpy as jnp
import numpy as np
from jax import lax
from jax.experimental import pallas as pl
from jax.experimental.pallas import tpu as pltpu
from jax.sharding import Mesh, PartitionSpec as P

NORM_EPS = 1e-05
SLOPE_SCALE = 0.7978845608028654
CUBIC_COEF = 0.044715
BF = jnp.bfloat16
F32 = jnp.float32

ROWS = 32
CHANS = 384
HALF = 192
TAPS = 9
DIL = (1, 2, 4, 8)
OWN = 16
XWIN = 80
CWIN = 48
PAD = 8
X_WIN = ((0, 80), (0, 80), (0, 80), (8, 64), (16, 48))
S_WIN = ((32, 16), (24, 32), (24, 32), (16, 48))
VMEM_LIMIT = 56 * 1024 * 1024
PARAMS = pltpu.CompilerParams(vmem_limit_bytes=VMEM_LIMIT)
NT = (((1,), (1,)), ((), ()))
NN = (((1,), (0,)), ((), ()))
LANES = TAPS * CHANS
CARRY = LANES + 128
R_NORM, R_EPI, R_BACK = 2, 2, 2


def dot(a, b, dims):
    return lax.dot_general(a, b, dims, preferred_element_type=F32)


def call(kernel, out_shape, scratch, args, smem=()):
    vm = pl.BlockSpec(memory_space=pltpu.VMEM)
    sm = pl.BlockSpec(memory_space=pltpu.SMEM)
    return pl.pallas_call(
        kernel,
        out_shape=out_shape,
        in_specs=[sm if i in smem else vm for i in range(len(args))],
        out_specs=jax.tree.map(lambda _: vm, out_shape),
        scratch_shapes=scratch,
        compiler_params=PARAMS,
    )(*args)


def shape(dims, dtype):
    return jax.ShapeDtypeStruct(dims, dtype)


def row_loop(body, rows, unroll=1):
    span = rows * unroll

    def step(i, carry):
        for k in range(unroll):
            body(pl.multiple_of(i * span, span) + k * rows)
        return carry

    lax.fori_loop(0, ROWS // span, step, 0)


def flat(value):
    return value.reshape(value.shape[0] * value.shape[1], value.shape[2])


def in_image(base, first, count, width):
    cols = lax.broadcasted_iota(jnp.int32, (1, count, HALF), 1) + (base - 32 + first)
    return (cols >= 0) & (cols < width)


def widen(own, oth):
    return jnp.concatenate([own.astype(F32), oth.astype(F32)], axis=1)


def chan_mean(value):
    folded = value[:, :128] + value[:, 128:256] + value[:, 256:]
    return jnp.sum(folded, axis=1, keepdims=True) / CHANS


def unit_of(value):
    mean = chan_mean(value)
    rstd = lax.rsqrt(chan_mean(value * value) - mean * mean + NORM_EPS)
    return (value - mean) * rstd, rstd


def read_gain(w_ref):
    tile = w_ref[0:16, LANES:CARRY].astype(F32)
    return jnp.concatenate(
        [(tile[p : p + 1] + tile[3 + p : 4 + p]) + tile[6 + p : 7 + p] for p in range(3)], axis=1
    )


def gelu_inner(pre):
    return jnp.tanh(SLOPE_SCALE * (pre + CUBIC_COEF * pre * pre * pre))


def gelu_slope(pre, tangent):
    return 0.5 * (1.0 + tangent) + 0.5 * pre * (1.0 - tangent * tangent) * SLOPE_SCALE * (
        1.0 + 3.0 * CUBIC_COEF * pre * pre
    )


def prep_kernel(w_ref, gain_ref, perm_ref, out_ref):
    for t in range(TAPS):
        out_ref[:, t * CHANS : (t + 1) * CHANS] = dot(w_ref[t], perm_ref[...], NN).astype(BF)
    rest = jnp.broadcast_to(gain_ref[...], (8, CHANS))
    row = lax.broadcasted_iota(jnp.int32, (out_ref.shape[0], 128), 0)
    tile = jnp.zeros((out_ref.shape[0], 128), F32)
    for k in range(3):
        piece = rest.astype(BF)
        rest = rest - piece.astype(F32)
        moved = dot(piece, perm_ref[...], NN)
        for p in range(3):
            tile = jnp.where(row == 3 * k + p, moved[0:1, 128 * p : 128 * p + 128], tile)
    out_ref[:, LANES:CARRY] = tile.astype(BF)


def assemble_kernel(slabs, rows, recv_ref, x_ref, cot_ref):
    lanes = XWIN + CWIN
    eye = (
        lax.broadcasted_iota(jnp.int32, (lanes, lanes), 0)
        == lax.broadcasted_iota(jnp.int32, (lanes, lanes), 1)
    ).astype(F32).astype(BF)

    def one(r, carry):
        for y in range(slabs):
            piece = recv_ref[:, y, pl.ds(r, 1)].astype(F32)
            piece = piece.reshape(HALF, lanes).astype(BF)
            flipped = dot(eye, piece, NT).astype(BF)
            x_ref[pl.ds(y * rows + r, 1)] = flipped[:XWIN].reshape(1, XWIN, HALF)
            cot_ref[pl.ds(y * rows + r, 1)] = flipped[XWIN:].reshape(1, CWIN, HALF)
        return carry

    lax.fori_loop(0, rows, one, 0)


def norm_phase(block, xo_ref, xt_ref, gain, nbuf, nk):
    d = DIL[block]
    first_in, width_in = X_WIN[block]
    first_out, width_out = X_WIN[block + 1]
    low = first_out - first_in
    own = 32 - first_in
    for edge in (0, PAD + ROWS):
        nbuf[edge : edge + PAD] = jnp.zeros((PAD, width_out, 3 * CHANS), BF)
        nk[edge : edge + PAD] = jnp.zeros((PAD, OWN, 3 * CHANS), BF)
    n = R_NORM

    def some(r):
        unit, _ = unit_of(widen(flat(xo_ref[pl.ds(r, n)]), flat(xt_ref[pl.ds(r, n)])))
        both = unit * gain
        for kx in range(3):
            shift = (-(kx - 1) * d) % (n * width_in)
            moved = pltpu.roll(both, shift, 0) if shift else both
            moved = moved.reshape(n, width_in, CHANS)
            lanes = slice(kx * CHANS, (kx + 1) * CHANS)
            nbuf[pl.ds(PAD + r, n), :, lanes] = moved[:, low : low + width_out].astype(BF)
            nk[pl.ds(PAD + r, n), :, lanes] = moved[:, own : own + OWN].astype(BF)

    row_loop(some, n)


def conv_phase(block, nbuf, w_ref, pre):
    d = DIL[block]
    width = X_WIN[block + 1][1]
    step = 8

    def one(i, carry):
        r0 = i * step
        acc = None
        for ky in range(3):
            left = nbuf[pl.ds(PAD + r0 + (ky - 1) * d, step)].reshape(step * width, 3 * CHANS)
            term = dot(left, w_ref[:, ky * 3 * CHANS : (ky + 1) * 3 * CHANS], NT)
            acc = term if acc is None else acc + term
        pre[pl.ds(r0, step)] = acc.reshape(step, width, HALF)
        return carry

    lax.fori_loop(0, ROWS // step, one, 0)


def forward_kernel(block, image, idx_ref, xo_ref, xt_ref, w_ref, y_ref, d_ref, nk, gain_ref, nbuf, pre):
    first_in = X_WIN[block][0]
    first_out, width_out = X_WIN[block + 1]
    first_s, width_s = S_WIN[block]
    gain = read_gain(w_ref)
    gain_ref[...] = gain
    norm_phase(block, xo_ref, xt_ref, gain, nbuf, nk)
    conv_phase(block, nbuf, w_ref, pre)
    live = in_image(idx_ref[0], first_out, width_out, image)
    low, at = first_out - first_in, first_s - first_out
    n = R_EPI

    def some(r):
        act = pre[pl.ds(r, n)]
        tangent = gelu_inner(act)
        out = xo_ref[pl.ds(r, n)].astype(F32)[:, low : low + width_out] + 0.5 * act * (1.0 + tangent)
        y_ref[pl.ds(r, n)] = jnp.where(live, out, 0.0).astype(BF)
        d_ref[pl.ds(r, n)] = gelu_slope(act[:, at : at + width_s], tangent[:, at : at + width_s])

    row_loop(some, n)


def scatter_s(block, s, r, n, sbuf, sown):
    first, width = S_WIN[block]
    rows = s.reshape(n, width, HALF)
    sown[pl.ds(r, n)] = rows[:, 32 - first : 32 - first + OWN].astype(BF)
    if sbuf is None:
        return
    d = DIL[block]
    first_q, width_q = S_WIN[block - 1]
    low = first_q - first
    gap = jnp.zeros((n * width, 256 - HALF), F32)
    wide = jnp.concatenate([s, gap], axis=1)
    for kx in range(3):
        shift = ((kx - 1) * d) % (n * width)
        moved = pltpu.roll(wide, shift, 0) if shift else wide
        moved = moved.reshape(n, width, 256)[:, low : low + width_q]
        sbuf[pl.ds(PAD + r, n), :, kx * 256 : (kx + 1) * 256] = moved.astype(BF)


def q_phase(block, sbuf, w_ref, wq, q_ref):
    d = DIL[block]
    width = S_WIN[block - 1][1]
    for ky in range(3):
        for kx in range(3):
            t = 3 * ky + kx
            wq[ky, kx * 256 : kx * 256 + HALF] = w_ref[:, t * CHANS : (t + 1) * CHANS]
            wq[ky, kx * 256 + HALF : (kx + 1) * 256] = jnp.zeros((256 - HALF, CHANS), BF)
    for edge in (0, PAD + ROWS):
        sbuf[edge : edge + PAD] = jnp.zeros((PAD, width, 768), BF)
    step = 512 // width

    def one(i, carry):
        r0 = i * step
        acc = None
        for ky in range(3):
            left = sbuf[pl.ds(PAD + r0 - (ky - 1) * d, step)].reshape(step * width, 768)
            term = dot(left, wq[ky], NN)
            acc = term if acc is None else acc + term
        q_ref[0, pl.ds(r0, step)] = acc[:, HALF:].reshape(step, width, HALF).astype(BF)
        q_ref[1, pl.ds(r0, step)] = acc[:, :HALF].reshape(step, width, HALF).astype(BF)
        return carry

    lax.fori_loop(0, ROWS // step, one, 0)


def weight_phase(block, dims, idx_ref, sown, nk, w_ref, gain, wg_ref):
    own_chans, share, lines = dims
    d = DIL[block]
    count = (HALF // own_chans) * lines
    bits = lines.bit_length() - 1
    line = lax.broadcasted_iota(jnp.int32, (count, HALF), 0)
    place = jnp.bitwise_and(line, lines - 1)
    want = jnp.right_shift(line, bits) * own_chans + share * idx_ref[1] + place
    pick = (lax.broadcasted_iota(jnp.int32, (count, HALF), 1) == want) & (place < share)
    pick = jnp.where(pick, 1.0, 0.0).astype(BF)
    left = dot(pick, sown[...].reshape(ROWS * OWN, HALF), NT).astype(BF)
    total = jnp.zeros((1, CHANS), F32)
    first = None
    for ky in range(3):
        lanes = slice(ky * 3 * CHANS, (ky + 1) * 3 * CHANS)
        start = PAD + (ky - 1) * d
        right = nk[start : start + ROWS].reshape(ROWS * OWN, 3 * CHANS)
        grads = dot(left, right, NN)
        wg_ref[:, lanes] = grads.astype(BF)
        part = jnp.sum(grads * dot(pick, w_ref[:, lanes], NN), axis=0, keepdims=True)
        for kx in range(3):
            total = total + part[:, kx * CHANS : (kx + 1) * CHANS]
        if ky == 0:
            first = grads[:, :CHANS]
    spot = jnp.bitwise_and(lax.broadcasted_iota(jnp.int32, (count, CHANS), 0), lines - 1)
    wg_ref[:, :CHANS] = jnp.where(spot == share, total / gain, first).astype(BF)


def turn_kernel(dims, idx_ref, xo_ref, xt_ref, cot_ref, w_ref, q_ref, wg_ref, gain_ref,
                nbuf, nk, pre, sbuf, sown, wq):
    gain = read_gain(w_ref)
    gain_ref[...] = gain
    norm_phase(3, xo_ref, xt_ref, gain, nbuf, nk)
    conv_phase(3, nbuf, w_ref, pre)
    n = R_BACK

    def some(r):
        act = flat(pre[pl.ds(r, n)])
        s = flat(cot_ref[pl.ds(r, n)]).astype(F32) * gelu_slope(act, gelu_inner(act))
        scatter_s(3, s, r, n, sbuf, sown)

    row_loop(some, n)
    q_phase(3, sbuf, w_ref, wq, q_ref)
    weight_phase(3, dims, idx_ref, sown, nk, w_ref, gain, wg_ref)


def backward_kernel(block, dims, image, first_g, idx_ref, qm_ref, qr_ref, xo_ref, xt_ref, g_ref,
                    gain_up_ref, d_ref, w_ref, nk_ref, gain_ref, *rest):
    if block:
        q_ref, gn_ref, wg_ref, sown, sbuf, wq = rest
    else:
        wg_ref, sown = rest
        q_ref = gn_ref = sbuf = wq = None
    first, width = S_WIN[block]
    at = first - X_WIN[block + 1][0]
    cut = first - first_g
    live = in_image(idx_ref[0], first, width, image)
    gain_up = gain_up_ref[...]
    n = R_BACK

    def some(r):
        rows = pl.ds(r, n)
        unit, rstd = unit_of(
            widen(flat(xo_ref[rows, at : at + width]), flat(xt_ref[rows, at : at + width]))
        )
        p = gain_up * jnp.concatenate(
            [
                flat(qm_ref[1, rows]).astype(F32) + flat(qr_ref[0, rows]).astype(F32),
                flat(qm_ref[0, rows]).astype(F32) + flat(qr_ref[1, rows]).astype(F32),
            ],
            axis=1,
        )
        change = p[:, :HALF] - chan_mean(p) - unit[:, :HALF] * chan_mean(p * unit)
        g = flat(g_ref[rows, cut : cut + width]).astype(F32) + rstd * change
        g = jnp.where(live, g.reshape(n, width, HALF), 0.0).astype(BF)
        if gn_ref is not None:
            gn_ref[rows] = g
        s = flat(g.astype(F32) * d_ref[rows])
        scatter_s(block, s, r, n, sbuf, sown)

    row_loop(some, n)
    if block:
        q_phase(block, sbuf, w_ref, wq, q_ref)
    weight_phase(block, dims, idx_ref, sown, nk_ref, w_ref, gain_ref[...], wg_ref)


def finish_kernel(dims, slabs, all_ref, perm_ref, out_ref):
    own_chans, share, lines = dims
    bits = lines.bit_length() - 1
    col = lax.broadcasted_iota(jnp.int32, (own_chans, slabs * lines), 1)
    place = jnp.bitwise_and(col, lines - 1)
    row = jnp.right_shift(col, bits) * share + place
    pick = (lax.broadcasted_iota(jnp.int32, (own_chans, slabs * lines), 0) == row) & (place < share)
    pick = jnp.where(pick, 1.0, 0.0).astype(BF)
    for t in range(TAPS):
        grads = dot(pick, all_ref[:, t * CHANS : (t + 1) * CHANS], NN).astype(BF)
        out_ref[t] = dot(grads, perm_ref[...], NT)


def local(sizes, x_in, cot, w1, gain):
    nx, nz, ny, ns = sizes
    own_chans, rows = x_in.shape[1], x_in.shape[2]
    image = x_in.shape[3]
    shards = nx * nz
    share = own_chans // ny
    lines = 8
    while lines < share + 1:
        lines *= 2
    dims = (own_chans, share, lines)
    sec, ax, az = lax.axis_index("section"), lax.axis_index("x"), lax.axis_index("zh")
    core, slab = lax.axis_index("core"), lax.axis_index("slab")
    patch = ax * nz + az
    idx = jnp.stack([patch * OWN, slab]).astype(jnp.int32)

    def other(value):
        return lax.ppermute(value, "core", [(0, 1), (1, 0)])

    order = np.arange(CHANS).reshape(shards, 2, own_chans)
    orders = [np.concatenate([order[:, h].ravel(), order[:, 1 - h].ravel()]) for h in (0, 1)]
    perms = np.stack([np.eye(CHANS, dtype=np.float32)[:, o] for o in orders])
    perm = lax.dynamic_index_in_dim(jnp.asarray(perms, BF), core, 0, keepdims=False)

    packed = call(prep_kernel, shape((own_chans, CARRY), BF), [], (w1[0], gain, perm))
    wide = jnp.broadcast_to(packed[None], (ns * nz, own_chans, CARRY))
    wide = lax.all_to_all(wide, ("section", "zh"), 0, 0, tiled=True)
    wide = wide.reshape(ns, nz * own_chans, CARRY)
    weights = [lax.all_gather(wide[b], "x", axis=0, tiled=True) for b in range(ns)]

    def mine(value, edge):
        value = lax.dynamic_index_in_dim(value, sec, 0, keepdims=False).transpose(1, 0, 2)
        return jnp.pad(value, ((0, 0), (0, 0), (edge, edge)))

    wide_x, wide_c = mine(x_in, 32), mine(cot, 16)
    windows = jnp.stack(
        [
            jnp.concatenate(
                [wide_x[:, :, OWN * p : OWN * p + XWIN], wide_c[:, :, OWN * p : OWN * p + CWIN]], axis=2
            )
            for p in range(shards)
        ]
    )
    windows = jnp.broadcast_to(windows[:, None], (shards, ny) + windows.shape[1:])
    windows = windows.reshape((shards * ny,) + windows.shape[2:])
    windows, _ = lax.optimization_barrier((windows, wide))
    recv = lax.all_to_all(windows, ("x", "zh", "slab"), 0, 0, tiled=True)
    recv = recv.reshape(shards, ny, rows, own_chans, XWIN + CWIN)
    x_own, cot_own = call(
        functools.partial(assemble_kernel, ny, rows),
        (shape((ROWS, XWIN, HALF), BF), shape((ROWS, CWIN, HALF), BF)),
        [],
        (recv,),
    )

    taps3 = 3 * CHANS
    nk_shape = (ROWS + 2 * PAD, OWN, taps3)
    gain_shape = shape((1, CHANS), F32)
    halves, slopes, shifted, gains = [(x_own, other(x_own))], [], [], []
    for b in range(ns - 1):
        width = X_WIN[b + 1][1]
        y, slope, nk, gain_b = call(
            functools.partial(forward_kernel, b, image),
            (
                shape((ROWS, width, HALF), BF),
                shape((ROWS, S_WIN[b][1], HALF), F32),
                shape(nk_shape, BF),
                gain_shape,
            ),
            [
                pltpu.VMEM((ROWS + 2 * PAD, width, taps3), BF),
                pltpu.VMEM((ROWS, width, HALF), F32),
            ],
            (idx, *halves[b], weights[b]),
            (0,),
        )
        halves.append((y, other(y)))
        slopes.append(slope)
        shifted.append(nk)
        gains.append(gain_b)

    def back_scratch(b):
        width = S_WIN[b - 1][1]
        return [
            pltpu.VMEM((ROWS + 2 * PAD, width, 768), BF),
            pltpu.VMEM((ROWS, OWN, HALF), BF),
            pltpu.VMEM((3, 768, CHANS), BF),
        ]

    count = shards * lines
    wg_shape = shape((count, TAPS * CHANS), BF)
    width = X_WIN[4][1]
    sbuf_s, sown_s, wq_s = back_scratch(3)
    q, grads, gain_b = call(
        functools.partial(turn_kernel, dims),
        (shape((2, ROWS, S_WIN[2][1], HALF), BF), wg_shape, gain_shape),
        [
            pltpu.VMEM((ROWS + 2 * PAD, width, taps3), BF),
            pltpu.VMEM(nk_shape, BF),
            pltpu.VMEM((ROWS, width, HALF), F32),
            sbuf_s,
            sown_s,
            wq_s,
        ],
        (idx, *halves[3], cot_own, weights[3]),
        (0,),
    )
    gains.append(gain_b)

    def reduced(value):
        value = value.reshape(nx, nz * lines, LANES)
        value = lax.all_to_all(value, "x", 0, 0, tiled=True)
        return jnp.sum(value.astype(F32), axis=0).astype(BF)

    weight_parts = [None] * 3 + [reduced(grads)]
    g, first_g = cot_own, S_WIN[3][0]
    for b in (2, 1, 0):
        args = (
            idx, q, other(q), *halves[b + 1], g, gains[b + 1], slopes[b], weights[b], shifted[b], gains[b],
        )
        kernel = functools.partial(backward_kernel, b, dims, image, first_g)
        if b:
            sbuf_s, sown_s, wq_s = back_scratch(b)
            q, g, grads = call(
                kernel,
                (
                    shape((2, ROWS, S_WIN[b - 1][1], HALF), BF),
                    shape((ROWS, S_WIN[b][1], HALF), BF),
                    wg_shape,
                ),
                [sown_s, sbuf_s, wq_s],
                args,
                (0,),
            )
        else:
            (grads,) = call(kernel, (wg_shape,), [pltpu.VMEM((ROWS, OWN, HALF), BF)], args, (0,))
        first_g = S_WIN[b][0]
        weight_parts[b] = reduced(grads)

    parts = jnp.stack(weight_parts).reshape(ns * nz, lines, LANES)
    parts = lax.all_to_all(parts, ("section", "zh"), 0, 0, tiled=True)
    total = jnp.sum(parts.astype(F32), axis=0).astype(BF)
    every = lax.all_gather(total, "slab", axis=0, tiled=True)
    weight_grad = call(
        functools.partial(finish_kernel, dims, ny),
        shape((TAPS, own_chans, CHANS), F32),
        [],
        (every, perm),
    )
    gain_rows = every.reshape(ny, lines, LANES)[:, share, :CHANS]
    gain_all = jnp.sum(gain_rows.astype(F32), axis=0)
    here = lax.dynamic_slice_in_dim(gain_all, patch * own_chans, own_chans)
    there = lax.dynamic_slice_in_dim(gain_all, HALF + patch * own_chans, own_chans)
    gain_grad = here + other(there)
    return weight_grad[None], gain_grad[None]


def solution(mesh):
    ns, chans, ny = mesh.shape["section"], mesh.shape["ch"], mesh.shape["slab"]
    nz = 2 if chans % 4 == 0 else 1
    nx = chans // (2 * nz)
    axes = ("section", "x", "zh", "core", "slab")
    fine = Mesh(mesh.devices.reshape(ns, nx, nz, 2, ny), axes)
    ch = ("x", "zh", "core")
    return jax.shard_map(
        functools.partial(local, (nx, nz, ny, ns)),
        mesh=fine,
        in_specs=(
            P(None, ch, "slab", None),
            P(None, ch, "slab", None),
            P("section", None, ch, None),
            P("section", None),
        ),
        out_specs=(P("section", None, ch, None), P("section", ch)),
        check_vma=False,
    )
```

```python
import functools

import jax
import jax.numpy as jnp
import numpy as np
from jax import lax
from jax.experimental import pallas as pl
from jax.experimental.pallas import tpu as pltpu
from jax.sharding import Mesh, PartitionSpec as P

NORM_EPS = 1e-05
SLOPE_SCALE = 0.7978845608028654
CUBIC_COEF = 0.044715
BF = jnp.bfloat16
F32 = jnp.float32

ROWS = 32
CHANS = 384
HALF = 192
TAPS = 9
DIL = (1, 2, 4, 8)
OWN = 16
XWIN = 80
CWIN = 48
PAD = 8
X_WIN = ((0, 80), (0, 80), (0, 80), (8, 64), (16, 48))
S_WIN = ((32, 16), (24, 32), (24, 32), (16, 48))
VMEM_LIMIT = 26 * 1024 * 1024
PARAMS = pltpu.CompilerParams(vmem_limit_bytes=VMEM_LIMIT)
NT = (((1,), (1,)), ((), ()))
NN = (((1,), (0,)), ((), ()))
LANES = TAPS * CHANS
CARRY = LANES + 128
R_NORM, R_EPI, R_TURN, R_BACK = 4, 2, 2, 8


def dot(a, b, dims):
    return lax.dot_general(a, b, dims, preferred_element_type=F32)


def call(kernel, out_shape, scratch, args, smem=()):
    vm = pl.BlockSpec(memory_space=pltpu.VMEM)
    sm = pl.BlockSpec(memory_space=pltpu.SMEM)
    return pl.pallas_call(
        kernel,
        out_shape=out_shape,
        in_specs=[sm if i in smem else vm for i in range(len(args))],
        out_specs=jax.tree.map(lambda _: vm, out_shape),
        scratch_shapes=scratch,
        compiler_params=PARAMS,
    )(*args)


def shape(dims, dtype):
    return jax.ShapeDtypeStruct(dims, dtype)


def row_loop(body, rows, unroll=1):
    span = rows * unroll

    def step(i, carry):
        for k in range(unroll):
            body(pl.multiple_of(i * span, span) + k * rows)
        return carry

    lax.fori_loop(0, ROWS // span, step, 0)


def flat(value):
    return value.reshape(value.shape[0] * value.shape[1], value.shape[2])


def in_image(base, first, count, width):
    cols = lax.broadcasted_iota(jnp.int32, (1, count, HALF), 1) + (base - 32 + first)
    return (cols >= 0) & (cols < width)


def widen(own, oth):
    return jnp.concatenate([own.astype(F32), oth.astype(F32)], axis=1)


def chan_mean(value):
    folded = value[:, :128] + value[:, 128:256] + value[:, 256:]
    return jnp.sum(folded, axis=1, keepdims=True) / CHANS


def unit_of(value):
    mean = chan_mean(value)
    rstd = lax.rsqrt(chan_mean(value * value) - mean * mean + NORM_EPS)
    return (value - mean) * rstd, rstd


def read_gain(w_ref):
    tile = w_ref[0:16, LANES:CARRY].astype(F32)
    return jnp.concatenate(
        [(tile[p : p + 1] + tile[3 + p : 4 + p]) + tile[6 + p : 7 + p] for p in range(3)], axis=1
    )


def gelu_inner(pre):
    return jnp.tanh(SLOPE_SCALE * (pre + CUBIC_COEF * pre * pre * pre))


def gelu_slope(pre, tangent):
    return 0.5 * (1.0 + tangent) + 0.5 * pre * (1.0 - tangent * tangent) * SLOPE_SCALE * (
        1.0 + 3.0 * CUBIC_COEF * pre * pre
    )


def prep_kernel(w_ref, gain_ref, perm_ref, out_ref):
    for t in range(TAPS):
        out_ref[:, t * CHANS : (t + 1) * CHANS] = dot(w_ref[t], perm_ref[...], NN).astype(BF)
    rest = jnp.broadcast_to(gain_ref[...], (8, CHANS))
    row = lax.broadcasted_iota(jnp.int32, (out_ref.shape[0], 128), 0)
    tile = jnp.zeros((out_ref.shape[0], 128), F32)
    for k in range(3):
        piece = rest.astype(BF)
        rest = rest - piece.astype(F32)
        moved = dot(piece, perm_ref[...], NN)
        for p in range(3):
            tile = jnp.where(row == 3 * k + p, moved[0:1, 128 * p : 128 * p + 128], tile)
    out_ref[:, LANES:CARRY] = tile.astype(BF)


def assemble_kernel(slabs, rows, recv_ref, x_ref, cot_ref):
    lanes = XWIN + CWIN
    eye = (
        lax.broadcasted_iota(jnp.int32, (lanes, lanes), 0)
        == lax.broadcasted_iota(jnp.int32, (lanes, lanes), 1)
    ).astype(F32).astype(BF)

    def one(r, carry):
        for y in range(slabs):
            piece = recv_ref[y, :, pl.ds(r, 1)].astype(F32)
            piece = piece.reshape(HALF, lanes).astype(BF)
            flipped = dot(eye, piece, NT).astype(BF)
            x_ref[pl.ds(y * rows + r, 1)] = flipped[:XWIN].reshape(1, XWIN, HALF)
            cot_ref[pl.ds(y * rows + r, 1)] = flipped[XWIN:].reshape(1, CWIN, HALF)
        return carry

    lax.fori_loop(0, rows, one, 0)


def norm_phase(block, xo_ref, xt_ref, gain, nbuf, nk):
    d = DIL[block]
    first_in, width_in = X_WIN[block]
    first_out, width_out = X_WIN[block + 1]
    low = first_out - first_in
    own = 32 - first_in
    for edge in (0, PAD + ROWS):
        nbuf[edge : edge + PAD] = jnp.zeros((PAD, width_out, 3 * CHANS), BF)
        nk[edge : edge + PAD] = jnp.zeros((PAD, OWN, 3 * CHANS), BF)
    n = R_NORM

    def some(r):
        unit, _ = unit_of(widen(flat(xo_ref[pl.ds(r, n)]), flat(xt_ref[pl.ds(r, n)])))
        both = unit * gain
        for kx in range(3):
            shift = (-(kx - 1) * d) % (n * width_in)
            moved = pltpu.roll(both, shift, 0) if shift else both
            moved = moved.reshape(n, width_in, CHANS)
            lanes = slice(kx * CHANS, (kx + 1) * CHANS)
            nbuf[pl.ds(PAD + r, n), :, lanes] = moved[:, low : low + width_out].astype(BF)
            nk[pl.ds(PAD + r, n), :, lanes] = moved[:, own : own + OWN].astype(BF)

    row_loop(some, n)


def conv_phase(block, nbuf, w_ref, pre):
    d = DIL[block]
    width = X_WIN[block + 1][1]
    step = 8

    def one(i, carry):
        r0 = i * step
        acc = None
        for ky in range(3):
            left = nbuf[pl.ds(PAD + r0 + (ky - 1) * d, step)].reshape(step * width, 3 * CHANS)
            term = dot(left, w_ref[:, ky * 3 * CHANS : (ky + 1) * 3 * CHANS], NT)
            acc = term if acc is None else acc + term
        pre[pl.ds(r0, step)] = acc.reshape(step, width, HALF)
        return carry

    lax.fori_loop(0, ROWS // step, one, 0)


def forward_kernel(block, image, pieces, idx_ref, xo_ref, xt_ref, *rest):
    w_refs, rest = rest[:pieces], rest[pieces:]
    y_ref, d_ref, nk, gain_ref, *rest = rest
    w_ref = w_refs[0]
    if pieces > 1:
        w_ref, *rest = rest
        lines = HALF // pieces
        for j in range(pieces):
            place = lax.rem(idx_ref[2] + j, pieces) * lines
            w_ref[pl.ds(pl.multiple_of(place, lines), lines)] = w_refs[j][...]
    nbuf, pre = rest
    first_in = X_WIN[block][0]
    first_out, width_out = X_WIN[block + 1]
    first_s, width_s = S_WIN[block]
    gain = read_gain(w_ref)
    gain_ref[...] = gain
    norm_phase(block, xo_ref, xt_ref, gain, nbuf, nk)
    conv_phase(block, nbuf, w_ref, pre)
    live = in_image(idx_ref[0], first_out, width_out, image)
    low, at = first_out - first_in, first_s - first_out
    n = R_EPI

    def some(r):
        act = pre[pl.ds(r, n)]
        tangent = gelu_inner(act)
        out = xo_ref[pl.ds(r, n)].astype(F32)[:, low : low + width_out] + 0.5 * act * (1.0 + tangent)
        y_ref[pl.ds(r, n)] = jnp.where(live, out, 0.0).astype(BF)
        d_ref[pl.ds(r, n)] = gelu_slope(act[:, at : at + width_s], tangent[:, at : at + width_s])

    row_loop(some, n)


def scatter_s(block, s, r, n, sbuf, sown):
    first, width = S_WIN[block]
    rows = s.reshape(n, width, HALF)
    sown[pl.ds(r, n)] = rows[:, 32 - first : 32 - first + OWN].astype(BF)
    if sbuf is None:
        return
    d = DIL[block]
    first_q, width_q = S_WIN[block - 1]
    low = first_q - first
    gap = jnp.zeros((n * width, 256 - HALF), F32)
    wide = jnp.concatenate([s, gap], axis=1)
    for kx in range(3):
        shift = ((kx - 1) * d) % (n * width)
        moved = pltpu.roll(wide, shift, 0) if shift else wide
        moved = moved.reshape(n, width, 256)[:, low : low + width_q]
        sbuf[pl.ds(PAD + r, n), :, kx * 256 : (kx + 1) * 256] = moved.astype(BF)


def q_phase(block, sbuf, w_ref, wq, q_ref):
    d = DIL[block]
    width = S_WIN[block - 1][1]
    for ky in range(3):
        for kx in range(3):
            t = 3 * ky + kx
            wq[ky, kx * 256 : kx * 256 + HALF] = w_ref[:, t * CHANS : (t + 1) * CHANS]
            wq[ky, kx * 256 + HALF : (kx + 1) * 256] = jnp.zeros((256 - HALF, CHANS), BF)
    for edge in (0, PAD + ROWS):
        sbuf[edge : edge + PAD] = jnp.zeros((PAD, width, 768), BF)
    step = 512 // width

    def one(i, carry):
        r0 = i * step
        acc = None
        for ky in range(3):
            left = sbuf[pl.ds(PAD + r0 - (ky - 1) * d, step)].reshape(step * width, 768)
            term = dot(left, wq[ky], NN)
            acc = term if acc is None else acc + term
        q_ref[0, pl.ds(r0, step)] = acc[:, HALF:].reshape(step, width, HALF).astype(BF)
        q_ref[1, pl.ds(r0, step)] = acc[:, :HALF].reshape(step, width, HALF).astype(BF)
        return carry

    lax.fori_loop(0, ROWS // step, one, 0)


def weight_phase(block, dims, idx_ref, sown, nk, w_ref, gain, wg_ref):
    own_chans, share, lines = dims
    d = DIL[block]
    count = (HALF // own_chans) * lines
    bits = lines.bit_length() - 1
    line = lax.broadcasted_iota(jnp.int32, (count, HALF), 0)
    place = jnp.bitwise_and(line, lines - 1)
    want = jnp.right_shift(line, bits) * own_chans + share * idx_ref[1] + place
    pick = (lax.broadcasted_iota(jnp.int32, (count, HALF), 1) == want) & (place < share)
    pick = jnp.where(pick, 1.0, 0.0).astype(BF)
    left = dot(pick, sown[...].reshape(ROWS * OWN, HALF), NT).astype(BF)
    total = jnp.zeros((1, CHANS), F32)
    first = None
    for ky in range(3):
        lanes = slice(ky * 3 * CHANS, (ky + 1) * 3 * CHANS)
        start = PAD + (ky - 1) * d
        right = nk[start : start + ROWS].reshape(ROWS * OWN, 3 * CHANS)
        grads = dot(left, right, NN)
        wg_ref[:, lanes] = grads.astype(BF)
        part = jnp.sum(grads * dot(pick, w_ref[:, lanes], NN), axis=0, keepdims=True)
        for kx in range(3):
            total = total + part[:, kx * CHANS : (kx + 1) * CHANS]
        if ky == 0:
            first = grads[:, :CHANS]
    spot = jnp.bitwise_and(lax.broadcasted_iota(jnp.int32, (count, CHANS), 0), lines - 1)
    wg_ref[:, :CHANS] = jnp.where(spot == share, total / gain, first).astype(BF)


def turn_kernel(dims, idx_ref, xo_ref, xt_ref, cot_ref, w_ref, q_ref, wg_ref, gain_ref,
                nbuf, nk, pre, sbuf, sown, wq):
    gain = read_gain(w_ref)
    gain_ref[...] = gain
    norm_phase(3, xo_ref, xt_ref, gain, nbuf, nk)
    conv_phase(3, nbuf, w_ref, pre)
    n = R_TURN

    def some(r):
        act = flat(pre[pl.ds(r, n)])
        s = flat(cot_ref[pl.ds(r, n)]).astype(F32) * gelu_slope(act, gelu_inner(act))
        scatter_s(3, s, r, n, sbuf, sown)

    row_loop(some, n)
    q_phase(3, sbuf, w_ref, wq, q_ref)
    weight_phase(3, dims, idx_ref, sown, nk, w_ref, gain, wg_ref)


def backward_kernel(block, dims, image, first_g, idx_ref, qm_ref, qr_ref, xo_ref, xt_ref, g_ref,
                    gain_up_ref, d_ref, w_ref, nk_ref, gain_ref, *rest):
    if block:
        q_ref, gn_ref, wg_ref, sown, sbuf, wq = rest
    else:
        wg_ref, sown = rest
        q_ref = gn_ref = sbuf = wq = None
    first, width = S_WIN[block]
    at = first - X_WIN[block + 1][0]
    cut = first - first_g
    live = in_image(idx_ref[0], first, width, image)
    gain_up = gain_up_ref[...]
    n = R_BACK

    def some(r):
        rows = pl.ds(r, n)
        unit, rstd = unit_of(
            widen(flat(xo_ref[rows, at : at + width]), flat(xt_ref[rows, at : at + width]))
        )
        p = gain_up * jnp.concatenate(
            [
                flat(qm_ref[1, rows]).astype(F32) + flat(qr_ref[0, rows]).astype(F32),
                flat(qm_ref[0, rows]).astype(F32) + flat(qr_ref[1, rows]).astype(F32),
            ],
            axis=1,
        )
        change = p[:, :HALF] - chan_mean(p) - unit[:, :HALF] * chan_mean(p * unit)
        g = flat(g_ref[rows, cut : cut + width]).astype(F32) + rstd * change
        g = jnp.where(live, g.reshape(n, width, HALF), 0.0).astype(BF)
        if gn_ref is not None:
            gn_ref[rows] = g
        s = flat(g.astype(F32) * d_ref[rows])
        scatter_s(block, s, r, n, sbuf, sown)

    row_loop(some, n)
    if block:
        q_phase(block, sbuf, w_ref, wq, q_ref)
    weight_phase(block, dims, idx_ref, sown, nk_ref, w_ref, gain_ref[...], wg_ref)


def finish_kernel(dims, slabs, all_ref, perm_ref, out_ref):
    own_chans, share, lines = dims
    bits = lines.bit_length() - 1
    col = lax.broadcasted_iota(jnp.int32, (own_chans, slabs * lines), 1)
    place = jnp.bitwise_and(col, lines - 1)
    row = jnp.right_shift(col, bits) * share + place
    pick = (lax.broadcasted_iota(jnp.int32, (own_chans, slabs * lines), 0) == row) & (place < share)
    pick = jnp.where(pick, 1.0, 0.0).astype(BF)
    for t in range(TAPS):
        grads = dot(pick, all_ref[:, t * CHANS : (t + 1) * CHANS], NN).astype(BF)
        out_ref[t] = dot(grads, perm_ref[...], NT)


def local(sizes, x_in, cot, w1, gain):
    nx, nz, ny, ns = sizes
    own_chans, rows = x_in.shape[1], x_in.shape[2]
    image = x_in.shape[3]
    shards = nx * nz
    share = own_chans // ny
    lines = 8
    while lines < share + 1:
        lines *= 2
    dims = (own_chans, share, lines)
    sec, ax, az = lax.axis_index("section"), lax.axis_index("x"), lax.axis_index("zh")
    core, slab = lax.axis_index("core"), lax.axis_index("slab")
    patch = ax * nz + az
    idx = jnp.stack([patch * OWN, slab, ax]).astype(jnp.int32)

    def other(value):
        return lax.ppermute(value, "core", [(0, 1), (1, 0)])

    order = np.arange(CHANS).reshape(shards, 2, own_chans)
    orders = [np.concatenate([order[:, h].ravel(), order[:, 1 - h].ravel()]) for h in (0, 1)]
    perms = np.stack([np.eye(CHANS, dtype=np.float32)[:, o] for o in orders])
    perm = lax.dynamic_index_in_dim(jnp.asarray(perms, BF), core, 0, keepdims=False)

    def mine(value, edge):
        value = lax.dynamic_index_in_dim(value, sec, 0, keepdims=False).transpose(1, 0, 2)
        return jnp.pad(value, ((0, 0), (0, 0), (edge, edge)))

    wide_x, wide_c = mine(x_in, 32), mine(cot, 16)
    windows = jnp.stack(
        [
            jnp.concatenate(
                [wide_x[:, :, OWN * p : OWN * p + XWIN], wide_c[:, :, OWN * p : OWN * p + CWIN]], axis=2
            )
            for p in range(shards)
        ]
    )
    recv = lax.all_to_all(windows, ("x", "zh"), 0, 0, tiled=True)

    packed = call(prep_kernel, shape((own_chans, CARRY), BF), [], (w1[0], gain, perm))
    wide = jnp.broadcast_to(packed[None], (ns * nz, own_chans, CARRY))
    wide, recv = lax.optimization_barrier((wide, recv))
    wide = lax.all_to_all(wide, ("section", "zh"), 0, 0, tiled=True)
    wide = wide.reshape(ns, nz * own_chans, CARRY)


    def from_chips(value):
        moves = [[(i, (i - j) % nx) for i in range(nx)] for j in range(1, nx)]
        return [value] + [lax.ppermute(value, "x", move) for move in moves]

    weights = [
        from_chips(wide[b]) if b < 2 else [lax.all_gather(wide[b], "x", axis=0, tiled=True)]
        for b in range(ns)
    ]

    every_row = lax.all_gather(recv, "slab", axis=0)
    x_own, cot_own = call(
        functools.partial(assemble_kernel, ny, rows),
        (shape((ROWS, XWIN, HALF), BF), shape((ROWS, CWIN, HALF), BF)),
        [],
        (every_row,),
    )

    taps3 = 3 * CHANS
    nk_shape = (ROWS + 2 * PAD, OWN, taps3)
    gain_shape = shape((1, CHANS), F32)
    halves, slopes, shifted, gains = [(x_own, other(x_own))], [], [], []
    for b in range(ns - 1):
        width = X_WIN[b + 1][1]
        pieces = len(weights[b])
        y, slope, nk, gain_b, *whole = call(
            functools.partial(forward_kernel, b, image, pieces),
            (
                shape((ROWS, width, HALF), BF),
                shape((ROWS, S_WIN[b][1], HALF), F32),
                shape(nk_shape, BF),
                gain_shape,
            )
            + (shape((HALF, CARRY), BF),) * (pieces > 1),
            [
                pltpu.VMEM((ROWS + 2 * PAD, width, taps3), BF),
                pltpu.VMEM((ROWS, width, HALF), F32),
            ],
            (idx, *halves[b], *weights[b]),
            (0,),
        )
        halves.append((y, other(y)))
        slopes.append(slope)
        shifted.append(nk)
        gains.append(gain_b)
        weights[b] = whole[0] if whole else weights[b][0]

    def back_scratch(b):
        width = S_WIN[b - 1][1]
        return [
            pltpu.VMEM((ROWS + 2 * PAD, width, 768), BF),
            pltpu.VMEM((ROWS, OWN, HALF), BF),
            pltpu.VMEM((3, 768, CHANS), BF),
        ]

    count = shards * lines
    wg_shape = shape((count, TAPS * CHANS), BF)
    width = X_WIN[4][1]
    sbuf_s, sown_s, wq_s = back_scratch(3)
    q, grads, gain_b = call(
        functools.partial(turn_kernel, dims),
        (shape((2, ROWS, S_WIN[2][1], HALF), BF), wg_shape, gain_shape),
        [
            pltpu.VMEM((ROWS + 2 * PAD, width, taps3), BF),
            pltpu.VMEM(nk_shape, BF),
            pltpu.VMEM((ROWS, width, HALF), F32),
            sbuf_s,
            sown_s,
            wq_s,
        ],
        (idx, *halves[3], cot_own, weights[3][0]),
        (0,),
    )
    gains.append(gain_b)

    def reduced(b, value):
        if b > 1:
            return lax.psum_scatter(value, "x", scatter_dimension=0, tiled=True)
        value = value.reshape(nx, nz * lines, LANES)
        value = lax.all_to_all(value, "x", 0, 0, tiled=True)
        return jnp.sum(value.astype(F32), axis=0).astype(BF)

    weight_parts = [None] * 3 + [reduced(3, grads)]
    g, first_g = cot_own, S_WIN[3][0]
    for b in (2, 1, 0):
        args = (
            idx, q, other(q), *halves[b + 1], g, gains[b + 1], slopes[b], weights[b], shifted[b], gains[b],
        )
        kernel = functools.partial(backward_kernel, b, dims, image, first_g)
        if b:
            sbuf_s, sown_s, wq_s = back_scratch(b)
            q, g, grads = call(
                kernel,
                (
                    shape((2, ROWS, S_WIN[b - 1][1], HALF), BF),
                    shape((ROWS, S_WIN[b][1], HALF), BF),
                    wg_shape,
                ),
                [sown_s, sbuf_s, wq_s],
                args,
                (0,),
            )
        else:
            (grads,) = call(kernel, (wg_shape,), [pltpu.VMEM((ROWS, OWN, HALF), BF)], args, (0,))
        first_g = S_WIN[b][0]
        weight_parts[b] = reduced(b, grads)

    parts = jnp.stack(weight_parts).reshape(ns * nz, lines, LANES)
    parts = lax.all_to_all(parts, ("section", "zh"), 0, 0, tiled=True)
    total = jnp.sum(parts.astype(F32), axis=0).astype(BF)
    every = lax.all_gather(total, "slab", axis=0, tiled=True)
    weight_grad = call(
        functools.partial(finish_kernel, dims, ny),
        shape((TAPS, own_chans, CHANS), F32),
        [],
        (every, perm),
    )
    gain_rows = every.reshape(ny, lines, LANES)[:, share, :CHANS]
    gain_all = jnp.sum(gain_rows.astype(F32), axis=0)
    here = lax.dynamic_slice_in_dim(gain_all, patch * own_chans, own_chans)
    there = lax.dynamic_slice_in_dim(gain_all, HALF + patch * own_chans, own_chans)
    gain_grad = here + other(there)
    return weight_grad[None], gain_grad[None]


def solution(mesh):
    ns, chans, ny = mesh.shape["section"], mesh.shape["ch"], mesh.shape["slab"]
    nz = 2 if chans % 4 == 0 else 1
    nx = chans // (2 * nz)
    axes = ("section", "x", "zh", "core", "slab")
    fine = Mesh(mesh.devices.reshape(ns, nx, nz, 2, ny), axes)
    ch = ("x", "zh", "core")
    return jax.shard_map(
        functools.partial(local, (nx, nz, ny, ns)),
        mesh=fine,
        in_specs=(
            P(None, ch, "slab", None),
            P(None, ch, "slab", None),
            P("section", None, ch, None),
            P("section", None),
        ),
        out_specs=(P("section", None, ch, None), P("section", ch)),
        check_vma=False,
    )
```

```python
import functools

import jax
import jax.numpy as jnp
import numpy as np
from jax import lax
from jax.experimental import pallas as pl
from jax.experimental.pallas import tpu as pltpu
from jax.sharding import Mesh, PartitionSpec as P

NORM_EPS = 1e-05
SLOPE_SCALE = 0.7978845608028654
CUBIC_COEF = 0.044715
BF = jnp.bfloat16
F32 = jnp.float32

ROWS = 32
CHANS = 384
HALF = 192
TAPS = 9
DIL = (1, 2, 4, 8)
OWN = 16
XWIN = 80
CWIN = 48
PAD = 8
X_WIN = ((0, 80), (0, 80), (0, 80), (8, 64), (16, 48))
S_WIN = ((32, 16), (24, 32), (24, 32), (16, 48))
VMEM_LIMIT = 56 * 1024 * 1024
PARAMS = pltpu.CompilerParams(vmem_limit_bytes=VMEM_LIMIT)
NT = (((1,), (1,)), ((), ()))
NN = (((1,), (0,)), ((), ()))
LANES = TAPS * CHANS
CARRY = LANES + 128
R_NORM, R_EPI, R_TURN, R_BACK = 4, 2, 2, 8


def dot(a, b, dims):
    return lax.dot_general(a, b, dims, preferred_element_type=F32)


def call(kernel, out_shape, scratch, args, smem=(), far=(), far_out=()):
    vm = pl.BlockSpec(memory_space=pltpu.VMEM)
    sm = pl.BlockSpec(memory_space=pltpu.SMEM)
    hb = pl.BlockSpec(memory_space=pltpu.HBM)
    if isinstance(out_shape, tuple):
        out_specs = tuple(hb if i in far_out else vm for i in range(len(out_shape)))
    else:
        out_specs = vm
    return pl.pallas_call(
        kernel,
        out_shape=out_shape,
        in_specs=[sm if i in smem else hb if i in far else vm for i in range(len(args))],
        out_specs=out_specs,
        scratch_shapes=scratch,
        compiler_params=PARAMS,
    )(*args)


def shape(dims, dtype):
    return jax.ShapeDtypeStruct(dims, dtype)


def row_loop(body, rows, unroll=1):
    span = rows * unroll

    def step(i, carry):
        for k in range(unroll):
            body(pl.multiple_of(i * span, span) + k * rows)
        return carry

    lax.fori_loop(0, ROWS // span, step, 0)


def flat(value):
    return value.reshape(value.shape[0] * value.shape[1], value.shape[2])


def in_image(base, first, count, width):
    cols = lax.broadcasted_iota(jnp.int32, (1, count, HALF), 1) + (base - 32 + first)
    return (cols >= 0) & (cols < width)


def widen(own, oth):
    return jnp.concatenate([own.astype(F32), oth.astype(F32)], axis=1)


def chan_mean(value):
    folded = value[:, :128] + value[:, 128:256] + value[:, 256:]
    return jnp.sum(folded, axis=1, keepdims=True) / CHANS


def unit_of(value):
    mean = chan_mean(value)
    rstd = lax.rsqrt(chan_mean(value * value) - mean * mean + NORM_EPS)
    return (value - mean) * rstd, rstd


def read_gain(w_ref):
    tile = w_ref[0:16, LANES:CARRY].astype(F32)
    return jnp.concatenate(
        [(tile[p : p + 1] + tile[3 + p : 4 + p]) + tile[6 + p : 7 + p] for p in range(3)], axis=1
    )


def gelu_inner(pre):
    return jnp.tanh(SLOPE_SCALE * (pre + CUBIC_COEF * pre * pre * pre))


def gelu_slope(pre, tangent):
    return 0.5 * (1.0 + tangent) + 0.5 * pre * (1.0 - tangent * tangent) * SLOPE_SCALE * (
        1.0 + 3.0 * CUBIC_COEF * pre * pre
    )


def prep_kernel(w_ref, gain_ref, perm_ref, out_ref):
    for t in range(TAPS):
        out_ref[:, t * CHANS : (t + 1) * CHANS] = dot(w_ref[t], perm_ref[...], NN).astype(BF)
    rest = jnp.broadcast_to(gain_ref[...], (8, CHANS))
    row = lax.broadcasted_iota(jnp.int32, (out_ref.shape[0], 128), 0)
    tile = jnp.zeros((out_ref.shape[0], 128), F32)
    for k in range(3):
        piece = rest.astype(BF)
        rest = rest - piece.astype(F32)
        moved = dot(piece, perm_ref[...], NN)
        for p in range(3):
            tile = jnp.where(row == 3 * k + p, moved[0:1, 128 * p : 128 * p + 128], tile)
    out_ref[:, LANES:CARRY] = tile.astype(BF)


def window_kernel(idx_ref, x_ref, cot_ref, out_ref):
    shards, rows, chans, lanes = out_ref.shape
    image = x_ref.shape[3]
    x = x_ref[idx_ref[3]].astype(F32)
    cot = cot_ref[idx_ref[3]].astype(F32)
    lane = lax.broadcasted_iota(jnp.int32, (chans, lanes), 1)
    room = jnp.zeros((chans, lanes - image), F32)
    for r in range(rows):
        from_x, from_cot = x[:, r, :], cot[:, r, :]
        if image < lanes:
            from_x = jnp.concatenate([from_x, room], axis=1)
            from_cot = jnp.concatenate([from_cot, room], axis=1)
        for p in range(shards):
            here = None
            for value, start in ((from_x, OWN * p - 32), (from_cot, OWN * p - 16 - XWIN)):
                shift = (-start) % lanes
                moved = pltpu.roll(value, shift, 1) if shift else value
                moved = jnp.where((lane + start >= 0) & (lane + start < image), moved, 0.0)
                here = moved if here is None else jnp.where(lane < XWIN, here, moved)
            out_ref[p, r] = here.astype(BF)


def assemble_kernel(slabs, rows, recv_ref, x_ref, cot_ref):
    lanes = XWIN + CWIN
    eye = (
        lax.broadcasted_iota(jnp.int32, (lanes, lanes), 0)
        == lax.broadcasted_iota(jnp.int32, (lanes, lanes), 1)
    ).astype(F32).astype(BF)

    def one(r, carry):
        for y in range(slabs):
            piece = recv_ref[y, :, pl.ds(r, 1)].astype(F32)
            piece = piece.reshape(HALF, lanes).astype(BF)
            flipped = dot(eye, piece, NT).astype(BF)
            x_ref[pl.ds(y * rows + r, 1)] = flipped[:XWIN].reshape(1, XWIN, HALF)
            cot_ref[pl.ds(y * rows + r, 1)] = flipped[XWIN:].reshape(1, CWIN, HALF)
        return carry

    lax.fori_loop(0, rows, one, 0)


def norm_phase(block, xo_ref, xt_ref, gain, nbuf, nk):
    d = DIL[block]
    first_in, width_in = X_WIN[block]
    first_out, width_out = X_WIN[block + 1]
    low = first_out - first_in
    own = 32 - first_in
    for edge in (0, PAD + ROWS):
        nbuf[edge : edge + PAD] = jnp.zeros((PAD, width_out, 3 * CHANS), BF)
        nk[edge : edge + PAD] = jnp.zeros((PAD, OWN, 3 * CHANS), BF)
    n = R_NORM

    def some(r):
        unit, _ = unit_of(widen(flat(xo_ref[pl.ds(r, n)]), flat(xt_ref[pl.ds(r, n)])))
        both = unit * gain
        for kx in range(3):
            shift = (-(kx - 1) * d) % (n * width_in)
            moved = pltpu.roll(both, shift, 0) if shift else both
            moved = moved.reshape(n, width_in, CHANS)
            lanes = slice(kx * CHANS, (kx + 1) * CHANS)
            nbuf[pl.ds(PAD + r, n), :, lanes] = moved[:, low : low + width_out].astype(BF)
            nk[pl.ds(PAD + r, n), :, lanes] = moved[:, own : own + OWN].astype(BF)

    row_loop(some, n)


def conv_phase(block, nbuf, w_ref, pre):
    d = DIL[block]
    width = X_WIN[block + 1][1]
    step = 8

    def one(i, carry):
        r0 = i * step
        acc = None
        for ky in range(3):
            left = nbuf[pl.ds(PAD + r0 + (ky - 1) * d, step)].reshape(step * width, 3 * CHANS)
            term = dot(left, w_ref[:, ky * 3 * CHANS : (ky + 1) * 3 * CHANS], NT)
            acc = term if acc is None else acc + term
        pre[pl.ds(r0, step)] = acc.reshape(step, width, HALF)
        return carry

    lax.fori_loop(0, ROWS // step, one, 0)


def forward_kernel(block, image, pieces, spin, idx_ref, xo_ref, xt_ref, *rest):
    w_refs, rest = rest[:pieces], rest[pieces:]
    y_ref, d_ref, gain_ref, nk_far, *rest = rest
    w_ref = w_refs[0]
    whole = None
    if pieces > 1:
        whole_far, nk, nbuf, pre, sem, w_ref = rest
        lines = HALF // pieces
        for j in range(pieces):
            place = lax.rem(idx_ref[spin] + j, pieces) * lines
            w_ref[pl.ds(pl.multiple_of(place, lines), lines)] = w_refs[j][...]
        whole = pltpu.make_async_copy(w_ref, whole_far, sem.at[1])
        whole.start()
    else:
        nk, nbuf, pre, sem = rest
    first_in = X_WIN[block][0]
    first_out, width_out = X_WIN[block + 1]
    first_s, width_s = S_WIN[block]
    gain = read_gain(w_ref)
    gain_ref[...] = gain
    norm_phase(block, xo_ref, xt_ref, gain, nbuf, nk)
    kept = pltpu.make_async_copy(nk, nk_far, sem.at[0])
    kept.start()
    conv_phase(block, nbuf, w_ref, pre)
    live = in_image(idx_ref[0], first_out, width_out, image)
    low, at = first_out - first_in, first_s - first_out
    n = R_EPI

    def some(r):
        act = pre[pl.ds(r, n)]
        tangent = gelu_inner(act)
        out = xo_ref[pl.ds(r, n)].astype(F32)[:, low : low + width_out] + 0.5 * act * (1.0 + tangent)
        y_ref[pl.ds(r, n)] = jnp.where(live, out, 0.0).astype(BF)
        d_ref[pl.ds(r, n)] = gelu_slope(act[:, at : at + width_s], tangent[:, at : at + width_s])

    row_loop(some, n)
    kept.wait()
    if whole is not None:
        whole.wait()


def scatter_s(block, s, r, n, sbuf, sown):
    first, width = S_WIN[block]
    rows = s.reshape(n, width, HALF)
    sown[pl.ds(r, n)] = rows[:, 32 - first : 32 - first + OWN].astype(BF)
    if sbuf is None:
        return
    d = DIL[block]
    first_q, width_q = S_WIN[block - 1]
    low = first_q - first
    gap = jnp.zeros((n * width, 256 - HALF), F32)
    wide = jnp.concatenate([s, gap], axis=1)
    for kx in range(3):
        shift = ((kx - 1) * d) % (n * width)
        moved = pltpu.roll(wide, shift, 0) if shift else wide
        moved = moved.reshape(n, width, 256)[:, low : low + width_q]
        sbuf[pl.ds(PAD + r, n), :, kx * 256 : (kx + 1) * 256] = moved.astype(BF)


def q_phase(block, sbuf, w_ref, wq, q_ref):
    d = DIL[block]
    width = S_WIN[block - 1][1]
    for ky in range(3):
        for kx in range(3):
            t = 3 * ky + kx
            wq[ky, kx * 256 : kx * 256 + HALF] = w_ref[:, t * CHANS : (t + 1) * CHANS]
            wq[ky, kx * 256 + HALF : (kx + 1) * 256] = jnp.zeros((256 - HALF, CHANS), BF)
    for edge in (0, PAD + ROWS):
        sbuf[edge : edge + PAD] = jnp.zeros((PAD, width, 768), BF)
    step = 512 // width

    def one(i, carry):
        r0 = i * step
        acc = None
        for ky in range(3):
            left = sbuf[pl.ds(PAD + r0 - (ky - 1) * d, step)].reshape(step * width, 768)
            term = dot(left, wq[ky], NN)
            acc = term if acc is None else acc + term
        q_ref[0, pl.ds(r0, step)] = acc[:, HALF:].reshape(step, width, HALF).astype(BF)
        q_ref[1, pl.ds(r0, step)] = acc[:, :HALF].reshape(step, width, HALF).astype(BF)
        return carry

    lax.fori_loop(0, ROWS // step, one, 0)


def weight_phase(block, dims, idx_ref, sown, nk, w_ref, gain, wg_ref):
    own_chans, share, lines = dims
    d = DIL[block]
    count = (HALF // own_chans) * lines
    bits = lines.bit_length() - 1
    line = lax.broadcasted_iota(jnp.int32, (count, HALF), 0)
    place = jnp.bitwise_and(line, lines - 1)
    want = jnp.right_shift(line, bits) * own_chans + share * idx_ref[1] + place
    pick = (lax.broadcasted_iota(jnp.int32, (count, HALF), 1) == want) & (place < share)
    pick = jnp.where(pick, 1.0, 0.0).astype(BF)
    left = dot(pick, sown[...].reshape(ROWS * OWN, HALF), NT).astype(BF)
    total = jnp.zeros((1, CHANS), F32)
    first = None
    for ky in range(3):
        lanes = slice(ky * 3 * CHANS, (ky + 1) * 3 * CHANS)
        start = PAD + (ky - 1) * d
        right = nk[start : start + ROWS].reshape(ROWS * OWN, 3 * CHANS)
        grads = dot(left, right, NN)
        wg_ref[:, lanes] = grads.astype(BF)
        part = jnp.sum(grads * dot(pick, w_ref[:, lanes], NN), axis=0, keepdims=True)
        for kx in range(3):
            total = total + part[:, kx * CHANS : (kx + 1) * CHANS]
        if ky == 0:
            first = grads[:, :CHANS]
    spot = jnp.bitwise_and(lax.broadcasted_iota(jnp.int32, (count, CHANS), 0), lines - 1)
    wg_ref[:, :CHANS] = jnp.where(spot == share, total / gain, first).astype(BF)


def turn_kernel(dims, idx_ref, xo_ref, xt_ref, cot_ref, w_ref, q_ref, wg_ref, gain_ref,
                nbuf, nk, pre, sbuf, sown, wq):
    gain = read_gain(w_ref)
    gain_ref[...] = gain
    norm_phase(3, xo_ref, xt_ref, gain, nbuf, nk)
    conv_phase(3, nbuf, w_ref, pre)
    n = R_TURN

    def some(r):
        act = flat(pre[pl.ds(r, n)])
        s = flat(cot_ref[pl.ds(r, n)]).astype(F32) * gelu_slope(act, gelu_inner(act))
        scatter_s(3, s, r, n, sbuf, sown)

    row_loop(some, n)
    q_phase(3, sbuf, w_ref, wq, q_ref)
    weight_phase(3, dims, idx_ref, sown, nk, w_ref, gain, wg_ref)


def backward_kernel(block, dims, image, first_g, idx_ref, qm_ref, qr_ref, xo_ref, xt_ref, g_ref,
                    gain_up_ref, d_ref, w_far, nk_far, gain_ref, *rest):
    if block:
        q_ref, gn_ref, wg_ref, w_ref, nk_ref, sem, sown, sbuf, wq = rest
    else:
        wg_ref, w_ref, nk_ref, sem, sown = rest
        q_ref = gn_ref = sbuf = wq = None
    weights_in = pltpu.make_async_copy(w_far, w_ref, sem.at[0])
    kept_in = pltpu.make_async_copy(nk_far, nk_ref, sem.at[1])
    weights_in.start()
    kept_in.start()
    first, width = S_WIN[block]
    at = first - X_WIN[block + 1][0]
    cut = first - first_g
    live = in_image(idx_ref[0], first, width, image)
    gain_up = gain_up_ref[...]
    n = R_BACK

    def some(r):
        rows = pl.ds(r, n)
        unit, rstd = unit_of(
            widen(flat(xo_ref[rows, at : at + width]), flat(xt_ref[rows, at : at + width]))
        )
        p = gain_up * jnp.concatenate(
            [
                flat(qm_ref[1, rows]).astype(F32) + flat(qr_ref[0, rows]).astype(F32),
                flat(qm_ref[0, rows]).astype(F32) + flat(qr_ref[1, rows]).astype(F32),
            ],
            axis=1,
        )
        change = p[:, :HALF] - chan_mean(p) - unit[:, :HALF] * chan_mean(p * unit)
        g = flat(g_ref[rows, cut : cut + width]).astype(F32) + rstd * change
        g = jnp.where(live, g.reshape(n, width, HALF), 0.0).astype(BF)
        if gn_ref is not None:
            gn_ref[rows] = g
        s = flat(g.astype(F32) * d_ref[rows])
        scatter_s(block, s, r, n, sbuf, sown)

    row_loop(some, n)
    weights_in.wait()
    if block:
        q_phase(block, sbuf, w_ref, wq, q_ref)
    kept_in.wait()
    weight_phase(block, dims, idx_ref, sown, nk_ref, w_ref, gain_ref[...], wg_ref)


def finish_kernel(dims, slabs, all_ref, perm_ref, out_ref):
    own_chans, share, lines = dims
    bits = lines.bit_length() - 1
    col = lax.broadcasted_iota(jnp.int32, (own_chans, slabs * lines), 1)
    place = jnp.bitwise_and(col, lines - 1)
    row = jnp.right_shift(col, bits) * share + place
    pick = (lax.broadcasted_iota(jnp.int32, (own_chans, slabs * lines), 0) == row) & (place < share)
    pick = jnp.where(pick, 1.0, 0.0).astype(BF)
    for t in range(TAPS):
        grads = dot(pick, all_ref[:, t * CHANS : (t + 1) * CHANS], NN).astype(BF)
        out_ref[t] = dot(grads, perm_ref[...], NT)


def local(sizes, x_in, cot, w1, gain):
    nx, nz, ny, ns = sizes
    own_chans, rows = x_in.shape[1], x_in.shape[2]
    image = x_in.shape[3]
    shards = nx * nz
    share = own_chans // ny
    lines = 8
    while lines < share + 1:
        lines *= 2
    dims = (own_chans, share, lines)
    sec, ax, az = lax.axis_index("section"), lax.axis_index("x"), lax.axis_index("zh")
    core, slab = lax.axis_index("core"), lax.axis_index("slab")
    patch = ax * nz + az
    idx = jnp.stack([patch * OWN, slab, ax, sec]).astype(jnp.int32)

    def other(value):
        return lax.ppermute(value, "core", [(0, 1), (1, 0)])

    order = np.arange(CHANS).reshape(shards, 2, own_chans)
    orders = [np.concatenate([order[:, h].ravel(), order[:, 1 - h].ravel()]) for h in (0, 1)]
    perms = np.stack([np.eye(CHANS, dtype=np.float32)[:, o] for o in orders])
    perm = lax.dynamic_index_in_dim(jnp.asarray(perms, BF), core, 0, keepdims=False)

    windows = call(
        window_kernel, shape((shards, rows, own_chans, XWIN + CWIN), BF), [], (idx, x_in, cot), (0,)
    )
    recv = lax.all_to_all(windows, ("x", "zh"), 0, 0, tiled=True)

    packed = call(prep_kernel, shape((own_chans, CARRY), BF), [], (w1[0], gain, perm))
    if nx == ny:
        turn = []
        for n in range(ns * nx * ny):
            b, i, j = n // (nx * ny), n // ny % nx, n % ny
            turn.append((n, (b * nx + j) * ny + i if b % 2 else n))
        packed = lax.ppermute(packed, ("section", "x", "slab"), turn)
    wide = jnp.broadcast_to(packed[None], (ns * nz, own_chans, CARRY))
    wide, recv = lax.optimization_barrier((wide, recv))
    wide = lax.all_to_all(wide, ("section", "zh"), 0, 0, tiled=True)
    wide = wide.reshape(ns, nz * own_chans, CARRY)


    def from_chips(value, axis, size):
        moves = [[(i, (i - j) % size) for i in range(size)] for j in range(1, size)]
        return [value] + [lax.ppermute(value, axis, move) for move in moves]

    along = [("slab" if b % 2 and nx == ny else "x") for b in range(ns)]
    weights = [
        [lax.all_gather(wide[b], along[b], axis=0, tiled=True)] if b % 2 else from_chips(wide[b], "x", nx)
        for b in range(ns)
    ]

    every_row = lax.all_gather(recv, "slab", axis=0)
    x_own, cot_own = call(
        functools.partial(assemble_kernel, ny, rows),
        (shape((ROWS, XWIN, HALF), BF), shape((ROWS, CWIN, HALF), BF)),
        [],
        (every_row,),
    )

    taps3 = 3 * CHANS
    nk_shape = (ROWS + 2 * PAD, OWN, taps3)
    gain_shape = shape((1, CHANS), F32)
    halves, slopes, shifted, gains = [(x_own, other(x_own))], [], [], []
    for b in range(ns - 1):
        width = X_WIN[b + 1][1]
        pieces = len(weights[b])
        many = pieces > 1
        whole_shape = shape((HALF, CARRY), BF)
        y, slope, gain_b, nk, *whole = call(
            functools.partial(forward_kernel, b, image, pieces, 2),
            (
                shape((ROWS, width, HALF), BF),
                shape((ROWS, S_WIN[b][1], HALF), F32),
                gain_shape,
                shape(nk_shape, BF),
            )
            + (whole_shape,) * many,
            [
                pltpu.VMEM(nk_shape, BF),
                pltpu.VMEM((ROWS + 2 * PAD, width, taps3), BF),
                pltpu.VMEM((ROWS, width, HALF), F32),
                pltpu.SemaphoreType.DMA((2,)),
            ]
            + [pltpu.VMEM((HALF, CARRY), BF)] * many,
            (idx, *halves[b], *weights[b]),
            (0,),
            (),
            (3, 4),
        )
        halves.append((y, other(y)))
        slopes.append(slope)
        shifted.append(nk)
        gains.append(gain_b)
        weights[b] = whole[0] if whole else weights[b][0]

    def back_scratch(b):
        width = S_WIN[b - 1][1]
        return [
            pltpu.VMEM((ROWS + 2 * PAD, width, 768), BF),
            pltpu.VMEM((ROWS, OWN, HALF), BF),
            pltpu.VMEM((3, 768, CHANS), BF),
        ]

    count = shards * lines
    wg_shape = shape((count, TAPS * CHANS), BF)
    width = X_WIN[4][1]
    sbuf_s, sown_s, wq_s = back_scratch(3)
    q, grads, gain_b = call(
        functools.partial(turn_kernel, dims),
        (shape((2, ROWS, S_WIN[2][1], HALF), BF), wg_shape, gain_shape),
        [
            pltpu.VMEM((ROWS + 2 * PAD, width, taps3), BF),
            pltpu.VMEM(nk_shape, BF),
            pltpu.VMEM((ROWS, width, HALF), F32),
            sbuf_s,
            sown_s,
            wq_s,
        ],
        (idx, *halves[3], cot_own, weights[3][0]),
        (0,),
    )
    gains.append(gain_b)

    def reduced(b, value):
        if b > 1:
            return lax.psum_scatter(value, "x", scatter_dimension=0, tiled=True)
        value = value.reshape(nx, nz * lines, LANES)
        value = lax.all_to_all(value, "x", 0, 0, tiled=True)
        return jnp.sum(value.astype(F32), axis=0).astype(BF)

    weight_parts = [None] * 3 + [reduced(3, grads)]
    g, first_g = cot_own, S_WIN[3][0]
    for b in (2, 1, 0):
        args = (
            idx, q, other(q), *halves[b + 1], g, gains[b + 1], slopes[b], weights[b], shifted[b], gains[b],
        )
        kernel = functools.partial(backward_kernel, b, dims, image, first_g)
        fetched = [
            pltpu.VMEM((HALF, CARRY), BF),
            pltpu.VMEM(nk_shape, BF),
            pltpu.SemaphoreType.DMA((2,)),
        ]
        if b:
            sbuf_s, sown_s, wq_s = back_scratch(b)
            q, g, grads = call(
                kernel,
                (
                    shape((2, ROWS, S_WIN[b - 1][1], HALF), BF),
                    shape((ROWS, S_WIN[b][1], HALF), BF),
                    wg_shape,
                ),
                fetched + [sown_s, sbuf_s, wq_s],
                args,
                (0,),
                (8, 9),
            )
        else:
            own_s = pltpu.VMEM((ROWS, OWN, HALF), BF)
            (grads,) = call(kernel, (wg_shape,), fetched + [own_s], args, (0,), (8, 9))
        first_g = S_WIN[b][0]
        weight_parts[b] = reduced(b, grads)

    parts = jnp.stack(weight_parts).reshape(ns * nz, lines, LANES)
    parts = lax.all_to_all(parts, ("section", "zh"), 0, 0, tiled=True)
    total = jnp.sum(parts.astype(F32), axis=0).astype(BF)
    every = lax.all_gather(total, "slab", axis=0, tiled=True)
    weight_grad = call(
        functools.partial(finish_kernel, dims, ny),
        shape((TAPS, own_chans, CHANS), F32),
        [],
        (every, perm),
    )
    gain_rows = every.reshape(ny, lines, LANES)[:, share, :CHANS]
    gain_all = jnp.sum(gain_rows.astype(F32), axis=0)
    here = lax.dynamic_slice_in_dim(gain_all, patch * own_chans, own_chans)
    there = lax.dynamic_slice_in_dim(gain_all, HALF + patch * own_chans, own_chans)
    gain_grad = here + other(there)
    return weight_grad[None], gain_grad[None]


def solution(mesh):
    ns, chans, ny = mesh.shape["section"], mesh.shape["ch"], mesh.shape["slab"]
    nz = 2 if chans % 4 == 0 else 1
    nx = chans // (2 * nz)
    axes = ("section", "x", "zh", "core", "slab")
    fine = Mesh(mesh.devices.reshape(ns, nx, nz, 2, ny), axes)
    ch = ("x", "zh", "core")
    return jax.shard_map(
        functools.partial(local, (nx, nz, ny, ns)),
        mesh=fine,
        in_specs=(
            P(None, ch, "slab", None),
            P(None, ch, "slab", None),
            P("section", None, ch, None),
            P("section", None),
        ),
        out_specs=(P("section", None, ch, None), P("section", ch)),
        check_vma=False,
    )
```

```python
import functools

import jax
import jax.numpy as jnp
import numpy as np
from jax import lax
from jax.experimental import pallas as pl
from jax.experimental.pallas import tpu as pltpu
from jax.sharding import Mesh, PartitionSpec as P

NORM_EPS = 1e-05
SLOPE_SCALE = 0.7978845608028654
CUBIC_COEF = 0.044715
BF = jnp.bfloat16
F32 = jnp.float32

ROWS = 32
CHANS = 384
HALF = 192
TAPS = 9
DIL = (1, 2, 4, 8)
OWN = 16
XWIN = 80
CWIN = 48
PAD = 8
X_WIN = ((0, 80), (0, 80), (0, 80), (8, 64), (16, 48))
S_WIN = ((32, 16), (24, 32), (24, 32), (16, 48))
VMEM_LIMIT = 56 * 1024 * 1024
PARAMS = pltpu.CompilerParams(vmem_limit_bytes=VMEM_LIMIT)
NT = (((1,), (1,)), ((), ()))
NN = (((1,), (0,)), ((), ()))
LANES = TAPS * CHANS
CARRY = LANES + 128
R_NORM, R_EPI, R_TURN, R_BACK = 4, 2, 2, 8


def dot(a, b, dims):
    return lax.dot_general(a, b, dims, preferred_element_type=F32)


def call(kernel, out_shape, scratch, args, smem=(), far=(), far_out=(), micros=2):
    vm = pl.BlockSpec(memory_space=pltpu.VMEM)
    sm = pl.BlockSpec(memory_space=pltpu.SMEM)
    hb = pl.BlockSpec(memory_space=pltpu.HBM)
    if isinstance(out_shape, tuple):
        out_specs = tuple(hb if i in far_out else vm for i in range(len(out_shape)))
    else:
        out_specs = vm
    return pl.pallas_call(
        kernel,
        out_shape=out_shape,
        in_specs=[sm if i in smem else hb if i in far else vm for i in range(len(args))],
        out_specs=out_specs,
        scratch_shapes=scratch,
        compiler_params=PARAMS,
        cost_estimate=pl.CostEstimate(flops=micros * 10**9, bytes_accessed=micros * 10**6, transcendentals=0),
    )(*args)


def shape(dims, dtype):
    return jax.ShapeDtypeStruct(dims, dtype)


def row_loop(body, rows, unroll=1):
    span = rows * unroll

    def step(i, carry):
        for k in range(unroll):
            body(pl.multiple_of(i * span, span) + k * rows)
        return carry

    lax.fori_loop(0, ROWS // span, step, 0)


def flat(value):
    return value.reshape(value.shape[0] * value.shape[1], value.shape[2])


def in_image(base, first, count, width):
    cols = lax.broadcasted_iota(jnp.int32, (1, count, HALF), 1) + (base - 32 + first)
    return (cols >= 0) & (cols < width)


def widen(own, oth):
    return jnp.concatenate([own.astype(F32), oth.astype(F32)], axis=1)


def chan_mean(value):
    folded = value[:, :128] + value[:, 128:256] + value[:, 256:]
    return jnp.sum(folded, axis=1, keepdims=True) / CHANS


def unit_of(value):
    mean = chan_mean(value)
    rstd = lax.rsqrt(chan_mean(value * value) - mean * mean + NORM_EPS)
    return (value - mean) * rstd, rstd


def read_gain(w_ref):
    tile = w_ref[0:16, LANES:CARRY].astype(F32)
    return jnp.concatenate(
        [(tile[p : p + 1] + tile[3 + p : 4 + p]) + tile[6 + p : 7 + p] for p in range(3)], axis=1
    )


def gelu_inner(pre):
    return jnp.tanh(SLOPE_SCALE * (pre + CUBIC_COEF * pre * pre * pre))


def gelu_slope(pre, tangent):
    return 0.5 * (1.0 + tangent) + 0.5 * pre * (1.0 - tangent * tangent) * SLOPE_SCALE * (
        1.0 + 3.0 * CUBIC_COEF * pre * pre
    )


def prep_kernel(w_ref, gain_ref, perm_ref, out_ref):
    for t in range(TAPS):
        out_ref[:, t * CHANS : (t + 1) * CHANS] = dot(w_ref[t], perm_ref[...], NN).astype(BF)
    rest = jnp.broadcast_to(gain_ref[...], (8, CHANS))
    row = lax.broadcasted_iota(jnp.int32, (out_ref.shape[0], 128), 0)
    tile = jnp.zeros((out_ref.shape[0], 128), F32)
    for k in range(3):
        piece = rest.astype(BF)
        rest = rest - piece.astype(F32)
        moved = dot(piece, perm_ref[...], NN)
        for p in range(3):
            tile = jnp.where(row == 3 * k + p, moved[0:1, 128 * p : 128 * p + 128], tile)
    out_ref[:, LANES:CARRY] = tile.astype(BF)


def window_kernel(idx_ref, x_ref, cot_ref, out_ref):
    shards, rows, chans, lanes = out_ref.shape
    image = x_ref.shape[3]
    x = x_ref[idx_ref[3]].astype(F32)
    cot = cot_ref[idx_ref[3]].astype(F32)
    lane = lax.broadcasted_iota(jnp.int32, (chans, lanes), 1)
    room = jnp.zeros((chans, lanes - image), F32)
    for r in range(rows):
        from_x, from_cot = x[:, r, :], cot[:, r, :]
        if image < lanes:
            from_x = jnp.concatenate([from_x, room], axis=1)
            from_cot = jnp.concatenate([from_cot, room], axis=1)
        for p in range(shards):
            here = None
            for value, start in ((from_x, OWN * p - 32), (from_cot, OWN * p - 16 - XWIN)):
                shift = (-start) % lanes
                moved = pltpu.roll(value, shift, 1) if shift else value
                moved = jnp.where((lane + start >= 0) & (lane + start < image), moved, 0.0)
                here = moved if here is None else jnp.where(lane < XWIN, here, moved)
            out_ref[p, r] = here.astype(BF)


def assemble_kernel(slabs, rows, recv_ref, x_ref, cot_ref):
    lanes = XWIN + CWIN
    eye = (
        lax.broadcasted_iota(jnp.int32, (lanes, lanes), 0)
        == lax.broadcasted_iota(jnp.int32, (lanes, lanes), 1)
    ).astype(F32).astype(BF)

    def one(r, carry):
        for y in range(slabs):
            piece = recv_ref[y, :, pl.ds(r, 1)].astype(F32)
            piece = piece.reshape(HALF, lanes).astype(BF)
            flipped = dot(eye, piece, NT).astype(BF)
            x_ref[pl.ds(y * rows + r, 1)] = flipped[:XWIN].reshape(1, XWIN, HALF)
            cot_ref[pl.ds(y * rows + r, 1)] = flipped[XWIN:].reshape(1, CWIN, HALF)
        return carry

    lax.fori_loop(0, rows, one, 0)


def norm_phase(block, xo_ref, xt_ref, gain, nbuf, nk):
    d = DIL[block]
    first_in, width_in = X_WIN[block]
    first_out, width_out = X_WIN[block + 1]
    low = first_out - first_in
    own = 32 - first_in
    for edge in (0, PAD + ROWS):
        nbuf[edge : edge + PAD] = jnp.zeros((PAD, width_out, 3 * CHANS), BF)
        nk[edge : edge + PAD] = jnp.zeros((PAD, OWN, 3 * CHANS), BF)
    n = R_NORM

    def some(r):
        unit, _ = unit_of(widen(flat(xo_ref[pl.ds(r, n)]), flat(xt_ref[pl.ds(r, n)])))
        both = unit * gain
        for kx in range(3):
            shift = (-(kx - 1) * d) % (n * width_in)
            moved = pltpu.roll(both, shift, 0) if shift else both
            moved = moved.reshape(n, width_in, CHANS)
            lanes = slice(kx * CHANS, (kx + 1) * CHANS)
            nbuf[pl.ds(PAD + r, n), :, lanes] = moved[:, low : low + width_out].astype(BF)
            nk[pl.ds(PAD + r, n), :, lanes] = moved[:, own : own + OWN].astype(BF)

    row_loop(some, n)


def conv_phase(block, nbuf, w_ref, pre):
    d = DIL[block]
    width = X_WIN[block + 1][1]
    step = 8

    def one(i, carry):
        r0 = i * step
        acc = None
        for ky in range(3):
            left = nbuf[pl.ds(PAD + r0 + (ky - 1) * d, step)].reshape(step * width, 3 * CHANS)
            term = dot(left, w_ref[:, ky * 3 * CHANS : (ky + 1) * 3 * CHANS], NT)
            acc = term if acc is None else acc + term
        pre[pl.ds(r0, step)] = acc.reshape(step, width, HALF)
        return carry

    lax.fori_loop(0, ROWS // step, one, 0)


def forward_kernel(block, image, pieces, spin, idx_ref, xo_ref, xt_ref, *rest):
    w_refs, rest = rest[:pieces], rest[pieces:]
    y_ref, d_ref, gain_ref, nk_far, *rest = rest
    w_ref = w_refs[0]
    whole = None
    if pieces > 1:
        whole_far, nk, nbuf, pre, sem, w_ref = rest
        lines = HALF // pieces
        for j in range(pieces):
            place = lax.rem(idx_ref[spin] + j, pieces) * lines
            w_ref[pl.ds(pl.multiple_of(place, lines), lines)] = w_refs[j][...]
        whole = pltpu.make_async_copy(w_ref, whole_far, sem.at[1])
        whole.start()
    else:
        nk, nbuf, pre, sem = rest
    first_in = X_WIN[block][0]
    first_out, width_out = X_WIN[block + 1]
    first_s, width_s = S_WIN[block]
    gain = read_gain(w_ref)
    gain_ref[...] = gain
    norm_phase(block, xo_ref, xt_ref, gain, nbuf, nk)
    kept = pltpu.make_async_copy(nk, nk_far, sem.at[0])
    kept.start()
    conv_phase(block, nbuf, w_ref, pre)
    live = in_image(idx_ref[0], first_out, width_out, image)
    low, at = first_out - first_in, first_s - first_out
    n = R_EPI

    def some(r):
        act = pre[pl.ds(r, n)]
        tangent = gelu_inner(act)
        out = xo_ref[pl.ds(r, n)].astype(F32)[:, low : low + width_out] + 0.5 * act * (1.0 + tangent)
        y_ref[pl.ds(r, n)] = jnp.where(live, out, 0.0).astype(BF)
        d_ref[pl.ds(r, n)] = gelu_slope(act[:, at : at + width_s], tangent[:, at : at + width_s])

    row_loop(some, n)
    kept.wait()
    if whole is not None:
        whole.wait()


def scatter_s(block, s, r, n, sbuf, sown):
    first, width = S_WIN[block]
    rows = s.reshape(n, width, HALF)
    sown[pl.ds(r, n)] = rows[:, 32 - first : 32 - first + OWN].astype(BF)
    if sbuf is None:
        return
    d = DIL[block]
    first_q, width_q = S_WIN[block - 1]
    low = first_q - first
    gap = jnp.zeros((n * width, 256 - HALF), F32)
    wide = jnp.concatenate([s, gap], axis=1)
    for kx in range(3):
        shift = ((kx - 1) * d) % (n * width)
        moved = pltpu.roll(wide, shift, 0) if shift else wide
        moved = moved.reshape(n, width, 256)[:, low : low + width_q]
        sbuf[pl.ds(PAD + r, n), :, kx * 256 : (kx + 1) * 256] = moved.astype(BF)


def q_phase(block, sbuf, w_ref, wq, q_ref):
    d = DIL[block]
    width = S_WIN[block - 1][1]
    for ky in range(3):
        for kx in range(3):
            t = 3 * ky + kx
            wq[ky, kx * 256 : kx * 256 + HALF] = w_ref[:, t * CHANS : (t + 1) * CHANS]
            wq[ky, kx * 256 + HALF : (kx + 1) * 256] = jnp.zeros((256 - HALF, CHANS), BF)
    for edge in (0, PAD + ROWS):
        sbuf[edge : edge + PAD] = jnp.zeros((PAD, width, 768), BF)
    step = 512 // width

    def one(i, carry):
        r0 = i * step
        acc = None
        for ky in range(3):
            left = sbuf[pl.ds(PAD + r0 - (ky - 1) * d, step)].reshape(step * width, 768)
            term = dot(left, wq[ky], NN)
            acc = term if acc is None else acc + term
        q_ref[0, pl.ds(r0, step)] = acc[:, HALF:].reshape(step, width, HALF).astype(BF)
        q_ref[1, pl.ds(r0, step)] = acc[:, :HALF].reshape(step, width, HALF).astype(BF)
        return carry

    lax.fori_loop(0, ROWS // step, one, 0)


def weight_phase(block, dims, idx_ref, sown, nk, w_ref, gain, wg_ref):
    own_chans, share, lines = dims
    d = DIL[block]
    count = (HALF // own_chans) * lines
    bits = lines.bit_length() - 1
    line = lax.broadcasted_iota(jnp.int32, (count, HALF), 0)
    place = jnp.bitwise_and(line, lines - 1)
    want = jnp.right_shift(line, bits) * own_chans + share * idx_ref[1] + place
    pick = (lax.broadcasted_iota(jnp.int32, (count, HALF), 1) == want) & (place < share)
    pick = jnp.where(pick, 1.0, 0.0).astype(BF)
    left = dot(pick, sown[...].reshape(ROWS * OWN, HALF), NT).astype(BF)
    total = jnp.zeros((1, CHANS), F32)
    first = None
    for ky in range(3):
        lanes = slice(ky * 3 * CHANS, (ky + 1) * 3 * CHANS)
        start = PAD + (ky - 1) * d
        right = nk[start : start + ROWS].reshape(ROWS * OWN, 3 * CHANS)
        grads = dot(left, right, NN)
        wg_ref[:, lanes] = grads.astype(BF)
        part = jnp.sum(grads * dot(pick, w_ref[:, lanes], NN), axis=0, keepdims=True)
        for kx in range(3):
            total = total + part[:, kx * CHANS : (kx + 1) * CHANS]
        if ky == 0:
            first = grads[:, :CHANS]
    spot = jnp.bitwise_and(lax.broadcasted_iota(jnp.int32, (count, CHANS), 0), lines - 1)
    wg_ref[:, :CHANS] = jnp.where(spot == share, total / gain, first).astype(BF)


def turn_kernel(dims, idx_ref, xo_ref, xt_ref, cot_ref, w_ref, q_ref, wg_ref, gain_ref,
                nbuf, nk, pre, sbuf, sown, wq):
    gain = read_gain(w_ref)
    gain_ref[...] = gain
    norm_phase(3, xo_ref, xt_ref, gain, nbuf, nk)
    conv_phase(3, nbuf, w_ref, pre)
    n = R_TURN

    def some(r):
        act = flat(pre[pl.ds(r, n)])
        s = flat(cot_ref[pl.ds(r, n)]).astype(F32) * gelu_slope(act, gelu_inner(act))
        scatter_s(3, s, r, n, sbuf, sown)

    row_loop(some, n)
    q_phase(3, sbuf, w_ref, wq, q_ref)
    weight_phase(3, dims, idx_ref, sown, nk, w_ref, gain, wg_ref)


def backward_kernel(block, dims, image, first_g, idx_ref, qm_ref, qr_ref, xo_ref, xt_ref, g_ref,
                    gain_up_ref, d_ref, w_far, nk_far, gain_ref, *rest):
    if block:
        q_ref, gn_ref, wg_ref, w_ref, nk_ref, sem, sown, sbuf, wq = rest
    else:
        wg_ref, w_ref, nk_ref, sem, sown = rest
        q_ref = gn_ref = sbuf = wq = None
    weights_in = pltpu.make_async_copy(w_far, w_ref, sem.at[0])
    kept_in = pltpu.make_async_copy(nk_far, nk_ref, sem.at[1])
    weights_in.start()
    kept_in.start()
    first, width = S_WIN[block]
    at = first - X_WIN[block + 1][0]
    cut = first - first_g
    live = in_image(idx_ref[0], first, width, image)
    gain_up = gain_up_ref[...]
    n = R_BACK

    def some(r):
        rows = pl.ds(r, n)
        unit, rstd = unit_of(
            widen(flat(xo_ref[rows, at : at + width]), flat(xt_ref[rows, at : at + width]))
        )
        p = gain_up * jnp.concatenate(
            [
                flat(qm_ref[1, rows]).astype(F32) + flat(qr_ref[0, rows]).astype(F32),
                flat(qm_ref[0, rows]).astype(F32) + flat(qr_ref[1, rows]).astype(F32),
            ],
            axis=1,
        )
        change = p[:, :HALF] - chan_mean(p) - unit[:, :HALF] * chan_mean(p * unit)
        g = flat(g_ref[rows, cut : cut + width]).astype(F32) + rstd * change
        g = jnp.where(live, g.reshape(n, width, HALF), 0.0).astype(BF)
        if gn_ref is not None:
            gn_ref[rows] = g
        s = flat(g.astype(F32) * d_ref[rows])
        scatter_s(block, s, r, n, sbuf, sown)

    row_loop(some, n)
    weights_in.wait()
    if block:
        q_phase(block, sbuf, w_ref, wq, q_ref)
    kept_in.wait()
    weight_phase(block, dims, idx_ref, sown, nk_ref, w_ref, gain_ref[...], wg_ref)


def finish_kernel(dims, slabs, all_ref, perm_ref, out_ref):
    own_chans, share, lines = dims
    bits = lines.bit_length() - 1
    col = lax.broadcasted_iota(jnp.int32, (own_chans, slabs * lines), 1)
    place = jnp.bitwise_and(col, lines - 1)
    row = jnp.right_shift(col, bits) * share + place
    pick = (lax.broadcasted_iota(jnp.int32, (own_chans, slabs * lines), 0) == row) & (place < share)
    pick = jnp.where(pick, 1.0, 0.0).astype(BF)
    for t in range(TAPS):
        grads = dot(pick, all_ref[:, t * CHANS : (t + 1) * CHANS], NN).astype(BF)
        out_ref[t] = dot(grads, perm_ref[...], NT)


def local(sizes, x_in, cot, w1, gain):
    nx, nz, ny, ns = sizes
    own_chans, rows = x_in.shape[1], x_in.shape[2]
    image = x_in.shape[3]
    shards = nx * nz
    share = own_chans // ny
    lines = 8
    while lines < share + 1:
        lines *= 2
    dims = (own_chans, share, lines)
    sec, ax, az = lax.axis_index("section"), lax.axis_index("x"), lax.axis_index("zh")
    core, slab = lax.axis_index("core"), lax.axis_index("slab")
    patch = ax * nz + az
    idx = jnp.stack([patch * OWN, slab, ax, sec]).astype(jnp.int32)

    def other(value):
        return lax.ppermute(value, "core", [(0, 1), (1, 0)])

    order = np.arange(CHANS).reshape(shards, 2, own_chans)
    orders = [np.concatenate([order[:, h].ravel(), order[:, 1 - h].ravel()]) for h in (0, 1)]
    perms = np.stack([np.eye(CHANS, dtype=np.float32)[:, o] for o in orders])
    perm = lax.dynamic_index_in_dim(jnp.asarray(perms, BF), core, 0, keepdims=False)

    windows = call(
        window_kernel, shape((shards, rows, own_chans, XWIN + CWIN), BF), [], (idx, x_in, cot), (0,)
    )
    recv = lax.all_to_all(windows, ("x", "zh"), 0, 0, tiled=True)

    packed = call(prep_kernel, shape((own_chans, CARRY), BF), [], (w1[0], gain, perm))
    wide = jnp.broadcast_to(packed[None], (ns * nz, own_chans, CARRY))
    wide, recv = lax.optimization_barrier((wide, recv))
    wide = lax.all_to_all(wide, ("section", "zh"), 0, 0, tiled=True)
    wide = wide.reshape(ns, nz * own_chans, CARRY)


    def from_chips(value, axis, size):
        moves = [[(i, (i - j) % size) for i in range(size)] for j in range(1, size)]
        return [value] + [lax.ppermute(value, axis, move) for move in moves]

    weights = [
        from_chips(wide[b], "x", nx) if b < 1 else [lax.all_gather(wide[b], "x", axis=0, tiled=True)]
        for b in range(ns)
    ]

    every_row = lax.all_gather(recv, "slab", axis=0)
    x_own, cot_own = call(
        functools.partial(assemble_kernel, ny, rows),
        (shape((ROWS, XWIN, HALF), BF), shape((ROWS, CWIN, HALF), BF)),
        [],
        (every_row,),
    )

    taps3 = 3 * CHANS
    nk_shape = (ROWS + 2 * PAD, OWN, taps3)
    gain_shape = shape((1, CHANS), F32)
    halves, slopes, shifted, gains = [(x_own, other(x_own))], [], [], []
    for b in range(ns - 1):
        width = X_WIN[b + 1][1]
        pieces = len(weights[b])
        many = pieces > 1
        whole_shape = shape((HALF, CARRY), BF)
        y, slope, gain_b, nk, *whole = call(
            functools.partial(forward_kernel, b, image, pieces, 2),
            (
                shape((ROWS, width, HALF), BF),
                shape((ROWS, S_WIN[b][1], HALF), F32),
                gain_shape,
                shape(nk_shape, BF),
            )
            + (whole_shape,) * many,
            [
                pltpu.VMEM(nk_shape, BF),
                pltpu.VMEM((ROWS + 2 * PAD, width, taps3), BF),
                pltpu.VMEM((ROWS, width, HALF), F32),
                pltpu.SemaphoreType.DMA((2,)),
            ]
            + [pltpu.VMEM((HALF, CARRY), BF)] * many,
            (idx, *halves[b], *weights[b]),
            (0,),
            (),
            (3, 4),
            30,
        )
        halves.append((y, other(y)))
        slopes.append(slope)
        shifted.append(nk)
        gains.append(gain_b)
        weights[b] = whole[0] if whole else weights[b][0]

    def back_scratch(b):
        width = S_WIN[b - 1][1]
        return [
            pltpu.VMEM((ROWS + 2 * PAD, width, 768), BF),
            pltpu.VMEM((ROWS, OWN, HALF), BF),
            pltpu.VMEM((3, 768, CHANS), BF),
        ]

    count = shards * lines
    wg_shape = shape((count, TAPS * CHANS), BF)
    width = X_WIN[4][1]
    sbuf_s, sown_s, wq_s = back_scratch(3)
    q, grads, gain_b = call(
        functools.partial(turn_kernel, dims),
        (shape((2, ROWS, S_WIN[2][1], HALF), BF), wg_shape, gain_shape),
        [
            pltpu.VMEM((ROWS + 2 * PAD, width, taps3), BF),
            pltpu.VMEM(nk_shape, BF),
            pltpu.VMEM((ROWS, width, HALF), F32),
            sbuf_s,
            sown_s,
            wq_s,
        ],
        (idx, *halves[3], cot_own, weights[3][0]),
        (0,),
        micros=12,
    )
    gains.append(gain_b)

    def reduced(b, value):
        if b > 1:
            return lax.psum_scatter(value, "x", scatter_dimension=0, tiled=True)
        value = value.reshape(nx, nz * lines, LANES)
        value = lax.all_to_all(value, "x", 0, 0, tiled=True)
        return jnp.sum(value.astype(F32), axis=0).astype(BF)

    weight_parts = [None] * 3 + [reduced(3, grads)]
    g, first_g = cot_own, S_WIN[3][0]
    for b in (2, 1, 0):
        args = (
            idx, q, other(q), *halves[b + 1], g, gains[b + 1], slopes[b], weights[b], shifted[b], gains[b],
        )
        kernel = functools.partial(backward_kernel, b, dims, image, first_g)
        fetched = [
            pltpu.VMEM((HALF, CARRY), BF),
            pltpu.VMEM(nk_shape, BF),
            pltpu.SemaphoreType.DMA((2,)),
        ]
        if b:
            sbuf_s, sown_s, wq_s = back_scratch(b)
            q, g, grads = call(
                kernel,
                (
                    shape((2, ROWS, S_WIN[b - 1][1], HALF), BF),
                    shape((ROWS, S_WIN[b][1], HALF), BF),
                    wg_shape,
                ),
                fetched + [sown_s, sbuf_s, wq_s],
                args,
                (0,),
                (8, 9),
                micros=8,
            )
        else:
            own_s = pltpu.VMEM((ROWS, OWN, HALF), BF)
            (grads,) = call(kernel, (wg_shape,), fetched + [own_s], args, (0,), (8, 9))
        first_g = S_WIN[b][0]
        weight_parts[b] = reduced(b, grads)

    parts = jnp.stack(weight_parts).reshape(ns * nz, lines, LANES)
    parts = lax.all_to_all(parts, ("section", "zh"), 0, 0, tiled=True)
    total = jnp.sum(parts.astype(F32), axis=0).astype(BF)
    every = lax.all_gather(total, "slab", axis=0, tiled=True)
    weight_grad = call(
        functools.partial(finish_kernel, dims, ny),
        shape((TAPS, own_chans, CHANS), F32),
        [],
        (every, perm),
    )
    gain_rows = every.reshape(ny, lines, LANES)[:, share, :CHANS]
    gain_all = jnp.sum(gain_rows.astype(F32), axis=0)
    here = lax.dynamic_slice_in_dim(gain_all, patch * own_chans, own_chans)
    there = lax.dynamic_slice_in_dim(gain_all, HALF + patch * own_chans, own_chans)
    gain_grad = here + other(there)
    return weight_grad[None], gain_grad[None]


def solution(mesh):
    ns, chans, ny = mesh.shape["section"], mesh.shape["ch"], mesh.shape["slab"]
    nz = 2 if chans % 4 == 0 else 1
    nx = chans // (2 * nz)
    axes = ("section", "x", "zh", "core", "slab")
    fine = Mesh(mesh.devices.reshape(ns, nx, nz, 2, ny), axes)
    ch = ("x", "zh", "core")
    return jax.shard_map(
        functools.partial(local, (nx, nz, ny, ns)),
        mesh=fine,
        in_specs=(
            P(None, ch, "slab", None),
            P(None, ch, "slab", None),
            P("section", None, ch, None),
            P("section", None),
        ),
        out_specs=(P("section", None, ch, None), P("section", ch)),
        check_vma=False,
    )
```

```python
import functools

import jax
import jax.numpy as jnp
import numpy as np
from jax import lax
from jax.experimental import pallas as pl
from jax.experimental.pallas import tpu as pltpu
from jax.sharding import Mesh, PartitionSpec as P

NORM_EPS = 1e-05
SLOPE_SCALE = 0.7978845608028654
CUBIC_COEF = 0.044715
BF = jnp.bfloat16
F32 = jnp.float32

ROWS = 32
CHANS = 384
HALF = 192
TAPS = 9
DIL = (1, 2, 4, 8)
OWN = 16
XWIN = 80
CWIN = 48
PAD = 8
X_WIN = ((0, 80), (0, 80), (0, 80), (8, 64), (16, 48))
S_WIN = ((32, 16), (24, 32), (24, 32), (16, 48))
VMEM_LIMIT = 56 * 1024 * 1024
PARAMS = pltpu.CompilerParams(vmem_limit_bytes=VMEM_LIMIT)
NT = (((1,), (1,)), ((), ()))
NN = (((1,), (0,)), ((), ()))
LANES = TAPS * CHANS
CARRY = LANES + 128
R_NORM, R_EPI, R_TURN, R_BACK = 4, 2, 2, 8


def dot(a, b, dims):
    return lax.dot_general(a, b, dims, preferred_element_type=F32)


def call(kernel, out_shape, scratch, args, smem=(), far=(), far_out=(), micros=2):
    vm = pl.BlockSpec(memory_space=pltpu.VMEM)
    sm = pl.BlockSpec(memory_space=pltpu.SMEM)
    hb = pl.BlockSpec(memory_space=pltpu.HBM)
    if isinstance(out_shape, tuple):
        out_specs = tuple(hb if i in far_out else vm for i in range(len(out_shape)))
    else:
        out_specs = vm
    return pl.pallas_call(
        kernel,
        out_shape=out_shape,
        in_specs=[sm if i in smem else hb if i in far else vm for i in range(len(args))],
        out_specs=out_specs,
        scratch_shapes=scratch,
        compiler_params=PARAMS,
        cost_estimate=pl.CostEstimate(flops=micros * 10**9, bytes_accessed=micros * 10**6, transcendentals=0),
    )(*args)


def shape(dims, dtype):
    return jax.ShapeDtypeStruct(dims, dtype)


def row_loop(body, rows, unroll=1):
    span = rows * unroll

    def step(i, carry):
        for k in range(unroll):
            body(pl.multiple_of(i * span, span) + k * rows)
        return carry

    lax.fori_loop(0, ROWS // span, step, 0)


def flat(value):
    return value.reshape(value.shape[0] * value.shape[1], value.shape[2])


def in_image(base, first, count, width):
    cols = lax.broadcasted_iota(jnp.int32, (1, count, HALF), 1) + (base - 32 + first)
    return (cols >= 0) & (cols < width)


def widen(own, oth):
    return jnp.concatenate([own.astype(F32), oth.astype(F32)], axis=1)


def chan_mean(value):
    folded = value[:, :128] + value[:, 128:256] + value[:, 256:]
    return jnp.sum(folded, axis=1, keepdims=True) / CHANS


def unit_of(value):
    mean = chan_mean(value)
    rstd = lax.rsqrt(chan_mean(value * value) - mean * mean + NORM_EPS)
    return (value - mean) * rstd, rstd


def read_gain(w_ref):
    tile = w_ref[0:16, LANES:CARRY].astype(F32)
    return jnp.concatenate(
        [(tile[p : p + 1] + tile[3 + p : 4 + p]) + tile[6 + p : 7 + p] for p in range(3)], axis=1
    )


def gelu_inner(pre):
    return jnp.tanh(SLOPE_SCALE * (pre + CUBIC_COEF * pre * pre * pre))


def gelu_slope(pre, tangent):
    return 0.5 * (1.0 + tangent) + 0.5 * pre * (1.0 - tangent * tangent) * SLOPE_SCALE * (
        1.0 + 3.0 * CUBIC_COEF * pre * pre
    )


def prep_kernel(w_ref, gain_ref, perm_ref, out_ref):
    for t in range(TAPS):
        out_ref[:, t * CHANS : (t + 1) * CHANS] = dot(w_ref[t], perm_ref[...], NN).astype(BF)
    rest = jnp.broadcast_to(gain_ref[...], (8, CHANS))
    row = lax.broadcasted_iota(jnp.int32, (out_ref.shape[0], 128), 0)
    tile = jnp.zeros((out_ref.shape[0], 128), F32)
    for k in range(3):
        piece = rest.astype(BF)
        rest = rest - piece.astype(F32)
        moved = dot(piece, perm_ref[...], NN)
        for p in range(3):
            tile = jnp.where(row == 3 * k + p, moved[0:1, 128 * p : 128 * p + 128], tile)
    out_ref[:, LANES:CARRY] = tile.astype(BF)


def window_kernel(idx_ref, x_ref, cot_ref, out_ref):
    shards, rows, chans, lanes = out_ref.shape
    image = x_ref.shape[3]
    x = x_ref[idx_ref[3]].astype(F32)
    cot = cot_ref[idx_ref[3]].astype(F32)
    lane = lax.broadcasted_iota(jnp.int32, (chans, lanes), 1)
    room = jnp.zeros((chans, lanes - image), F32)
    for r in range(rows):
        from_x, from_cot = x[:, r, :], cot[:, r, :]
        if image < lanes:
            from_x = jnp.concatenate([from_x, room], axis=1)
            from_cot = jnp.concatenate([from_cot, room], axis=1)
        for p in range(shards):
            here = None
            for value, start in ((from_x, OWN * p - 32), (from_cot, OWN * p - 16 - XWIN)):
                shift = (-start) % lanes
                moved = pltpu.roll(value, shift, 1) if shift else value
                moved = jnp.where((lane + start >= 0) & (lane + start < image), moved, 0.0)
                here = moved if here is None else jnp.where(lane < XWIN, here, moved)
            out_ref[p, r] = here.astype(BF)


def assemble_kernel(slabs, rows, recv_ref, x_ref, cot_ref):
    lanes = XWIN + CWIN
    eye = (
        lax.broadcasted_iota(jnp.int32, (lanes, lanes), 0)
        == lax.broadcasted_iota(jnp.int32, (lanes, lanes), 1)
    ).astype(F32).astype(BF)

    def one(r, carry):
        for y in range(slabs):
            piece = recv_ref[y, :, pl.ds(r, 1)].astype(F32)
            piece = piece.reshape(HALF, lanes).astype(BF)
            flipped = dot(eye, piece, NT).astype(BF)
            x_ref[pl.ds(y * rows + r, 1)] = flipped[:XWIN].reshape(1, XWIN, HALF)
            cot_ref[pl.ds(y * rows + r, 1)] = flipped[XWIN:].reshape(1, CWIN, HALF)
        return carry

    lax.fori_loop(0, rows, one, 0)


def norm_phase(block, xo_ref, xt_ref, gain, nbuf, nk):
    d = DIL[block]
    first_in, width_in = X_WIN[block]
    first_out, width_out = X_WIN[block + 1]
    low = first_out - first_in
    own = 32 - first_in
    for edge in (0, PAD + ROWS):
        nbuf[edge : edge + PAD] = jnp.zeros((PAD, width_out, 3 * CHANS), BF)
        nk[edge : edge + PAD] = jnp.zeros((PAD, OWN, 3 * CHANS), BF)
    n = R_NORM

    def some(r):
        unit, _ = unit_of(widen(flat(xo_ref[pl.ds(r, n)]), flat(xt_ref[pl.ds(r, n)])))
        both = unit * gain
        for kx in range(3):
            shift = (-(kx - 1) * d) % (n * width_in)
            moved = pltpu.roll(both, shift, 0) if shift else both
            moved = moved.reshape(n, width_in, CHANS)
            lanes = slice(kx * CHANS, (kx + 1) * CHANS)
            nbuf[pl.ds(PAD + r, n), :, lanes] = moved[:, low : low + width_out].astype(BF)
            nk[pl.ds(PAD + r, n), :, lanes] = moved[:, own : own + OWN].astype(BF)

    row_loop(some, n)


def conv_phase(block, nbuf, w_ref, pre):
    d = DIL[block]
    width = X_WIN[block + 1][1]
    step = 8

    def one(i, carry):
        r0 = i * step
        acc = None
        for ky in range(3):
            left = nbuf[pl.ds(PAD + r0 + (ky - 1) * d, step)].reshape(step * width, 3 * CHANS)
            term = dot(left, w_ref[:, ky * 3 * CHANS : (ky + 1) * 3 * CHANS], NT)
            acc = term if acc is None else acc + term
        pre[pl.ds(r0, step)] = acc.reshape(step, width, HALF)
        return carry

    lax.fori_loop(0, ROWS // step, one, 0)


def forward_kernel(block, image, pieces, spin, idx_ref, xo_ref, xt_ref, *rest):
    w_refs, rest = rest[:pieces], rest[pieces:]
    y_ref, d_ref, gain_ref, nk_far, *rest = rest
    w_ref = w_refs[0]
    whole = None
    if pieces > 1:
        whole_far, nk, nbuf, pre, sem, w_ref = rest
        lines = HALF // pieces
        for j in range(pieces):
            place = lax.rem(idx_ref[spin] + j, pieces) * lines
            w_ref[pl.ds(pl.multiple_of(place, lines), lines)] = w_refs[j][...]
        whole = pltpu.make_async_copy(w_ref, whole_far, sem.at[1])
        whole.start()
    else:
        nk, nbuf, pre, sem = rest
    first_in = X_WIN[block][0]
    first_out, width_out = X_WIN[block + 1]
    first_s, width_s = S_WIN[block]
    gain = read_gain(w_ref)
    gain_ref[...] = gain
    norm_phase(block, xo_ref, xt_ref, gain, nbuf, nk)
    kept = pltpu.make_async_copy(nk, nk_far, sem.at[0])
    kept.start()
    conv_phase(block, nbuf, w_ref, pre)
    live = in_image(idx_ref[0], first_out, width_out, image)
    low, at = first_out - first_in, first_s - first_out
    n = R_EPI

    def some(r):
        act = pre[pl.ds(r, n)]
        tangent = gelu_inner(act)
        out = xo_ref[pl.ds(r, n)].astype(F32)[:, low : low + width_out] + 0.5 * act * (1.0 + tangent)
        y_ref[pl.ds(r, n)] = jnp.where(live, out, 0.0).astype(BF)
        d_ref[pl.ds(r, n)] = gelu_slope(act[:, at : at + width_s], tangent[:, at : at + width_s])

    row_loop(some, n)
    kept.wait()
    if whole is not None:
        whole.wait()


def scatter_s(block, s, r, n, sbuf, sown):
    first, width = S_WIN[block]
    rows = s.reshape(n, width, HALF)
    sown[pl.ds(r, n)] = rows[:, 32 - first : 32 - first + OWN].astype(BF)
    if sbuf is None:
        return
    d = DIL[block]
    first_q, width_q = S_WIN[block - 1]
    low = first_q - first
    gap = jnp.zeros((n * width, 256 - HALF), F32)
    wide = jnp.concatenate([s, gap], axis=1)
    for kx in range(3):
        shift = ((kx - 1) * d) % (n * width)
        moved = pltpu.roll(wide, shift, 0) if shift else wide
        moved = moved.reshape(n, width, 256)[:, low : low + width_q]
        sbuf[pl.ds(PAD + r, n), :, kx * 256 : (kx + 1) * 256] = moved.astype(BF)


def q_phase(block, sbuf, w_ref, wq, q_ref):
    d = DIL[block]
    width = S_WIN[block - 1][1]
    for ky in range(3):
        for kx in range(3):
            t = 3 * ky + kx
            wq[ky, kx * 256 : kx * 256 + HALF] = w_ref[:, t * CHANS : (t + 1) * CHANS]
            wq[ky, kx * 256 + HALF : (kx + 1) * 256] = jnp.zeros((256 - HALF, CHANS), BF)
    for edge in (0, PAD + ROWS):
        sbuf[edge : edge + PAD] = jnp.zeros((PAD, width, 768), BF)
    step = 512 // width

    def one(i, carry):
        r0 = i * step
        acc = None
        for ky in range(3):
            left = sbuf[pl.ds(PAD + r0 - (ky - 1) * d, step)].reshape(step * width, 768)
            term = dot(left, wq[ky], NN)
            acc = term if acc is None else acc + term
        q_ref[0, pl.ds(r0, step)] = acc[:, HALF:].reshape(step, width, HALF).astype(BF)
        q_ref[1, pl.ds(r0, step)] = acc[:, :HALF].reshape(step, width, HALF).astype(BF)
        return carry

    lax.fori_loop(0, ROWS // step, one, 0)


def weight_phase(block, dims, idx_ref, sown, nk, w_ref, gain, wg_ref):
    own_chans, share, lines = dims
    d = DIL[block]
    count = (HALF // own_chans) * lines
    bits = lines.bit_length() - 1
    line = lax.broadcasted_iota(jnp.int32, (count, HALF), 0)
    place = jnp.bitwise_and(line, lines - 1)
    want = jnp.right_shift(line, bits) * own_chans + share * idx_ref[1] + place
    pick = (lax.broadcasted_iota(jnp.int32, (count, HALF), 1) == want) & (place < share)
    pick = jnp.where(pick, 1.0, 0.0).astype(BF)
    left = dot(pick, sown[...].reshape(ROWS * OWN, HALF), NT).astype(BF)
    total = jnp.zeros((1, CHANS), F32)
    first = None
    for ky in range(3):
        lanes = slice(ky * 3 * CHANS, (ky + 1) * 3 * CHANS)
        start = PAD + (ky - 1) * d
        right = nk[start : start + ROWS].reshape(ROWS * OWN, 3 * CHANS)
        grads = dot(left, right, NN)
        wg_ref[:, lanes] = grads.astype(BF)
        part = jnp.sum(grads * dot(pick, w_ref[:, lanes], NN), axis=0, keepdims=True)
        for kx in range(3):
            total = total + part[:, kx * CHANS : (kx + 1) * CHANS]
        if ky == 0:
            first = grads[:, :CHANS]
    spot = jnp.bitwise_and(lax.broadcasted_iota(jnp.int32, (count, CHANS), 0), lines - 1)
    wg_ref[:, :CHANS] = jnp.where(spot == share, total / gain, first).astype(BF)


def turn_kernel(dims, idx_ref, xo_ref, xt_ref, cot_ref, w_ref, q_ref, wg_ref, gain_ref,
                nbuf, nk, pre, sbuf, sown, wq):
    gain = read_gain(w_ref)
    gain_ref[...] = gain
    norm_phase(3, xo_ref, xt_ref, gain, nbuf, nk)
    conv_phase(3, nbuf, w_ref, pre)
    n = R_TURN

    def some(r):
        act = flat(pre[pl.ds(r, n)])
        s = flat(cot_ref[pl.ds(r, n)]).astype(F32) * gelu_slope(act, gelu_inner(act))
        scatter_s(3, s, r, n, sbuf, sown)

    row_loop(some, n)
    q_phase(3, sbuf, w_ref, wq, q_ref)
    weight_phase(3, dims, idx_ref, sown, nk, w_ref, gain, wg_ref)


def backward_kernel(block, dims, image, first_g, idx_ref, qm_ref, qr_ref, xo_ref, xt_ref, g_ref,
                    gain_up_ref, d_ref, w_far, nk_far, gain_ref, *rest):
    if block:
        q_ref, gn_ref, wg_ref, w_ref, nk_ref, sem, sown, sbuf, wq = rest
    else:
        wg_ref, w_ref, nk_ref, sem, sown = rest
        q_ref = gn_ref = sbuf = wq = None
    weights_in = pltpu.make_async_copy(w_far, w_ref, sem.at[0])
    kept_in = pltpu.make_async_copy(nk_far, nk_ref, sem.at[1])
    weights_in.start()
    kept_in.start()
    first, width = S_WIN[block]
    at = first - X_WIN[block + 1][0]
    cut = first - first_g
    live = in_image(idx_ref[0], first, width, image)
    gain_up = gain_up_ref[...]
    n = R_BACK

    def some(r):
        rows = pl.ds(r, n)
        unit, rstd = unit_of(
            widen(flat(xo_ref[rows, at : at + width]), flat(xt_ref[rows, at : at + width]))
        )
        p = gain_up * jnp.concatenate(
            [
                flat(qm_ref[1, rows]).astype(F32) + flat(qr_ref[0, rows]).astype(F32),
                flat(qm_ref[0, rows]).astype(F32) + flat(qr_ref[1, rows]).astype(F32),
            ],
            axis=1,
        )
        change = p[:, :HALF] - chan_mean(p) - unit[:, :HALF] * chan_mean(p * unit)
        g = flat(g_ref[rows, cut : cut + width]).astype(F32) + rstd * change
        g = jnp.where(live, g.reshape(n, width, HALF), 0.0).astype(BF)
        if gn_ref is not None:
            gn_ref[rows] = g
        s = flat(g.astype(F32) * d_ref[rows])
        scatter_s(block, s, r, n, sbuf, sown)

    row_loop(some, n)
    weights_in.wait()
    if block:
        q_phase(block, sbuf, w_ref, wq, q_ref)
    kept_in.wait()
    weight_phase(block, dims, idx_ref, sown, nk_ref, w_ref, gain_ref[...], wg_ref)


def finish_kernel(dims, slabs, all_ref, perm_ref, out_ref):
    own_chans, share, lines = dims
    bits = lines.bit_length() - 1
    col = lax.broadcasted_iota(jnp.int32, (own_chans, slabs * lines), 1)
    place = jnp.bitwise_and(col, lines - 1)
    row = jnp.right_shift(col, bits) * share + place
    pick = (lax.broadcasted_iota(jnp.int32, (own_chans, slabs * lines), 0) == row) & (place < share)
    pick = jnp.where(pick, 1.0, 0.0).astype(BF)
    for t in range(TAPS):
        grads = dot(pick, all_ref[:, t * CHANS : (t + 1) * CHANS], NN).astype(BF)
        out_ref[t] = dot(grads, perm_ref[...], NT)


def local(sizes, x_in, cot, w1, gain):
    nx, nz, ny, ns = sizes
    own_chans, rows = x_in.shape[1], x_in.shape[2]
    image = x_in.shape[3]
    shards = nx * nz
    share = own_chans // ny
    lines = 8
    while lines < share + 1:
        lines *= 2
    dims = (own_chans, share, lines)
    sec, ax, az = lax.axis_index("section"), lax.axis_index("x"), lax.axis_index("zh")
    core, slab = lax.axis_index("core"), lax.axis_index("slab")
    patch = ax * nz + az
    idx = jnp.stack([patch * OWN, slab, ax, sec]).astype(jnp.int32)

    def other(value):
        return lax.ppermute(value, "core", [(0, 1), (1, 0)])

    order = np.arange(CHANS).reshape(shards, 2, own_chans)
    orders = [np.concatenate([order[:, h].ravel(), order[:, 1 - h].ravel()]) for h in (0, 1)]
    perms = np.stack([np.eye(CHANS, dtype=np.float32)[:, o] for o in orders])
    perm = lax.dynamic_index_in_dim(jnp.asarray(perms, BF), core, 0, keepdims=False)

    windows = call(
        window_kernel, shape((shards, rows, own_chans, XWIN + CWIN), BF), [], (idx, x_in, cot), (0,)
    )
    recv = lax.all_to_all(windows, ("x", "zh"), 0, 0, tiled=True)

    packed = call(prep_kernel, shape((own_chans, CARRY), BF), [], (w1[0], gain, perm))
    wide = jnp.broadcast_to(packed[None], (ns * nz, own_chans, CARRY))
    wide, recv = lax.optimization_barrier((wide, recv))
    wide = lax.all_to_all(wide, ("section", "zh"), 0, 0, tiled=True)
    wide = wide.reshape(ns, nz * own_chans, CARRY)


    def from_chips(value, axis, size):
        moves = [[(i, (i - j) % size) for i in range(size)] for j in range(1, size)]
        return [value] + [lax.ppermute(value, axis, move) for move in moves]

    first = from_chips(wide[0], "x", nx)
    pair = lax.all_gather(wide[1:3], "x", axis=1, tiled=True)
    last = lax.all_gather(wide[3], "x", axis=0, tiled=True)
    weights = [first, [pair[0]], [pair[1]], [last]]

    every_row = lax.all_gather(recv, "slab", axis=0)
    x_own, cot_own = call(
        functools.partial(assemble_kernel, ny, rows),
        (shape((ROWS, XWIN, HALF), BF), shape((ROWS, CWIN, HALF), BF)),
        [],
        (every_row,),
    )

    taps3 = 3 * CHANS
    nk_shape = (ROWS + 2 * PAD, OWN, taps3)
    gain_shape = shape((1, CHANS), F32)
    halves, slopes, shifted, gains = [(x_own, other(x_own))], [], [], []
    for b in range(ns - 1):
        width = X_WIN[b + 1][1]
        pieces = len(weights[b])
        many = pieces > 1
        whole_shape = shape((HALF, CARRY), BF)
        y, slope, gain_b, nk, *whole = call(
            functools.partial(forward_kernel, b, image, pieces, 2),
            (
                shape((ROWS, width, HALF), BF),
                shape((ROWS, S_WIN[b][1], HALF), F32),
                gain_shape,
                shape(nk_shape, BF),
            )
            + (whole_shape,) * many,
            [
                pltpu.VMEM(nk_shape, BF),
                pltpu.VMEM((ROWS + 2 * PAD, width, taps3), BF),
                pltpu.VMEM((ROWS, width, HALF), F32),
                pltpu.SemaphoreType.DMA((2,)),
            ]
            + [pltpu.VMEM((HALF, CARRY), BF)] * many,
            (idx, *halves[b], *weights[b]),
            (0,),
            (),
            (3, 4),
            30,
        )
        halves.append((y, other(y)))
        slopes.append(slope)
        shifted.append(nk)
        gains.append(gain_b)
        weights[b] = whole[0] if whole else weights[b][0]

    def back_scratch(b):
        width = S_WIN[b - 1][1]
        return [
            pltpu.VMEM((ROWS + 2 * PAD, width, 768), BF),
            pltpu.VMEM((ROWS, OWN, HALF), BF),
            pltpu.VMEM((3, 768, CHANS), BF),
        ]

    count = shards * lines
    wg_shape = shape((count, TAPS * CHANS), BF)
    width = X_WIN[4][1]
    sbuf_s, sown_s, wq_s = back_scratch(3)
    q, grads, gain_b = call(
        functools.partial(turn_kernel, dims),
        (shape((2, ROWS, S_WIN[2][1], HALF), BF), wg_shape, gain_shape),
        [
            pltpu.VMEM((ROWS + 2 * PAD, width, taps3), BF),
            pltpu.VMEM(nk_shape, BF),
            pltpu.VMEM((ROWS, width, HALF), F32),
            sbuf_s,
            sown_s,
            wq_s,
        ],
        (idx, *halves[3], cot_own, weights[3][0]),
        (0,),
        micros=12,
    )
    gains.append(gain_b)

    def reduced(*values):
        value = jnp.stack([v.reshape(nx, nz * lines, LANES) for v in values], axis=1)
        value = lax.all_to_all(value, "x", 0, 0, tiled=True)
        return jnp.sum(value.astype(F32), axis=0).astype(BF)

    weight_parts = [None] * 3 + [grads]
    g, first_g = cot_own, S_WIN[3][0]
    for b in (2, 1, 0):
        args = (
            idx, q, other(q), *halves[b + 1], g, gains[b + 1], slopes[b], weights[b], shifted[b], gains[b],
        )
        kernel = functools.partial(backward_kernel, b, dims, image, first_g)
        fetched = [
            pltpu.VMEM((HALF, CARRY), BF),
            pltpu.VMEM(nk_shape, BF),
            pltpu.SemaphoreType.DMA((2,)),
        ]
        if b:
            sbuf_s, sown_s, wq_s = back_scratch(b)
            q, g, grads = call(
                kernel,
                (
                    shape((2, ROWS, S_WIN[b - 1][1], HALF), BF),
                    shape((ROWS, S_WIN[b][1], HALF), BF),
                    wg_shape,
                ),
                fetched + [sown_s, sbuf_s, wq_s],
                args,
                (0,),
                (8, 9),
                micros=8,
            )
        else:
            own_s = pltpu.VMEM((ROWS, OWN, HALF), BF)
            (grads,) = call(kernel, (wg_shape,), fetched + [own_s], args, (0,), (8, 9))
        first_g = S_WIN[b][0]
        weight_parts[b] = grads
        if b == 2:
            late = reduced(*weight_parts[2:])

    parts = jnp.concatenate([reduced(*weight_parts[:2]), late]).reshape(ns * nz, lines, LANES)
    parts = lax.all_to_all(parts, ("section", "zh"), 0, 0, tiled=True)
    total = jnp.sum(parts.astype(F32), axis=0).astype(BF)
    every = lax.all_gather(total, "slab", axis=0, tiled=True)
    weight_grad = call(
        functools.partial(finish_kernel, dims, ny),
        shape((TAPS, own_chans, CHANS), F32),
        [],
        (every, perm),
    )
    gain_rows = every.reshape(ny, lines, LANES)[:, share, :CHANS]
    gain_all = jnp.sum(gain_rows.astype(F32), axis=0)
    here = lax.dynamic_slice_in_dim(gain_all, patch * own_chans, own_chans)
    there = lax.dynamic_slice_in_dim(gain_all, HALF + patch * own_chans, own_chans)
    gain_grad = here + other(there)
    return weight_grad[None], gain_grad[None]


def solution(mesh):
    ns, chans, ny = mesh.shape["section"], mesh.shape["ch"], mesh.shape["slab"]
    nz = 2 if chans % 4 == 0 else 1
    nx = chans // (2 * nz)
    axes = ("section", "x", "zh", "core", "slab")
    fine = Mesh(mesh.devices.reshape(ns, nx, nz, 2, ny), axes)
    ch = ("x", "zh", "core")
    return jax.shard_map(
        functools.partial(local, (nx, nz, ny, ns)),
        mesh=fine,
        in_specs=(
            P(None, ch, "slab", None),
            P(None, ch, "slab", None),
            P("section", None, ch, None),
            P("section", None),
        ),
        out_specs=(P("section", None, ch, None), P("section", ch)),
        check_vma=False,
    )
```

```python
import functools

import jax
import jax.numpy as jnp
import numpy as np
from jax import lax
from jax.experimental import pallas as pl
from jax.experimental.pallas import tpu as pltpu
from jax.sharding import Mesh, PartitionSpec as P

NORM_EPS = 1e-05
SLOPE_SCALE = 0.7978845608028654
CUBIC_COEF = 0.044715
BF = jnp.bfloat16
F32 = jnp.float32

ROWS = 32
CHANS = 384
HALF = 192
TAPS = 9
DIL = (1, 2, 4, 8)
OWN = 16
XWIN = 80
CWIN = 48
PAD = 8
X_WIN = ((0, 80), (0, 80), (0, 80), (8, 64), (16, 48))
S_WIN = ((32, 16), (24, 32), (24, 32), (16, 48))
VMEM_LIMIT = 56 * 1024 * 1024
PARAMS = pltpu.CompilerParams(vmem_limit_bytes=VMEM_LIMIT)
NT = (((1,), (1,)), ((), ()))
NN = (((1,), (0,)), ((), ()))
LANES = TAPS * CHANS
CARRY = LANES + 128
R_NORM, R_EPI, R_TURN, R_BACK = 4, 2, 2, 8


def dot(a, b, dims):
    return lax.dot_general(a, b, dims, preferred_element_type=F32)


def call(kernel, out_shape, scratch, args, smem=(), far=(), far_out=(), micros=2):
    vm = pl.BlockSpec(memory_space=pltpu.VMEM)
    sm = pl.BlockSpec(memory_space=pltpu.SMEM)
    hb = pl.BlockSpec(memory_space=pltpu.HBM)
    if isinstance(out_shape, tuple):
        out_specs = tuple(hb if i in far_out else vm for i in range(len(out_shape)))
    else:
        out_specs = vm
    return pl.pallas_call(
        kernel,
        out_shape=out_shape,
        in_specs=[sm if i in smem else hb if i in far else vm for i in range(len(args))],
        out_specs=out_specs,
        scratch_shapes=scratch,
        compiler_params=PARAMS,
        cost_estimate=pl.CostEstimate(flops=micros * 10**9, bytes_accessed=micros * 10**6, transcendentals=0),
    )(*args)


def shape(dims, dtype):
    return jax.ShapeDtypeStruct(dims, dtype)


def row_loop(body, rows, unroll=1):
    span = rows * unroll

    def step(i, carry):
        for k in range(unroll):
            body(pl.multiple_of(i * span, span) + k * rows)
        return carry

    lax.fori_loop(0, ROWS // span, step, 0)


def flat(value):
    return value.reshape(value.shape[0] * value.shape[1], value.shape[2])


def in_image(base, first, count, width):
    cols = lax.broadcasted_iota(jnp.int32, (1, count, HALF), 1) + (base - 32 + first)
    return (cols >= 0) & (cols < width)


def widen(own, oth):
    return jnp.concatenate([own.astype(F32), oth.astype(F32)], axis=1)


def chan_mean(value):
    folded = value[:, :128] + value[:, 128:256] + value[:, 256:]
    return jnp.sum(folded, axis=1, keepdims=True) / CHANS


def unit_of(value):
    mean = chan_mean(value)
    rstd = lax.rsqrt(chan_mean(value * value) - mean * mean + NORM_EPS)
    return (value - mean) * rstd, rstd


def read_gain(w_ref):
    tile = w_ref[0:16, LANES:CARRY].astype(F32)
    return jnp.concatenate(
        [(tile[p : p + 1] + tile[3 + p : 4 + p]) + tile[6 + p : 7 + p] for p in range(3)], axis=1
    )


def gelu_inner(pre):
    return jnp.tanh(SLOPE_SCALE * (pre + CUBIC_COEF * pre * pre * pre))


def gelu_slope(pre, tangent):
    return 0.5 * (1.0 + tangent) + 0.5 * pre * (1.0 - tangent * tangent) * SLOPE_SCALE * (
        1.0 + 3.0 * CUBIC_COEF * pre * pre
    )


def prep_kernel(w_ref, gain_ref, perm_ref, out_ref):
    for t in range(TAPS):
        out_ref[:, t * CHANS : (t + 1) * CHANS] = dot(w_ref[t], perm_ref[...], NN).astype(BF)
    rest = jnp.broadcast_to(gain_ref[...], (8, CHANS))
    row = lax.broadcasted_iota(jnp.int32, (out_ref.shape[0], 128), 0)
    tile = jnp.zeros((out_ref.shape[0], 128), F32)
    for k in range(3):
        piece = rest.astype(BF)
        rest = rest - piece.astype(F32)
        moved = dot(piece, perm_ref[...], NN)
        for p in range(3):
            tile = jnp.where(row == 3 * k + p, moved[0:1, 128 * p : 128 * p + 128], tile)
    out_ref[:, LANES:CARRY] = tile.astype(BF)


def window_kernel(idx_ref, x_ref, cot_ref, out_ref):
    shards, rows, chans, lanes = out_ref.shape
    image = x_ref.shape[3]
    x = x_ref[idx_ref[3]].astype(F32)
    cot = cot_ref[idx_ref[3]].astype(F32)
    lane = lax.broadcasted_iota(jnp.int32, (chans, lanes), 1)
    room = jnp.zeros((chans, lanes - image), F32)
    for r in range(rows):
        from_x, from_cot = x[:, r, :], cot[:, r, :]
        if image < lanes:
            from_x = jnp.concatenate([from_x, room], axis=1)
            from_cot = jnp.concatenate([from_cot, room], axis=1)
        for p in range(shards):
            here = None
            for value, start in ((from_x, OWN * p - 32), (from_cot, OWN * p - 16 - XWIN)):
                shift = (-start) % lanes
                moved = pltpu.roll(value, shift, 1) if shift else value
                moved = jnp.where((lane + start >= 0) & (lane + start < image), moved, 0.0)
                here = moved if here is None else jnp.where(lane < XWIN, here, moved)
            out_ref[p, r] = here.astype(BF)


def assemble_kernel(slabs, rows, idx_ref, *refs):
    pieces, (x_ref, cot_ref) = refs[:slabs], refs[slabs:]
    lanes = XWIN + CWIN
    eye = (
        lax.broadcasted_iota(jnp.int32, (lanes, lanes), 0)
        == lax.broadcasted_iota(jnp.int32, (lanes, lanes), 1)
    ).astype(F32).astype(BF)

    def one(r, carry):
        for y in range(slabs):
            piece = pieces[y][:, pl.ds(r, 1)].astype(F32)
            piece = piece.reshape(HALF, lanes).astype(BF)
            flipped = dot(eye, piece, NT).astype(BF)
            place = lax.rem(idx_ref[1] + y, slabs) * rows + r
            x_ref[pl.ds(place, 1)] = flipped[:XWIN].reshape(1, XWIN, HALF)
            cot_ref[pl.ds(place, 1)] = flipped[XWIN:].reshape(1, CWIN, HALF)
        return carry

    lax.fori_loop(0, rows, one, 0)


def norm_phase(block, xo_ref, xt_ref, gain, nbuf, nk):
    d = DIL[block]
    first_in, width_in = X_WIN[block]
    first_out, width_out = X_WIN[block + 1]
    low = first_out - first_in
    own = 32 - first_in
    for edge in (0, PAD + ROWS):
        nbuf[edge : edge + PAD] = jnp.zeros((PAD, width_out, 3 * CHANS), BF)
        nk[edge : edge + PAD] = jnp.zeros((PAD, OWN, 3 * CHANS), BF)
    n = R_NORM

    def some(r):
        unit, _ = unit_of(widen(flat(xo_ref[pl.ds(r, n)]), flat(xt_ref[pl.ds(r, n)])))
        both = unit * gain
        for kx in range(3):
            shift = (-(kx - 1) * d) % (n * width_in)
            moved = pltpu.roll(both, shift, 0) if shift else both
            moved = moved.reshape(n, width_in, CHANS)
            lanes = slice(kx * CHANS, (kx + 1) * CHANS)
            nbuf[pl.ds(PAD + r, n), :, lanes] = moved[:, low : low + width_out].astype(BF)
            nk[pl.ds(PAD + r, n), :, lanes] = moved[:, own : own + OWN].astype(BF)

    row_loop(some, n)


def conv_phase(block, nbuf, w_ref, pre):
    d = DIL[block]
    width = X_WIN[block + 1][1]
    step = 8

    def one(i, carry):
        r0 = i * step
        acc = None
        for ky in range(3):
            left = nbuf[pl.ds(PAD + r0 + (ky - 1) * d, step)].reshape(step * width, 3 * CHANS)
            term = dot(left, w_ref[:, ky * 3 * CHANS : (ky + 1) * 3 * CHANS], NT)
            acc = term if acc is None else acc + term
        pre[pl.ds(r0, step)] = acc.reshape(step, width, HALF)
        return carry

    lax.fori_loop(0, ROWS // step, one, 0)


def forward_kernel(block, image, pieces, index, idx_ref, xo_ref, xt_ref, *rest):
    w_refs, rest = rest[:pieces], rest[pieces:]
    y_ref, d_ref, gain_ref, nk_far, *rest = rest
    whole = None
    if pieces > 1:
        whole_far, nk, nbuf, pre, sem, w_ref = rest
        lines = HALF // pieces
        for j in range(pieces):
            place = lax.rem(idx_ref[2] + j, pieces) * lines
            w_ref[pl.ds(pl.multiple_of(place, lines), lines)] = w_refs[j][...]
        whole = pltpu.make_async_copy(w_ref, whole_far, sem.at[1])
        whole.start()
    else:
        nk, nbuf, pre, sem, w_ref = rest
        source = w_refs[0] if index is None else w_refs[0].at[index]
        coming = pltpu.make_async_copy(source, w_ref, sem.at[1])
        coming.start()
        coming.wait()
    first_in = X_WIN[block][0]
    first_out, width_out = X_WIN[block + 1]
    first_s, width_s = S_WIN[block]
    gain = read_gain(w_ref)
    gain_ref[...] = gain
    norm_phase(block, xo_ref, xt_ref, gain, nbuf, nk)
    kept = pltpu.make_async_copy(nk, nk_far, sem.at[0])
    kept.start()
    conv_phase(block, nbuf, w_ref, pre)
    live = in_image(idx_ref[0], first_out, width_out, image)
    low, at = first_out - first_in, first_s - first_out
    n = R_EPI

    def some(r):
        act = pre[pl.ds(r, n)]
        tangent = gelu_inner(act)
        out = xo_ref[pl.ds(r, n)].astype(F32)[:, low : low + width_out] + 0.5 * act * (1.0 + tangent)
        y_ref[pl.ds(r, n)] = jnp.where(live, out, 0.0).astype(BF)
        d_ref[pl.ds(r, n)] = gelu_slope(act[:, at : at + width_s], tangent[:, at : at + width_s])

    row_loop(some, n)
    kept.wait()
    if whole is not None:
        whole.wait()


def scatter_s(block, s, r, n, sbuf, sown):
    first, width = S_WIN[block]
    rows = s.reshape(n, width, HALF)
    sown[pl.ds(r, n)] = rows[:, 32 - first : 32 - first + OWN].astype(BF)
    if sbuf is None:
        return
    d = DIL[block]
    first_q, width_q = S_WIN[block - 1]
    low = first_q - first
    gap = jnp.zeros((n * width, 256 - HALF), F32)
    wide = jnp.concatenate([s, gap], axis=1)
    for kx in range(3):
        shift = ((kx - 1) * d) % (n * width)
        moved = pltpu.roll(wide, shift, 0) if shift else wide
        moved = moved.reshape(n, width, 256)[:, low : low + width_q]
        sbuf[pl.ds(PAD + r, n), :, kx * 256 : (kx + 1) * 256] = moved.astype(BF)


def q_phase(block, sbuf, w_ref, wq, q_ref):
    d = DIL[block]
    width = S_WIN[block - 1][1]
    for ky in range(3):
        for kx in range(3):
            t = 3 * ky + kx
            wq[ky, kx * 256 : kx * 256 + HALF] = w_ref[:, t * CHANS : (t + 1) * CHANS]
            wq[ky, kx * 256 + HALF : (kx + 1) * 256] = jnp.zeros((256 - HALF, CHANS), BF)
    for edge in (0, PAD + ROWS):
        sbuf[edge : edge + PAD] = jnp.zeros((PAD, width, 768), BF)
    step = 512 // width

    def one(i, carry):
        r0 = i * step
        acc = None
        for ky in range(3):
            left = sbuf[pl.ds(PAD + r0 - (ky - 1) * d, step)].reshape(step * width, 768)
            term = dot(left, wq[ky], NN)
            acc = term if acc is None else acc + term
        q_ref[0, pl.ds(r0, step)] = acc[:, HALF:].reshape(step, width, HALF).astype(BF)
        q_ref[1, pl.ds(r0, step)] = acc[:, :HALF].reshape(step, width, HALF).astype(BF)
        return carry

    lax.fori_loop(0, ROWS // step, one, 0)


def weight_phase(block, dims, idx_ref, sown, nk, w_ref, gain, wg_ref):
    own_chans, share, lines = dims
    d = DIL[block]
    count = (HALF // own_chans) * lines
    bits = lines.bit_length() - 1
    line = lax.broadcasted_iota(jnp.int32, (count, HALF), 0)
    place = jnp.bitwise_and(line, lines - 1)
    want = jnp.right_shift(line, bits) * own_chans + share * idx_ref[1] + place
    pick = (lax.broadcasted_iota(jnp.int32, (count, HALF), 1) == want) & (place < share)
    pick = jnp.where(pick, 1.0, 0.0).astype(BF)
    left = dot(pick, sown[...].reshape(ROWS * OWN, HALF), NT).astype(BF)
    total = jnp.zeros((1, CHANS), F32)
    first = None
    for ky in range(3):
        lanes = slice(ky * 3 * CHANS, (ky + 1) * 3 * CHANS)
        start = PAD + (ky - 1) * d
        right = nk[start : start + ROWS].reshape(ROWS * OWN, 3 * CHANS)
        grads = dot(left, right, NN)
        wg_ref[:, lanes] = grads.astype(BF)
        part = jnp.sum(grads * dot(pick, w_ref[:, lanes], NN), axis=0, keepdims=True)
        for kx in range(3):
            total = total + part[:, kx * CHANS : (kx + 1) * CHANS]
        if ky == 0:
            first = grads[:, :CHANS]
    spot = jnp.bitwise_and(lax.broadcasted_iota(jnp.int32, (count, CHANS), 0), lines - 1)
    wg_ref[:, :CHANS] = jnp.where(spot == share, total / gain, first).astype(BF)


def turn_kernel(dims, idx_ref, xo_ref, xt_ref, cot_ref, w_ref, q_ref, wg_ref, gain_ref,
                nbuf, nk, pre, sbuf, sown, wq):
    gain = read_gain(w_ref)
    gain_ref[...] = gain
    norm_phase(3, xo_ref, xt_ref, gain, nbuf, nk)
    conv_phase(3, nbuf, w_ref, pre)
    n = R_TURN

    def some(r):
        act = flat(pre[pl.ds(r, n)])
        s = flat(cot_ref[pl.ds(r, n)]).astype(F32) * gelu_slope(act, gelu_inner(act))
        scatter_s(3, s, r, n, sbuf, sown)

    row_loop(some, n)
    q_phase(3, sbuf, w_ref, wq, q_ref)
    weight_phase(3, dims, idx_ref, sown, nk, w_ref, gain, wg_ref)


def backward_kernel(block, dims, image, first_g, index, idx_ref, qm_ref, qr_ref, xo_ref, xt_ref, g_ref,
                    gain_up_ref, d_ref, w_far, nk_far, gain_ref, *rest):
    if block:
        q_ref, gn_ref, wg_ref, w_ref, nk_ref, sem, sown, sbuf, wq = rest
    else:
        wg_ref, w_ref, nk_ref, sem, sown = rest
        q_ref = gn_ref = sbuf = wq = None
    w_far = w_far if index is None else w_far.at[index]
    weights_in = pltpu.make_async_copy(w_far, w_ref, sem.at[0])
    kept_in = pltpu.make_async_copy(nk_far, nk_ref, sem.at[1])
    weights_in.start()
    kept_in.start()
    first, width = S_WIN[block]
    at = first - X_WIN[block + 1][0]
    cut = first - first_g
    live = in_image(idx_ref[0], first, width, image)
    gain_up = gain_up_ref[...]
    n = R_BACK

    def some(r):
        rows = pl.ds(r, n)
        unit, rstd = unit_of(
            widen(flat(xo_ref[rows, at : at + width]), flat(xt_ref[rows, at : at + width]))
        )
        p = gain_up * jnp.concatenate(
            [
                flat(qm_ref[1, rows]).astype(F32) + flat(qr_ref[0, rows]).astype(F32),
                flat(qm_ref[0, rows]).astype(F32) + flat(qr_ref[1, rows]).astype(F32),
            ],
            axis=1,
        )
        change = p[:, :HALF] - chan_mean(p) - unit[:, :HALF] * chan_mean(p * unit)
        g = flat(g_ref[rows, cut : cut + width]).astype(F32) + rstd * change
        g = jnp.where(live, g.reshape(n, width, HALF), 0.0).astype(BF)
        if gn_ref is not None:
            gn_ref[rows] = g
        s = flat(g.astype(F32) * d_ref[rows])
        scatter_s(block, s, r, n, sbuf, sown)

    row_loop(some, n)
    weights_in.wait()
    if block:
        q_phase(block, sbuf, w_ref, wq, q_ref)
    kept_in.wait()
    weight_phase(block, dims, idx_ref, sown, nk_ref, w_ref, gain_ref[...], wg_ref)


def finish_kernel(dims, slabs, all_ref, perm_ref, out_ref):
    own_chans, share, lines = dims
    bits = lines.bit_length() - 1
    col = lax.broadcasted_iota(jnp.int32, (own_chans, slabs * lines), 1)
    place = jnp.bitwise_and(col, lines - 1)
    row = jnp.right_shift(col, bits) * share + place
    pick = (lax.broadcasted_iota(jnp.int32, (own_chans, slabs * lines), 0) == row) & (place < share)
    pick = jnp.where(pick, 1.0, 0.0).astype(BF)
    for t in range(TAPS):
        grads = dot(pick, all_ref[:, t * CHANS : (t + 1) * CHANS], NN).astype(BF)
        out_ref[t] = dot(grads, perm_ref[...], NT)


def local(sizes, x_in, cot, w1, gain):
    nx, nz, ny, ns = sizes
    own_chans, rows = x_in.shape[1], x_in.shape[2]
    image = x_in.shape[3]
    shards = nx * nz
    share = own_chans // ny
    lines = 8
    while lines < share + 1:
        lines *= 2
    dims = (own_chans, share, lines)
    sec, ax, az = lax.axis_index("section"), lax.axis_index("x"), lax.axis_index("zh")
    core, slab = lax.axis_index("core"), lax.axis_index("slab")
    patch = ax * nz + az
    idx = jnp.stack([patch * OWN, slab, ax, sec]).astype(jnp.int32)

    def other(value):
        return lax.ppermute(value, "core", [(0, 1), (1, 0)])

    order = np.arange(CHANS).reshape(shards, 2, own_chans)
    orders = [np.concatenate([order[:, h].ravel(), order[:, 1 - h].ravel()]) for h in (0, 1)]
    perms = np.stack([np.eye(CHANS, dtype=np.float32)[:, o] for o in orders])
    perm = lax.dynamic_index_in_dim(jnp.asarray(perms, BF), core, 0, keepdims=False)

    windows = call(
        window_kernel, shape((shards, rows, own_chans, XWIN + CWIN), BF), [], (idx, x_in, cot), (0,)
    )

    def from_chips(value, axis, size):
        moves = [[(i, (i - j) % size) for i in range(size)] for j in range(1, size)]
        return [value] + [lax.ppermute(value, axis, move) for move in moves]

    packed = call(prep_kernel, shape((own_chans, CARRY), BF), [], (w1[0], gain, perm))
    wide = jnp.broadcast_to(packed[None], (ns * nz, own_chans, CARRY))
    wide = lax.all_to_all(wide, ("section", "zh"), 0, 0, tiled=True)
    wide = wide.reshape(ns, nz * own_chans, CARRY)


    first = from_chips(wide[0], "x", nx)
    pair = lax.all_gather(wide[1:3], "x", axis=1, tiled=True)
    last = lax.all_gather(wide[3], "x", axis=0, tiled=True)

    windows, wide = lax.optimization_barrier((windows, wide))
    recv = lax.all_to_all(windows, ("x", "zh"), 0, 0, tiled=True)
    recv, first = lax.optimization_barrier((recv, first))
    weights, index = [first, [pair], [pair], [last]], [None, 0, 1, None]
    row_pieces = from_chips(recv, "slab", ny)
    x_own, cot_own = call(
        functools.partial(assemble_kernel, ny, rows),
        (shape((ROWS, XWIN, HALF), BF), shape((ROWS, CWIN, HALF), BF)),
        [],
        (idx, *row_pieces),
        (0,),
    )

    taps3 = 3 * CHANS
    nk_shape = (ROWS + 2 * PAD, OWN, taps3)
    gain_shape = shape((1, CHANS), F32)
    halves, slopes, shifted, gains = [(x_own, other(x_own))], [], [], []
    for b in range(ns - 1):
        width = X_WIN[b + 1][1]
        pieces = len(weights[b])
        many = pieces > 1
        whole_shape = shape((HALF, CARRY), BF)
        y, slope, gain_b, nk, *whole = call(
            functools.partial(forward_kernel, b, image, pieces, index[b]),
            (
                shape((ROWS, width, HALF), BF),
                shape((ROWS, S_WIN[b][1], HALF), F32),
                gain_shape,
                shape(nk_shape, BF),
            )
            + (whole_shape,) * many,
            [
                pltpu.VMEM(nk_shape, BF),
                pltpu.VMEM((ROWS + 2 * PAD, width, taps3), BF),
                pltpu.VMEM((ROWS, width, HALF), F32),
                pltpu.SemaphoreType.DMA((2,)),
            ]
            + [pltpu.VMEM((HALF, CARRY), BF)],
            (idx, *halves[b], *weights[b]),
            (0,),
            () if many else (3,),
            (3, 4),
            0,
        )
        halves.append((y, other(y)))
        slopes.append(slope)
        shifted.append(nk)
        gains.append(gain_b)
        weights[b] = whole[0] if whole else weights[b][0]

    def back_scratch(b):
        width = S_WIN[b - 1][1]
        return [
            pltpu.VMEM((ROWS + 2 * PAD, width, 768), BF),
            pltpu.VMEM((ROWS, OWN, HALF), BF),
            pltpu.VMEM((3, 768, CHANS), BF),
        ]

    count = shards * lines
    wg_shape = shape((count, TAPS * CHANS), BF)
    width = X_WIN[4][1]
    sbuf_s, sown_s, wq_s = back_scratch(3)
    q, grads, gain_b = call(
        functools.partial(turn_kernel, dims),
        (shape((2, ROWS, S_WIN[2][1], HALF), BF), wg_shape, gain_shape),
        [
            pltpu.VMEM((ROWS + 2 * PAD, width, taps3), BF),
            pltpu.VMEM(nk_shape, BF),
            pltpu.VMEM((ROWS, width, HALF), F32),
            sbuf_s,
            sown_s,
            wq_s,
        ],
        (idx, *halves[3], cot_own, weights[3][0]),
        (0,),
        micros=12,
    )
    gains.append(gain_b)

    def reduced(*values):
        value = jnp.stack([v.reshape(nx, nz * lines, LANES) for v in values], axis=1)
        value = lax.all_to_all(value, "x", 0, 0, tiled=True)
        return jnp.sum(value.astype(F32), axis=0).astype(BF)

    weight_parts = [None] * 3 + [grads]
    g, first_g = cot_own, S_WIN[3][0]
    for b in (2, 1, 0):
        args = (
            idx, q, other(q), *halves[b + 1], g, gains[b + 1], slopes[b], weights[b], shifted[b], gains[b],
        )
        kernel = functools.partial(backward_kernel, b, dims, image, first_g, index[b])
        fetched = [
            pltpu.VMEM((HALF, CARRY), BF),
            pltpu.VMEM(nk_shape, BF),
            pltpu.SemaphoreType.DMA((2,)),
        ]
        if b:
            sbuf_s, sown_s, wq_s = back_scratch(b)
            q, g, grads = call(
                kernel,
                (
                    shape((2, ROWS, S_WIN[b - 1][1], HALF), BF),
                    shape((ROWS, S_WIN[b][1], HALF), BF),
                    wg_shape,
                ),
                fetched + [sown_s, sbuf_s, wq_s],
                args,
                (0,),
                (8, 9),
                micros=8,
            )
        else:
            own_s = pltpu.VMEM((ROWS, OWN, HALF), BF)
            (grads,) = call(kernel, (wg_shape,), fetched + [own_s], args, (0,), (8, 9))
        first_g = S_WIN[b][0]
        weight_parts[b] = grads
        if b == 2:
            late = reduced(*weight_parts[2:])

    parts = jnp.concatenate([reduced(*weight_parts[:2]), late]).reshape(ns * nz, lines, LANES)
    parts = lax.all_to_all(parts, ("section", "zh"), 0, 0, tiled=True)
    total = jnp.sum(parts.astype(F32), axis=0).astype(BF)
    every = lax.all_gather(total, "slab", axis=0, tiled=True)
    weight_grad = call(
        functools.partial(finish_kernel, dims, ny),
        shape((TAPS, own_chans, CHANS), F32),
        [],
        (every, perm),
    )
    gain_rows = every.reshape(ny, lines, LANES)[:, share, :CHANS]
    gain_all = jnp.sum(gain_rows.astype(F32), axis=0)
    here = lax.dynamic_slice_in_dim(gain_all, patch * own_chans, own_chans)
    there = lax.dynamic_slice_in_dim(gain_all, HALF + patch * own_chans, own_chans)
    gain_grad = here + other(there)
    return weight_grad[None], gain_grad[None]


def solution(mesh):
    ns, chans, ny = mesh.shape["section"], mesh.shape["ch"], mesh.shape["slab"]
    nz = 2 if chans % 4 == 0 else 1
    nx = chans // (2 * nz)
    axes = ("section", "x", "zh", "core", "slab")
    fine = Mesh(mesh.devices.reshape(ns, nx, nz, 2, ny), axes)
    ch = ("x", "zh", "core")
    return jax.shard_map(
        functools.partial(local, (nx, nz, ny, ns)),
        mesh=fine,
        in_specs=(
            P(None, ch, "slab", None),
            P(None, ch, "slab", None),
            P("section", None, ch, None),
            P("section", None),
        ),
        out_specs=(P("section", None, ch, None), P("section", ch)),
        check_vma=False,
    )
```

```python
import functools

import jax
import jax.numpy as jnp
import numpy as np
from jax import lax
from jax.experimental import pallas as pl
from jax.experimental.pallas import tpu as pltpu
from jax.sharding import Mesh, PartitionSpec as P

NORM_EPS = 1e-05
SLOPE_SCALE = 0.7978845608028654
CUBIC_COEF = 0.044715
BF = jnp.bfloat16
F32 = jnp.float32

ROWS = 32
CHANS = 384
HALF = 192
TAPS = 9
DIL = (1, 2, 4, 8)
OWN = 16
XWIN = 80
CWIN = 48
PAD = 8
X_WIN = ((0, 80), (0, 80), (0, 80), (8, 64), (16, 48))
S_WIN = ((32, 16), (24, 32), (24, 32), (16, 48))
VMEM_LIMIT = 56 * 1024 * 1024
PARAMS = pltpu.CompilerParams(vmem_limit_bytes=VMEM_LIMIT)
NT = (((1,), (1,)), ((), ()))
NN = (((1,), (0,)), ((), ()))
LANES = TAPS * CHANS
CARRY = LANES + 128
R_NORM, R_EPI, R_TURN, R_BACK = 4, 2, 2, 8


def dot(a, b, dims):
    return lax.dot_general(a, b, dims, preferred_element_type=F32)


def call(kernel, out_shape, scratch, args, smem=(), far=(), far_out=(), micros=2):
    vm = pl.BlockSpec(memory_space=pltpu.VMEM)
    sm = pl.BlockSpec(memory_space=pltpu.SMEM)
    hb = pl.BlockSpec(memory_space=pltpu.HBM)
    if isinstance(out_shape, tuple):
        out_specs = tuple(hb if i in far_out else vm for i in range(len(out_shape)))
    else:
        out_specs = vm
    return pl.pallas_call(
        kernel,
        out_shape=out_shape,
        in_specs=[sm if i in smem else hb if i in far else vm for i in range(len(args))],
        out_specs=out_specs,
        scratch_shapes=scratch,
        compiler_params=PARAMS,
        cost_estimate=pl.CostEstimate(flops=micros * 10**9, bytes_accessed=micros * 10**6, transcendentals=0),
    )(*args)


def shape(dims, dtype):
    return jax.ShapeDtypeStruct(dims, dtype)


def row_loop(body, rows, unroll=1):
    span = rows * unroll

    def step(i, carry):
        for k in range(unroll):
            body(pl.multiple_of(i * span, span) + k * rows)
        return carry

    lax.fori_loop(0, ROWS // span, step, 0)


def flat(value):
    return value.reshape(value.shape[0] * value.shape[1], value.shape[2])


def in_image(base, first, count, width):
    cols = lax.broadcasted_iota(jnp.int32, (1, count, HALF), 1) + (base - 32 + first)
    return (cols >= 0) & (cols < width)


def widen(own, oth):
    return jnp.concatenate([own.astype(F32), oth.astype(F32)], axis=1)


def chan_mean(value):
    folded = value[:, :128] + value[:, 128:256] + value[:, 256:]
    return jnp.sum(folded, axis=1, keepdims=True) / CHANS


def unit_of(value):
    mean = chan_mean(value)
    rstd = lax.rsqrt(chan_mean(value * value) - mean * mean + NORM_EPS)
    return (value - mean) * rstd, rstd


def read_gain(w_ref):
    tile = w_ref[0:16, LANES:CARRY].astype(F32)
    return jnp.concatenate(
        [(tile[p : p + 1] + tile[3 + p : 4 + p]) + tile[6 + p : 7 + p] for p in range(3)], axis=1
    )


def gelu_inner(pre):
    return jnp.tanh(SLOPE_SCALE * (pre + CUBIC_COEF * pre * pre * pre))


def gelu_slope(pre, tangent):
    return 0.5 * (1.0 + tangent) + 0.5 * pre * (1.0 - tangent * tangent) * SLOPE_SCALE * (
        1.0 + 3.0 * CUBIC_COEF * pre * pre
    )


def prep_kernel(w_ref, gain_ref, perm_ref, out_ref):
    for t in range(TAPS):
        out_ref[:, t * CHANS : (t + 1) * CHANS] = dot(w_ref[t], perm_ref[...], NN).astype(BF)
    rest = jnp.broadcast_to(gain_ref[...], (8, CHANS))
    row = lax.broadcasted_iota(jnp.int32, (out_ref.shape[0], 128), 0)
    tile = jnp.zeros((out_ref.shape[0], 128), F32)
    for k in range(3):
        piece = rest.astype(BF)
        rest = rest - piece.astype(F32)
        moved = dot(piece, perm_ref[...], NN)
        for p in range(3):
            tile = jnp.where(row == 3 * k + p, moved[0:1, 128 * p : 128 * p + 128], tile)
    out_ref[:, LANES:CARRY] = tile.astype(BF)


def window_kernel(idx_ref, x_ref, cot_ref, out_ref):
    shards, rows, chans, lanes = out_ref.shape
    image = x_ref.shape[3]
    x = x_ref[idx_ref[3]].astype(F32)
    cot = cot_ref[idx_ref[3]].astype(F32)
    lane = lax.broadcasted_iota(jnp.int32, (chans, lanes), 1)
    room = jnp.zeros((chans, lanes - image), F32)
    for r in range(rows):
        from_x, from_cot = x[:, r, :], cot[:, r, :]
        if image < lanes:
            from_x = jnp.concatenate([from_x, room], axis=1)
            from_cot = jnp.concatenate([from_cot, room], axis=1)
        for p in range(shards):
            here = None
            for value, start in ((from_x, OWN * p - 32), (from_cot, OWN * p - 16 - XWIN)):
                shift = (-start) % lanes
                moved = pltpu.roll(value, shift, 1) if shift else value
                moved = jnp.where((lane + start >= 0) & (lane + start < image), moved, 0.0)
                here = moved if here is None else jnp.where(lane < XWIN, here, moved)
            out_ref[p, r] = here.astype(BF)


def assemble_kernel(slabs, rows, idx_ref, *refs):
    pieces, (x_ref, cot_ref) = refs[:slabs], refs[slabs:]
    lanes = XWIN + CWIN
    eye = (
        lax.broadcasted_iota(jnp.int32, (lanes, lanes), 0)
        == lax.broadcasted_iota(jnp.int32, (lanes, lanes), 1)
    ).astype(F32).astype(BF)

    def one(r, carry):
        for y in range(slabs):
            piece = pieces[y][:, pl.ds(r, 1)].astype(F32)
            piece = piece.reshape(HALF, lanes).astype(BF)
            flipped = dot(eye, piece, NT).astype(BF)
            place = lax.rem(idx_ref[1] + y, slabs) * rows + r
            x_ref[pl.ds(place, 1)] = flipped[:XWIN].reshape(1, XWIN, HALF)
            cot_ref[pl.ds(place, 1)] = flipped[XWIN:].reshape(1, CWIN, HALF)
        return carry

    lax.fori_loop(0, rows, one, 0)


def norm_phase(block, xo_ref, xt_ref, gain, nbuf, nk):
    d = DIL[block]
    first_in, width_in = X_WIN[block]
    first_out, width_out = X_WIN[block + 1]
    low = first_out - first_in
    own = 32 - first_in
    for edge in (0, PAD + ROWS):
        nbuf[edge : edge + PAD] = jnp.zeros((PAD, width_out, 3 * CHANS), BF)
        nk[edge : edge + PAD] = jnp.zeros((PAD, OWN, 3 * CHANS), BF)
    n = R_NORM

    def some(r):
        unit, _ = unit_of(widen(flat(xo_ref[pl.ds(r, n)]), flat(xt_ref[pl.ds(r, n)])))
        both = unit * gain
        for kx in range(3):
            shift = (-(kx - 1) * d) % (n * width_in)
            moved = pltpu.roll(both, shift, 0) if shift else both
            moved = moved.reshape(n, width_in, CHANS)
            lanes = slice(kx * CHANS, (kx + 1) * CHANS)
            nbuf[pl.ds(PAD + r, n), :, lanes] = moved[:, low : low + width_out].astype(BF)
            nk[pl.ds(PAD + r, n), :, lanes] = moved[:, own : own + OWN].astype(BF)

    row_loop(some, n)


def conv_phase(block, nbuf, w_ref, pre):
    d = DIL[block]
    width = X_WIN[block + 1][1]
    step = 8

    def one(i, carry):
        r0 = i * step
        acc = None
        for ky in range(3):
            left = nbuf[pl.ds(PAD + r0 + (ky - 1) * d, step)].reshape(step * width, 3 * CHANS)
            term = dot(left, w_ref[:, ky * 3 * CHANS : (ky + 1) * 3 * CHANS], NT)
            acc = term if acc is None else acc + term
        pre[pl.ds(r0, step)] = acc.reshape(step, width, HALF)
        return carry

    lax.fori_loop(0, ROWS // step, one, 0)


def forward_kernel(block, image, pieces, index, idx_ref, xo_ref, xt_ref, *rest):
    w_refs, rest = rest[:pieces], rest[pieces:]
    y_ref, d_ref, gain_ref, nk_far, *rest = rest
    whole = None
    if pieces > 1:
        whole_far, nk, nbuf, pre, sem, w_ref = rest
        lines = HALF // pieces
        for j in range(pieces):
            place = lax.rem(idx_ref[2] + j, pieces) * lines
            w_ref[pl.ds(pl.multiple_of(place, lines), lines)] = w_refs[j][...]
        whole = pltpu.make_async_copy(w_ref, whole_far, sem.at[1])
        whole.start()
    else:
        nk, nbuf, pre, sem, w_ref = rest
        source = w_refs[0] if index is None else w_refs[0].at[index]
        coming = pltpu.make_async_copy(source, w_ref, sem.at[1])
        coming.start()
        coming.wait()
    first_in = X_WIN[block][0]
    first_out, width_out = X_WIN[block + 1]
    first_s, width_s = S_WIN[block]
    gain = read_gain(w_ref)
    gain_ref[...] = gain
    norm_phase(block, xo_ref, xt_ref, gain, nbuf, nk)
    kept = pltpu.make_async_copy(nk, nk_far, sem.at[0])
    kept.start()
    conv_phase(block, nbuf, w_ref, pre)
    live = in_image(idx_ref[0], first_out, width_out, image)
    low, at = first_out - first_in, first_s - first_out
    n = R_EPI

    def some(r):
        act = pre[pl.ds(r, n)]
        tangent = gelu_inner(act)
        out = xo_ref[pl.ds(r, n)].astype(F32)[:, low : low + width_out] + 0.5 * act * (1.0 + tangent)
        y_ref[pl.ds(r, n)] = jnp.where(live, out, 0.0).astype(BF)
        d_ref[pl.ds(r, n)] = gelu_slope(act[:, at : at + width_s], tangent[:, at : at + width_s])

    row_loop(some, n)
    kept.wait()
    if whole is not None:
        whole.wait()


def scatter_s(block, s, r, n, sbuf, sown):
    first, width = S_WIN[block]
    rows = s.reshape(n, width, HALF)
    sown[pl.ds(r, n)] = rows[:, 32 - first : 32 - first + OWN].astype(BF)
    if sbuf is None:
        return
    d = DIL[block]
    first_q, width_q = S_WIN[block - 1]
    low = first_q - first
    gap = jnp.zeros((n * width, 256 - HALF), F32)
    wide = jnp.concatenate([s, gap], axis=1)
    for kx in range(3):
        shift = ((kx - 1) * d) % (n * width)
        moved = pltpu.roll(wide, shift, 0) if shift else wide
        moved = moved.reshape(n, width, 256)[:, low : low + width_q]
        sbuf[pl.ds(PAD + r, n), :, kx * 256 : (kx + 1) * 256] = moved.astype(BF)


def q_phase(block, sbuf, w_ref, wq, q_ref):
    d = DIL[block]
    width = S_WIN[block - 1][1]
    for ky in range(3):
        for kx in range(3):
            t = 3 * ky + kx
            wq[ky, kx * 256 : kx * 256 + HALF] = w_ref[:, t * CHANS : (t + 1) * CHANS]
            wq[ky, kx * 256 + HALF : (kx + 1) * 256] = jnp.zeros((256 - HALF, CHANS), BF)
    for edge in (0, PAD + ROWS):
        sbuf[edge : edge + PAD] = jnp.zeros((PAD, width, 768), BF)
    step = 512 // width

    def one(i, carry):
        r0 = i * step
        acc = None
        for ky in range(3):
            left = sbuf[pl.ds(PAD + r0 - (ky - 1) * d, step)].reshape(step * width, 768)
            term = dot(left, wq[ky], NN)
            acc = term if acc is None else acc + term
        q_ref[0, pl.ds(r0, step)] = acc[:, HALF:].reshape(step, width, HALF).astype(BF)
        q_ref[1, pl.ds(r0, step)] = acc[:, :HALF].reshape(step, width, HALF).astype(BF)
        return carry

    lax.fori_loop(0, ROWS // step, one, 0)


def weight_phase(block, dims, idx_ref, sown, nk, w_ref, gain, wg_ref):
    own_chans, share, lines = dims
    d = DIL[block]
    count = (HALF // own_chans) * lines
    bits = lines.bit_length() - 1
    line = lax.broadcasted_iota(jnp.int32, (count, HALF), 0)
    place = jnp.bitwise_and(line, lines - 1)
    want = jnp.right_shift(line, bits) * own_chans + share * idx_ref[1] + place
    pick = (lax.broadcasted_iota(jnp.int32, (count, HALF), 1) == want) & (place < share)
    pick = jnp.where(pick, 1.0, 0.0).astype(BF)
    left = dot(pick, sown[...].reshape(ROWS * OWN, HALF), NT).astype(BF)
    total = jnp.zeros((1, CHANS), F32)
    first = None
    for ky in range(3):
        lanes = slice(ky * 3 * CHANS, (ky + 1) * 3 * CHANS)
        start = PAD + (ky - 1) * d
        right = nk[start : start + ROWS].reshape(ROWS * OWN, 3 * CHANS)
        grads = dot(left, right, NN)
        wg_ref[:, lanes] = grads.astype(BF)
        part = jnp.sum(grads * dot(pick, w_ref[:, lanes], NN), axis=0, keepdims=True)
        for kx in range(3):
            total = total + part[:, kx * CHANS : (kx + 1) * CHANS]
        if ky == 0:
            first = grads[:, :CHANS]
    spot = jnp.bitwise_and(lax.broadcasted_iota(jnp.int32, (count, CHANS), 0), lines - 1)
    wg_ref[:, :CHANS] = jnp.where(spot == share, total / gain, first).astype(BF)


def turn_kernel(dims, idx_ref, xo_ref, xt_ref, cot_ref, w_ref, q_ref, wg_ref, gain_ref,
                nbuf, nk, pre, sbuf, sown, wq):
    gain = read_gain(w_ref)
    gain_ref[...] = gain
    norm_phase(3, xo_ref, xt_ref, gain, nbuf, nk)
    conv_phase(3, nbuf, w_ref, pre)
    n = R_TURN

    def some(r):
        act = flat(pre[pl.ds(r, n)])
        s = flat(cot_ref[pl.ds(r, n)]).astype(F32) * gelu_slope(act, gelu_inner(act))
        scatter_s(3, s, r, n, sbuf, sown)

    row_loop(some, n)
    q_phase(3, sbuf, w_ref, wq, q_ref)
    weight_phase(3, dims, idx_ref, sown, nk, w_ref, gain, wg_ref)


def backward_kernel(block, dims, image, first_g, index, idx_ref, qm_ref, qr_ref, xo_ref, xt_ref, g_ref,
                    gain_up_ref, d_ref, w_far, nk_far, gain_ref, *rest):
    if block:
        q_ref, gn_ref, wg_ref, w_ref, nk_ref, sem, sown, sbuf, wq = rest
    else:
        wg_ref, w_ref, nk_ref, sem, sown = rest
        q_ref = gn_ref = sbuf = wq = None
    w_far = w_far if index is None else w_far.at[index]
    weights_in = pltpu.make_async_copy(w_far, w_ref, sem.at[0])
    kept_in = pltpu.make_async_copy(nk_far, nk_ref, sem.at[1])
    weights_in.start()
    kept_in.start()
    first, width = S_WIN[block]
    at = first - X_WIN[block + 1][0]
    cut = first - first_g
    live = in_image(idx_ref[0], first, width, image)
    gain_up = gain_up_ref[...]
    n = R_BACK

    def some(r):
        rows = pl.ds(r, n)
        unit, rstd = unit_of(
            widen(flat(xo_ref[rows, at : at + width]), flat(xt_ref[rows, at : at + width]))
        )
        p = gain_up * jnp.concatenate(
            [
                flat(qm_ref[1, rows]).astype(F32) + flat(qr_ref[0, rows]).astype(F32),
                flat(qm_ref[0, rows]).astype(F32) + flat(qr_ref[1, rows]).astype(F32),
            ],
            axis=1,
        )
        change = p[:, :HALF] - chan_mean(p) - unit[:, :HALF] * chan_mean(p * unit)
        g = flat(g_ref[rows, cut : cut + width]).astype(F32) + rstd * change
        g = jnp.where(live, g.reshape(n, width, HALF), 0.0).astype(BF)
        if gn_ref is not None:
            gn_ref[rows] = g
        s = flat(g.astype(F32) * d_ref[rows])
        scatter_s(block, s, r, n, sbuf, sown)

    row_loop(some, n)
    weights_in.wait()
    if block:
        q_phase(block, sbuf, w_ref, wq, q_ref)
    kept_in.wait()
    weight_phase(block, dims, idx_ref, sown, nk_ref, w_ref, gain_ref[...], wg_ref)


def finish_kernel(dims, slabs, all_ref, perm_ref, out_ref):
    own_chans, share, lines = dims
    bits = lines.bit_length() - 1
    col = lax.broadcasted_iota(jnp.int32, (own_chans, slabs * lines), 1)
    place = jnp.bitwise_and(col, lines - 1)
    row = jnp.right_shift(col, bits) * share + place
    pick = (lax.broadcasted_iota(jnp.int32, (own_chans, slabs * lines), 0) == row) & (place < share)
    pick = jnp.where(pick, 1.0, 0.0).astype(BF)
    for t in range(TAPS):
        grads = dot(pick, all_ref[:, t * CHANS : (t + 1) * CHANS], NN).astype(BF)
        out_ref[t] = dot(grads, perm_ref[...], NT)


def local(sizes, x_in, cot, w1, gain):
    nx, nz, ny, ns = sizes
    own_chans, rows = x_in.shape[1], x_in.shape[2]
    image = x_in.shape[3]
    shards = nx * nz
    share = own_chans // ny
    lines = 8
    while lines < share + 1:
        lines *= 2
    dims = (own_chans, share, lines)
    sec, ax, az = lax.axis_index("section"), lax.axis_index("x"), lax.axis_index("zh")
    core, slab = lax.axis_index("core"), lax.axis_index("slab")
    patch = ax * nz + az
    idx = jnp.stack([patch * OWN, slab, ax, sec]).astype(jnp.int32)

    def other(value):
        return lax.ppermute(value, "core", [(0, 1), (1, 0)])

    order = np.arange(CHANS).reshape(shards, 2, own_chans)
    orders = [np.concatenate([order[:, h].ravel(), order[:, 1 - h].ravel()]) for h in (0, 1)]
    perms = np.stack([np.eye(CHANS, dtype=np.float32)[:, o] for o in orders])
    perm = lax.dynamic_index_in_dim(jnp.asarray(perms, BF), core, 0, keepdims=False)

    windows = call(
        window_kernel, shape((shards, rows, own_chans, XWIN + CWIN), BF), [], (idx, x_in, cot), (0,)
    )

    def from_chips(value, axis, size):
        moves = [[(i, (i - j) % size) for i in range(size)] for j in range(1, size)]
        return [value] + [lax.ppermute(value, axis, move) for move in moves]

    packed = call(prep_kernel, shape((own_chans, CARRY), BF), [], (w1[0], gain, perm))
    wide = jnp.broadcast_to(packed[None], (ns * nz, own_chans, CARRY))
    wide = lax.all_to_all(wide, ("section", "zh"), 0, 0, tiled=True)
    wide = wide.reshape(ns, nz * own_chans, CARRY)


    first = from_chips(wide[0], "x", nx)

    windows, wide = lax.optimization_barrier((windows, wide))
    recv = lax.all_to_all(windows, ("x", "zh"), 0, 0, tiled=True)
    rest, first, recv = lax.optimization_barrier((wide[1:], first, recv))
    pair = lax.all_gather(rest[:2], "x", axis=1, tiled=True)
    last = lax.all_gather(rest[2], "x", axis=0, tiled=True)
    weights, index = [first, [pair], [pair], [last]], [None, 0, 1, None]
    row_pieces = from_chips(recv, "slab", ny)
    x_own, cot_own = call(
        functools.partial(assemble_kernel, ny, rows),
        (shape((ROWS, XWIN, HALF), BF), shape((ROWS, CWIN, HALF), BF)),
        [],
        (idx, *row_pieces),
        (0,),
    )

    taps3 = 3 * CHANS
    nk_shape = (ROWS + 2 * PAD, OWN, taps3)
    gain_shape = shape((1, CHANS), F32)
    halves, slopes, shifted, gains = [(x_own, other(x_own))], [], [], []
    for b in range(ns - 1):
        width = X_WIN[b + 1][1]
        pieces = len(weights[b])
        many = pieces > 1
        whole_shape = shape((HALF, CARRY), BF)
        y, slope, gain_b, nk, *whole = call(
            functools.partial(forward_kernel, b, image, pieces, index[b]),
            (
                shape((ROWS, width, HALF), BF),
                shape((ROWS, S_WIN[b][1], HALF), F32),
                gain_shape,
                shape(nk_shape, BF),
            )
            + (whole_shape,) * many,
            [
                pltpu.VMEM(nk_shape, BF),
                pltpu.VMEM((ROWS + 2 * PAD, width, taps3), BF),
                pltpu.VMEM((ROWS, width, HALF), F32),
                pltpu.SemaphoreType.DMA((2,)),
            ]
            + [pltpu.VMEM((HALF, CARRY), BF)],
            (idx, *halves[b], *weights[b]),
            (0,),
            () if many else (3,),
            (3, 4),
            0,
        )
        halves.append((y, other(y)))
        slopes.append(slope)
        shifted.append(nk)
        gains.append(gain_b)
        weights[b] = whole[0] if whole else weights[b][0]

    def back_scratch(b):
        width = S_WIN[b - 1][1]
        return [
            pltpu.VMEM((ROWS + 2 * PAD, width, 768), BF),
            pltpu.VMEM((ROWS, OWN, HALF), BF),
            pltpu.VMEM((3, 768, CHANS), BF),
        ]

    count = shards * lines
    wg_shape = shape((count, TAPS * CHANS), BF)
    width = X_WIN[4][1]
    sbuf_s, sown_s, wq_s = back_scratch(3)
    q, grads, gain_b = call(
        functools.partial(turn_kernel, dims),
        (shape((2, ROWS, S_WIN[2][1], HALF), BF), wg_shape, gain_shape),
        [
            pltpu.VMEM((ROWS + 2 * PAD, width, taps3), BF),
            pltpu.VMEM(nk_shape, BF),
            pltpu.VMEM((ROWS, width, HALF), F32),
            sbuf_s,
            sown_s,
            wq_s,
        ],
        (idx, *halves[3], cot_own, weights[3][0]),
        (0,),
        micros=12,
    )
    gains.append(gain_b)

    def reduced(*values):
        value = jnp.stack([v.reshape(nx, nz * lines, LANES) for v in values], axis=1)
        value = lax.all_to_all(value, "x", 0, 0, tiled=True)
        return jnp.sum(value.astype(F32), axis=0).astype(BF)

    weight_parts = [None] * 3 + [grads]
    g, first_g = cot_own, S_WIN[3][0]
    for b in (2, 1, 0):
        args = (
            idx, q, other(q), *halves[b + 1], g, gains[b + 1], slopes[b], weights[b], shifted[b], gains[b],
        )
        kernel = functools.partial(backward_kernel, b, dims, image, first_g, index[b])
        fetched = [
            pltpu.VMEM((HALF, CARRY), BF),
            pltpu.VMEM(nk_shape, BF),
            pltpu.SemaphoreType.DMA((2,)),
        ]
        if b:
            sbuf_s, sown_s, wq_s = back_scratch(b)
            q, g, grads = call(
                kernel,
                (
                    shape((2, ROWS, S_WIN[b - 1][1], HALF), BF),
                    shape((ROWS, S_WIN[b][1], HALF), BF),
                    wg_shape,
                ),
                fetched + [sown_s, sbuf_s, wq_s],
                args,
                (0,),
                (8, 9),
                micros=8,
            )
        else:
            own_s = pltpu.VMEM((ROWS, OWN, HALF), BF)
            (grads,) = call(kernel, (wg_shape,), fetched + [own_s], args, (0,), (8, 9))
        first_g = S_WIN[b][0]
        weight_parts[b] = grads
        if b == 2:
            late = [reduced(*weight_parts[2:])]
        else:
            late.insert(0, reduced(grads))

    parts = jnp.concatenate(late).reshape(ns * nz, lines, LANES)
    parts = lax.all_to_all(parts, ("section", "zh"), 0, 0, tiled=True)
    total = jnp.sum(parts.astype(F32), axis=0).astype(BF)
    every = lax.all_gather(total, "slab", axis=0, tiled=True)
    weight_grad = call(
        functools.partial(finish_kernel, dims, ny),
        shape((TAPS, own_chans, CHANS), F32),
        [],
        (every, perm),
    )
    gain_rows = every.reshape(ny, lines, LANES)[:, share, :CHANS]
    gain_all = jnp.sum(gain_rows.astype(F32), axis=0)
    here = lax.dynamic_slice_in_dim(gain_all, patch * own_chans, own_chans)
    there = lax.dynamic_slice_in_dim(gain_all, HALF + patch * own_chans, own_chans)
    gain_grad = here + other(there)
    return weight_grad[None], gain_grad[None]


def solution(mesh):
    ns, chans, ny = mesh.shape["section"], mesh.shape["ch"], mesh.shape["slab"]
    nz = 2 if chans % 4 == 0 else 1
    nx = chans // (2 * nz)
    axes = ("section", "x", "zh", "core", "slab")
    fine = Mesh(mesh.devices.reshape(ns, nx, nz, 2, ny), axes)
    ch = ("x", "zh", "core")
    return jax.shard_map(
        functools.partial(local, (nx, nz, ny, ns)),
        mesh=fine,
        in_specs=(
            P(None, ch, "slab", None),
            P(None, ch, "slab", None),
            P("section", None, ch, None),
            P("section", None),
        ),
        out_specs=(P("section", None, ch, None), P("section", ch)),
        check_vma=False,
    )
```

```python
import functools

import jax
import jax.numpy as jnp
import numpy as np
from jax import lax
from jax.experimental import pallas as pl
from jax.experimental.pallas import tpu as pltpu
from jax.sharding import Mesh, PartitionSpec as P

NORM_EPS = 1e-05
SLOPE_SCALE = 0.7978845608028654
CUBIC_COEF = 0.044715
BF = jnp.bfloat16
F32 = jnp.float32

ROWS = 32
CHANS = 384
HALF = 192
TAPS = 9
DIL = (1, 2, 4, 8)
OWN = 16
XWIN = 80
CWIN = 48
PAD = 8
X_WIN = ((0, 80), (0, 80), (0, 80), (8, 64), (16, 48))
S_WIN = ((32, 16), (24, 32), (24, 32), (16, 48))
VMEM_LIMIT = 56 * 1024 * 1024
PARAMS = pltpu.CompilerParams(vmem_limit_bytes=VMEM_LIMIT)
NT = (((1,), (1,)), ((), ()))
NN = (((1,), (0,)), ((), ()))
LANES = TAPS * CHANS
CARRY = LANES + 128
R_NORM, R_EPI, R_TURN, R_BACK = 4, 2, 2, 8


def dot(a, b, dims):
    return lax.dot_general(a, b, dims, preferred_element_type=F32)


def call(kernel, out_shape, scratch, args, smem=(), far=(), far_out=(), micros=2):
    vm = pl.BlockSpec(memory_space=pltpu.VMEM)
    sm = pl.BlockSpec(memory_space=pltpu.SMEM)
    hb = pl.BlockSpec(memory_space=pltpu.HBM)
    if isinstance(out_shape, tuple):
        out_specs = tuple(hb if i in far_out else vm for i in range(len(out_shape)))
    else:
        out_specs = vm
    return pl.pallas_call(
        kernel,
        out_shape=out_shape,
        in_specs=[sm if i in smem else hb if i in far else vm for i in range(len(args))],
        out_specs=out_specs,
        scratch_shapes=scratch,
        compiler_params=PARAMS,
        cost_estimate=pl.CostEstimate(flops=micros * 10**9, bytes_accessed=micros * 10**6, transcendentals=0),
    )(*args)


def shape(dims, dtype):
    return jax.ShapeDtypeStruct(dims, dtype)


def row_loop(body, rows, unroll=1):
    span = rows * unroll

    def step(i, carry):
        for k in range(unroll):
            body(pl.multiple_of(i * span, span) + k * rows)
        return carry

    lax.fori_loop(0, ROWS // span, step, 0)


def flat(value):
    return value.reshape(value.shape[0] * value.shape[1], value.shape[2])


def in_image(base, first, count, width):
    cols = lax.broadcasted_iota(jnp.int32, (1, count, HALF), 1) + (base - 32 + first)
    return (cols >= 0) & (cols < width)


def widen(own, oth):
    return jnp.concatenate([own.astype(F32), oth.astype(F32)], axis=1)


def chan_mean(value):
    folded = value[:, :128] + value[:, 128:256] + value[:, 256:]
    return jnp.sum(folded, axis=1, keepdims=True) / CHANS


def unit_of(value):
    mean = chan_mean(value)
    rstd = lax.rsqrt(chan_mean(value * value) - mean * mean + NORM_EPS)
    return (value - mean) * rstd, rstd


def read_gain(tile_ref, first=LANES):
    tile = tile_ref[0:16, first : first + 128].astype(F32)
    return jnp.concatenate(
        [(tile[p : p + 1] + tile[3 + p : 4 + p]) + tile[6 + p : 7 + p] for p in range(3)], axis=1
    )


def gelu_inner(pre):
    return jnp.tanh(SLOPE_SCALE * (pre + CUBIC_COEF * pre * pre * pre))


def gelu_slope(pre, tangent):
    return 0.5 * (1.0 + tangent) + 0.5 * pre * (1.0 - tangent * tangent) * SLOPE_SCALE * (
        1.0 + 3.0 * CUBIC_COEF * pre * pre
    )


def prep_kernel(w_ref, gain_ref, perm_ref, out_ref):
    for t in range(TAPS):
        out_ref[:, t * CHANS : (t + 1) * CHANS] = dot(w_ref[t], perm_ref[...], NN).astype(BF)
    rest = jnp.broadcast_to(gain_ref[...], (8, CHANS))
    row = lax.broadcasted_iota(jnp.int32, (out_ref.shape[0], 128), 0)
    tile = jnp.zeros((out_ref.shape[0], 128), F32)
    for k in range(3):
        piece = rest.astype(BF)
        rest = rest - piece.astype(F32)
        moved = dot(piece, perm_ref[...], NN)
        for p in range(3):
            tile = jnp.where(row == 3 * k + p, moved[0:1, 128 * p : 128 * p + 128], tile)
    out_ref[:, LANES:CARRY] = tile.astype(BF)


def window_kernel(idx_ref, x_ref, cot_ref, out_ref):
    shards, rows, chans, lanes = out_ref.shape
    image = x_ref.shape[3]
    x = x_ref[idx_ref[3]].astype(F32)
    cot = cot_ref[idx_ref[3]].astype(F32)
    lane = lax.broadcasted_iota(jnp.int32, (chans, lanes), 1)
    room = jnp.zeros((chans, lanes - image), F32)
    for r in range(rows):
        from_x, from_cot = x[:, r, :], cot[:, r, :]
        if image < lanes:
            from_x = jnp.concatenate([from_x, room], axis=1)
            from_cot = jnp.concatenate([from_cot, room], axis=1)
        for p in range(shards):
            here = None
            for value, start in ((from_x, OWN * p - 32), (from_cot, OWN * p - 16 - XWIN)):
                shift = (-start) % lanes
                moved = pltpu.roll(value, shift, 1) if shift else value
                moved = jnp.where((lane + start >= 0) & (lane + start < image), moved, 0.0)
                here = moved if here is None else jnp.where(lane < XWIN, here, moved)
            out_ref[p, r] = here.astype(BF)


def assemble_kernel(slabs, rows, idx_ref, *refs):
    pieces, (x_ref, cot_ref) = refs[:slabs], refs[slabs:]
    lanes = XWIN + CWIN
    eye = (
        lax.broadcasted_iota(jnp.int32, (lanes, lanes), 0)
        == lax.broadcasted_iota(jnp.int32, (lanes, lanes), 1)
    ).astype(F32).astype(BF)

    def one(r, carry):
        for y in range(slabs):
            piece = pieces[y][:, pl.ds(r, 1)].astype(F32)
            piece = piece.reshape(HALF, lanes).astype(BF)
            flipped = dot(eye, piece, NT).astype(BF)
            place = lax.rem(idx_ref[1] + y, slabs) * rows + r
            x_ref[pl.ds(place, 1)] = flipped[:XWIN].reshape(1, XWIN, HALF)
            cot_ref[pl.ds(place, 1)] = flipped[XWIN:].reshape(1, CWIN, HALF)
        return carry

    lax.fori_loop(0, rows, one, 0)


def norm_phase(block, xo_ref, xt_ref, gain, nbuf, nk):
    d = DIL[block]
    first_in, width_in = X_WIN[block]
    first_out, width_out = X_WIN[block + 1]
    low = first_out - first_in
    own = 32 - first_in
    for edge in (0, PAD + ROWS):
        nbuf[edge : edge + PAD] = jnp.zeros((PAD, width_out, 3 * CHANS), BF)
        nk[edge : edge + PAD] = jnp.zeros((PAD, OWN, 3 * CHANS), BF)
    n = R_NORM

    def some(r):
        unit, _ = unit_of(widen(flat(xo_ref[pl.ds(r, n)]), flat(xt_ref[pl.ds(r, n)])))
        both = unit * gain
        for kx in range(3):
            shift = (-(kx - 1) * d) % (n * width_in)
            moved = pltpu.roll(both, shift, 0) if shift else both
            moved = moved.reshape(n, width_in, CHANS)
            lanes = slice(kx * CHANS, (kx + 1) * CHANS)
            nbuf[pl.ds(PAD + r, n), :, lanes] = moved[:, low : low + width_out].astype(BF)
            nk[pl.ds(PAD + r, n), :, lanes] = moved[:, own : own + OWN].astype(BF)

    row_loop(some, n)


def conv_phase(block, nbuf, w_ref, pre):
    d = DIL[block]
    width = X_WIN[block + 1][1]
    step = 8

    def one(i, carry):
        r0 = i * step
        acc = None
        for ky in range(3):
            left = nbuf[pl.ds(PAD + r0 + (ky - 1) * d, step)].reshape(step * width, 3 * CHANS)
            term = dot(left, w_ref[:, ky * 3 * CHANS : (ky + 1) * 3 * CHANS], NT)
            acc = term if acc is None else acc + term
        pre[pl.ds(r0, step)] = acc.reshape(step, width, HALF)
        return carry

    lax.fori_loop(0, ROWS // step, one, 0)


def forward_kernel(block, image, pieces, index, idx_ref, xo_ref, xt_ref, *rest):
    w_refs, rest = rest[:pieces], rest[pieces:]
    y_ref, d_ref, gain_ref, nk_far, *rest = rest
    whole = None
    if pieces > 1:
        whole_far, nk, nbuf, pre, sem, w_ref = rest
        lines = HALF // pieces
        for j in range(pieces):
            place = lax.rem(idx_ref[2] + j, pieces) * lines
            w_ref[pl.ds(pl.multiple_of(place, lines), lines)] = w_refs[j][...]
        whole = pltpu.make_async_copy(w_ref, whole_far, sem.at[1])
        whole.start()
    else:
        nk, nbuf, pre, sem, w_ref, tile_ref = rest
        source = w_refs[0] if index is None else w_refs[0].at[index]
        part = pltpu.make_async_copy(source.at[pl.ds(0, 16), pl.ds(LANES, 128)], tile_ref, sem.at[2])
        part.start()
        coming = pltpu.make_async_copy(source, w_ref, sem.at[1])
        coming.start()
        part.wait()
    first_in = X_WIN[block][0]
    first_out, width_out = X_WIN[block + 1]
    first_s, width_s = S_WIN[block]
    gain = read_gain(w_ref) if pieces > 1 else read_gain(tile_ref, 0)
    gain_ref[...] = gain
    norm_phase(block, xo_ref, xt_ref, gain, nbuf, nk)
    if pieces == 1:
        coming.wait()
    kept = pltpu.make_async_copy(nk, nk_far, sem.at[0])
    kept.start()
    conv_phase(block, nbuf, w_ref, pre)
    live = in_image(idx_ref[0], first_out, width_out, image)
    low, at = first_out - first_in, first_s - first_out
    n = R_EPI

    def some(r):
        act = pre[pl.ds(r, n)]
        tangent = gelu_inner(act)
        out = xo_ref[pl.ds(r, n)].astype(F32)[:, low : low + width_out] + 0.5 * act * (1.0 + tangent)
        y_ref[pl.ds(r, n)] = jnp.where(live, out, 0.0).astype(BF)
        d_ref[pl.ds(r, n)] = gelu_slope(act[:, at : at + width_s], tangent[:, at : at + width_s])

    row_loop(some, n)
    kept.wait()
    if whole is not None:
        whole.wait()


def scatter_s(block, s, r, n, sbuf, sown):
    first, width = S_WIN[block]
    rows = s.reshape(n, width, HALF)
    sown[pl.ds(r, n)] = rows[:, 32 - first : 32 - first + OWN].astype(BF)
    if sbuf is None:
        return
    d = DIL[block]
    first_q, width_q = S_WIN[block - 1]
    low = first_q - first
    gap = jnp.zeros((n * width, 256 - HALF), F32)
    wide = jnp.concatenate([s, gap], axis=1)
    for kx in range(3):
        shift = ((kx - 1) * d) % (n * width)
        moved = pltpu.roll(wide, shift, 0) if shift else wide
        moved = moved.reshape(n, width, 256)[:, low : low + width_q]
        sbuf[pl.ds(PAD + r, n), :, kx * 256 : (kx + 1) * 256] = moved.astype(BF)


def q_phase(block, sbuf, w_ref, wq, q_ref):
    d = DIL[block]
    width = S_WIN[block - 1][1]
    for ky in range(3):
        for kx in range(3):
            t = 3 * ky + kx
            wq[ky, kx * 256 : kx * 256 + HALF] = w_ref[:, t * CHANS : (t + 1) * CHANS]
            wq[ky, kx * 256 + HALF : (kx + 1) * 256] = jnp.zeros((256 - HALF, CHANS), BF)
    for edge in (0, PAD + ROWS):
        sbuf[edge : edge + PAD] = jnp.zeros((PAD, width, 768), BF)
    step = 512 // width

    def one(i, carry):
        r0 = i * step
        acc = None
        for ky in range(3):
            left = sbuf[pl.ds(PAD + r0 - (ky - 1) * d, step)].reshape(step * width, 768)
            term = dot(left, wq[ky], NN)
            acc = term if acc is None else acc + term
        q_ref[0, pl.ds(r0, step)] = acc[:, HALF:].reshape(step, width, HALF).astype(BF)
        q_ref[1, pl.ds(r0, step)] = acc[:, :HALF].reshape(step, width, HALF).astype(BF)
        return carry

    lax.fori_loop(0, ROWS // step, one, 0)


def weight_phase(block, dims, idx_ref, sown, nk, w_ref, gain, wg_ref):
    own_chans, share, lines = dims
    d = DIL[block]
    count = (HALF // own_chans) * lines
    bits = lines.bit_length() - 1
    line = lax.broadcasted_iota(jnp.int32, (count, HALF), 0)
    place = jnp.bitwise_and(line, lines - 1)
    want = jnp.right_shift(line, bits) * own_chans + share * idx_ref[1] + place
    pick = (lax.broadcasted_iota(jnp.int32, (count, HALF), 1) == want) & (place < share)
    pick = jnp.where(pick, 1.0, 0.0).astype(BF)
    left = dot(pick, sown[...].reshape(ROWS * OWN, HALF), NT).astype(BF)
    total = jnp.zeros((1, CHANS), F32)
    first = None
    for ky in range(3):
        lanes = slice(ky * 3 * CHANS, (ky + 1) * 3 * CHANS)
        start = PAD + (ky - 1) * d
        right = nk[start : start + ROWS].reshape(ROWS * OWN, 3 * CHANS)
        grads = dot(left, right, NN)
        wg_ref[:, lanes] = grads.astype(BF)
        part = jnp.sum(grads * dot(pick, w_ref[:, lanes], NN), axis=0, keepdims=True)
        for kx in range(3):
            total = total + part[:, kx * CHANS : (kx + 1) * CHANS]
        if ky == 0:
            first = grads[:, :CHANS]
    spot = jnp.bitwise_and(lax.broadcasted_iota(jnp.int32, (count, CHANS), 0), lines - 1)
    wg_ref[:, :CHANS] = jnp.where(spot == share, total / gain, first).astype(BF)


def turn_kernel(dims, index, idx_ref, xo_ref, xt_ref, cot_ref, w_far, q_ref, wg_ref, gain_ref,
                nbuf, nk, pre, sbuf, sown, wq, w_ref, tile_ref, sem):
    source = w_far.at[index]
    part = pltpu.make_async_copy(source.at[pl.ds(0, 16), pl.ds(LANES, 128)], tile_ref, sem.at[0])
    part.start()
    coming = pltpu.make_async_copy(source, w_ref, sem.at[1])
    coming.start()
    part.wait()
    gain = read_gain(tile_ref, 0)
    gain_ref[...] = gain
    norm_phase(3, xo_ref, xt_ref, gain, nbuf, nk)
    coming.wait()
    conv_phase(3, nbuf, w_ref, pre)
    n = R_TURN

    def some(r):
        act = flat(pre[pl.ds(r, n)])
        s = flat(cot_ref[pl.ds(r, n)]).astype(F32) * gelu_slope(act, gelu_inner(act))
        scatter_s(3, s, r, n, sbuf, sown)

    row_loop(some, n)
    q_phase(3, sbuf, w_ref, wq, q_ref)
    weight_phase(3, dims, idx_ref, sown, nk, w_ref, gain, wg_ref)


def backward_kernel(block, dims, image, first_g, index, idx_ref, qm_ref, qr_ref, xo_ref, xt_ref, g_ref,
                    gain_up_ref, d_ref, w_far, nk_far, gain_ref, *rest):
    if block:
        q_ref, gn_ref, wg_ref, w_ref, nk_ref, sem, sown, sbuf, wq = rest
    else:
        wg_ref, w_ref, nk_ref, sem, sown = rest
        q_ref = gn_ref = sbuf = wq = None
    w_far = w_far if index is None else w_far.at[index]
    weights_in = pltpu.make_async_copy(w_far, w_ref, sem.at[0])
    kept_in = pltpu.make_async_copy(nk_far, nk_ref, sem.at[1])
    weights_in.start()
    kept_in.start()
    first, width = S_WIN[block]
    at = first - X_WIN[block + 1][0]
    cut = first - first_g
    live = in_image(idx_ref[0], first, width, image)
    gain_up = gain_up_ref[...]
    n = R_BACK

    def some(r):
        rows = pl.ds(r, n)
        unit, rstd = unit_of(
            widen(flat(xo_ref[rows, at : at + width]), flat(xt_ref[rows, at : at + width]))
        )
        p = gain_up * jnp.concatenate(
            [
                flat(qm_ref[1, rows]).astype(F32) + flat(qr_ref[0, rows]).astype(F32),
                flat(qm_ref[0, rows]).astype(F32) + flat(qr_ref[1, rows]).astype(F32),
            ],
            axis=1,
        )
        change = p[:, :HALF] - chan_mean(p) - unit[:, :HALF] * chan_mean(p * unit)
        g = flat(g_ref[rows, cut : cut + width]).astype(F32) + rstd * change
        g = jnp.where(live, g.reshape(n, width, HALF), 0.0).astype(BF)
        if gn_ref is not None:
            gn_ref[rows] = g
        s = flat(g.astype(F32) * d_ref[rows])
        scatter_s(block, s, r, n, sbuf, sown)

    row_loop(some, n)
    weights_in.wait()
    if block:
        q_phase(block, sbuf, w_ref, wq, q_ref)
    kept_in.wait()
    weight_phase(block, dims, idx_ref, sown, nk_ref, w_ref, gain_ref[...], wg_ref)


def finish_kernel(dims, slabs, all_ref, perm_ref, out_ref):
    own_chans, share, lines = dims
    bits = lines.bit_length() - 1
    col = lax.broadcasted_iota(jnp.int32, (own_chans, slabs * lines), 1)
    place = jnp.bitwise_and(col, lines - 1)
    row = jnp.right_shift(col, bits) * share + place
    pick = (lax.broadcasted_iota(jnp.int32, (own_chans, slabs * lines), 0) == row) & (place < share)
    pick = jnp.where(pick, 1.0, 0.0).astype(BF)
    for t in range(TAPS):
        grads = dot(pick, all_ref[:, t * CHANS : (t + 1) * CHANS], NN).astype(BF)
        out_ref[t] = dot(grads, perm_ref[...], NT)


def local(sizes, x_in, cot, w1, gain):
    nx, nz, ny, ns = sizes
    own_chans, rows = x_in.shape[1], x_in.shape[2]
    image = x_in.shape[3]
    shards = nx * nz
    share = own_chans // ny
    lines = 8
    while lines < share + 1:
        lines *= 2
    dims = (own_chans, share, lines)
    sec, ax, az = lax.axis_index("section"), lax.axis_index("x"), lax.axis_index("zh")
    core, slab = lax.axis_index("core"), lax.axis_index("slab")
    patch = ax * nz + az
    idx = jnp.stack([patch * OWN, slab, ax, sec]).astype(jnp.int32)

    def other(value):
        return lax.ppermute(value, "core", [(0, 1), (1, 0)])

    order = np.arange(CHANS).reshape(shards, 2, own_chans)
    orders = [np.concatenate([order[:, h].ravel(), order[:, 1 - h].ravel()]) for h in (0, 1)]
    perms = np.stack([np.eye(CHANS, dtype=np.float32)[:, o] for o in orders])
    perm = lax.dynamic_index_in_dim(jnp.asarray(perms, BF), core, 0, keepdims=False)

    windows = call(
        window_kernel, shape((shards, rows, own_chans, XWIN + CWIN), BF), [], (idx, x_in, cot), (0,)
    )

    def from_chips(value, axis, size):
        moves = [[(i, (i - j) % size) for i in range(size)] for j in range(1, size)]
        return [value] + [lax.ppermute(value, axis, move) for move in moves]

    packed = call(prep_kernel, shape((own_chans, CARRY), BF), [], (w1[0], gain, perm))
    wide = jnp.broadcast_to(packed[None], (ns * nz, own_chans, CARRY))
    wide = lax.all_to_all(wide, ("section", "zh"), 0, 0, tiled=True)
    wide = wide.reshape(ns, nz * own_chans, CARRY)


    first, second = from_chips(wide[0], "x", nx), from_chips(wide[1], "x", nx)

    windows, wide = lax.optimization_barrier((windows, wide))
    recv = lax.all_to_all(windows, ("x", "zh"), 0, 0, tiled=True)
    row_pieces = from_chips(recv, "slab", ny)
    row_pieces, first, second = lax.optimization_barrier((row_pieces, first, second))
    rest, _ = lax.optimization_barrier((wide[2:], second))
    pair = lax.all_gather(rest, "x", axis=1, tiled=True)
    weights, index = [first, second, [pair], [pair]], [None, None, 0, 1]
    x_own, cot_own = call(
        functools.partial(assemble_kernel, ny, rows),
        (shape((ROWS, XWIN, HALF), BF), shape((ROWS, CWIN, HALF), BF)),
        [],
        (idx, *row_pieces),
        (0,),
    )

    taps3 = 3 * CHANS
    nk_shape = (ROWS + 2 * PAD, OWN, taps3)
    gain_shape = shape((1, CHANS), F32)
    halves, slopes, shifted, gains = [(x_own, other(x_own))], [], [], []
    for b in range(ns - 1):
        width = X_WIN[b + 1][1]
        pieces = len(weights[b])
        many = pieces > 1
        whole_shape = shape((HALF, CARRY), BF)
        y, slope, gain_b, nk, *whole = call(
            functools.partial(forward_kernel, b, image, pieces, index[b]),
            (
                shape((ROWS, width, HALF), BF),
                shape((ROWS, S_WIN[b][1], HALF), F32),
                gain_shape,
                shape(nk_shape, BF),
            )
            + (whole_shape,) * many,
            [
                pltpu.VMEM(nk_shape, BF),
                pltpu.VMEM((ROWS + 2 * PAD, width, taps3), BF),
                pltpu.VMEM((ROWS, width, HALF), F32),
                pltpu.SemaphoreType.DMA((3,)),
                pltpu.VMEM((HALF, CARRY), BF),
            ]
            + [pltpu.VMEM((16, 128), BF)] * (not many),
            (idx, *halves[b], *weights[b]),
            (0,),
            () if many else (3,),
            (3, 4),
            0,
        )
        halves.append((y, other(y)))
        slopes.append(slope)
        shifted.append(nk)
        gains.append(gain_b)
        weights[b] = whole[0] if whole else weights[b][0]

    def back_scratch(b):
        width = S_WIN[b - 1][1]
        return [
            pltpu.VMEM((ROWS + 2 * PAD, width, 768), BF),
            pltpu.VMEM((ROWS, OWN, HALF), BF),
            pltpu.VMEM((3, 768, CHANS), BF),
        ]

    count = shards * lines
    wg_shape = shape((count, TAPS * CHANS), BF)
    width = X_WIN[4][1]
    sbuf_s, sown_s, wq_s = back_scratch(3)
    q, grads, gain_b = call(
        functools.partial(turn_kernel, dims, index[3]),
        (shape((2, ROWS, S_WIN[2][1], HALF), BF), wg_shape, gain_shape),
        [
            pltpu.VMEM((ROWS + 2 * PAD, width, taps3), BF),
            pltpu.VMEM(nk_shape, BF),
            pltpu.VMEM((ROWS, width, HALF), F32),
            sbuf_s,
            sown_s,
            wq_s,
            pltpu.VMEM((HALF, CARRY), BF),
            pltpu.VMEM((16, 128), BF),
            pltpu.SemaphoreType.DMA((2,)),
        ],
        (idx, *halves[3], cot_own, weights[3][0]),
        (0,),
        (4,),
        micros=12,
    )
    gains.append(gain_b)

    def reduced(*values):
        value = jnp.stack([v.reshape(nx, nz * lines, LANES) for v in values], axis=1)
        value = lax.all_to_all(value, "x", 0, 0, tiled=True)
        return jnp.sum(value.astype(F32), axis=0).astype(BF)

    weight_parts = [None] * 3 + [grads]
    g, first_g = cot_own, S_WIN[3][0]
    for b in (2, 1, 0):
        args = (
            idx, q, other(q), *halves[b + 1], g, gains[b + 1], slopes[b], weights[b], shifted[b], gains[b],
        )
        kernel = functools.partial(backward_kernel, b, dims, image, first_g, index[b])
        fetched = [
            pltpu.VMEM((HALF, CARRY), BF),
            pltpu.VMEM(nk_shape, BF),
            pltpu.SemaphoreType.DMA((2,)),
        ]
        if b:
            sbuf_s, sown_s, wq_s = back_scratch(b)
            q, g, grads = call(
                kernel,
                (
                    shape((2, ROWS, S_WIN[b - 1][1], HALF), BF),
                    shape((ROWS, S_WIN[b][1], HALF), BF),
                    wg_shape,
                ),
                fetched + [sown_s, sbuf_s, wq_s],
                args,
                (0,),
                (8, 9),
                micros=8,
            )
        else:
            own_s = pltpu.VMEM((ROWS, OWN, HALF), BF)
            (grads,) = call(kernel, (wg_shape,), fetched + [own_s], args, (0,), (8, 9))
        first_g = S_WIN[b][0]
        weight_parts[b] = grads
        if b == 2:
            late = [reduced(*weight_parts[2:])]
        else:
            late.insert(0, reduced(grads))

    parts = jnp.concatenate(late).reshape(ns * nz, lines, LANES)
    parts = lax.all_to_all(parts, ("section", "zh"), 0, 0, tiled=True)
    total = jnp.sum(parts.astype(F32), axis=0).astype(BF)
    every = lax.all_gather(total, "slab", axis=0, tiled=True)
    weight_grad = call(
        functools.partial(finish_kernel, dims, ny),
        shape((TAPS, own_chans, CHANS), F32),
        [],
        (every, perm),
    )
    gain_rows = every.reshape(ny, lines, LANES)[:, share, :CHANS]
    gain_all = jnp.sum(gain_rows.astype(F32), axis=0)
    here = lax.dynamic_slice_in_dim(gain_all, patch * own_chans, own_chans)
    there = lax.dynamic_slice_in_dim(gain_all, HALF + patch * own_chans, own_chans)
    gain_grad = here + other(there)
    return weight_grad[None], gain_grad[None]


def solution(mesh):
    ns, chans, ny = mesh.shape["section"], mesh.shape["ch"], mesh.shape["slab"]
    nz = 2 if chans % 4 == 0 else 1
    nx = chans // (2 * nz)
    axes = ("section", "x", "zh", "core", "slab")
    fine = Mesh(mesh.devices.reshape(ns, nx, nz, 2, ny), axes)
    ch = ("x", "zh", "core")
    return jax.shard_map(
        functools.partial(local, (nx, nz, ny, ns)),
        mesh=fine,
        in_specs=(
            P(None, ch, "slab", None),
            P(None, ch, "slab", None),
            P("section", None, ch, None),
            P("section", None),
        ),
        out_specs=(P("section", None, ch, None), P("section", ch)),
        check_vma=False,
    )
```

```python
import functools

import jax
import jax.numpy as jnp
import numpy as np
from jax import lax
from jax.experimental import pallas as pl
from jax.experimental.pallas import tpu as pltpu
from jax.sharding import Mesh, PartitionSpec as P

NORM_EPS = 1e-05
SLOPE_SCALE = 0.7978845608028654
CUBIC_COEF = 0.044715
BF = jnp.bfloat16
F32 = jnp.float32

ROWS = 32
CHANS = 384
HALF = 192
TAPS = 9
DIL = (1, 2, 4, 8)
OWN = 16
XWIN = 80
CWIN = 48
PAD = 8
X_WIN = ((0, 80), (0, 80), (0, 80), (8, 64), (16, 48))
S_WIN = ((32, 16), (24, 32), (24, 32), (16, 48))
VMEM_LIMIT = 56 * 1024 * 1024
PARAMS = pltpu.CompilerParams(vmem_limit_bytes=VMEM_LIMIT)
NT = (((1,), (1,)), ((), ()))
NN = (((1,), (0,)), ((), ()))
LANES = TAPS * CHANS
CARRY = LANES + 128
R_NORM, R_EPI, R_TURN, R_BACK = 8, 2, 4, 16


def dot(a, b, dims):
    return lax.dot_general(a, b, dims, preferred_element_type=F32)


def call(kernel, out_shape, scratch, args, smem=(), far=(), far_out=(), micros=2):
    vm = pl.BlockSpec(memory_space=pltpu.VMEM)
    sm = pl.BlockSpec(memory_space=pltpu.SMEM)
    hb = pl.BlockSpec(memory_space=pltpu.HBM)
    if isinstance(out_shape, tuple):
        out_specs = tuple(hb if i in far_out else vm for i in range(len(out_shape)))
    else:
        out_specs = vm
    return pl.pallas_call(
        kernel,
        out_shape=out_shape,
        in_specs=[sm if i in smem else hb if i in far else vm for i in range(len(args))],
        out_specs=out_specs,
        scratch_shapes=scratch,
        compiler_params=PARAMS,
        cost_estimate=pl.CostEstimate(flops=micros * 10**9, bytes_accessed=micros * 10**6, transcendentals=0),
    )(*args)


def shape(dims, dtype):
    return jax.ShapeDtypeStruct(dims, dtype)


def row_loop(body, rows, unroll=1):
    span = rows * unroll

    def step(i, carry):
        for k in range(unroll):
            body(pl.multiple_of(i * span, span) + k * rows)
        return carry

    lax.fori_loop(0, ROWS // span, step, 0)


def flat(value):
    return value.reshape(value.shape[0] * value.shape[1], value.shape[2])


def in_image(base, first, count, width):
    cols = lax.broadcasted_iota(jnp.int32, (1, count, HALF), 1) + (base - 32 + first)
    return (cols >= 0) & (cols < width)


def widen(own, oth):
    return jnp.concatenate([own.astype(F32), oth.astype(F32)], axis=1)


def chan_mean(value):
    folded = value[:, :128] + value[:, 128:256] + value[:, 256:]
    return jnp.sum(folded, axis=1, keepdims=True) / CHANS


def unit_of(value):
    mean = chan_mean(value)
    rstd = lax.rsqrt(chan_mean(value * value) - mean * mean + NORM_EPS)
    return (value - mean) * rstd, rstd


def read_gain(tile_ref, first=LANES):
    tile = tile_ref[0:16, first : first + 128].astype(F32)
    return jnp.concatenate(
        [(tile[p : p + 1] + tile[3 + p : 4 + p]) + tile[6 + p : 7 + p] for p in range(3)], axis=1
    )


def gelu_inner(pre):
    return jnp.tanh(SLOPE_SCALE * (pre + CUBIC_COEF * pre * pre * pre))


def gelu_slope(pre, tangent):
    return 0.5 * (1.0 + tangent) + 0.5 * pre * (1.0 - tangent * tangent) * SLOPE_SCALE * (
        1.0 + 3.0 * CUBIC_COEF * pre * pre
    )


def prep_kernel(idx_ref, w_ref, gain_ref, perms_ref, out_ref, one_ref):
    perm = perms_ref[idx_ref[4]]
    for t in range(TAPS):
        one_ref[:, t * CHANS : (t + 1) * CHANS] = dot(w_ref[t], perm, NN).astype(BF)
    rest = jnp.broadcast_to(gain_ref[...], (8, CHANS))
    row = lax.broadcasted_iota(jnp.int32, (one_ref.shape[0], 128), 0)
    tile = jnp.zeros((one_ref.shape[0], 128), F32)
    for k in range(3):
        piece = rest.astype(BF)
        rest = rest - piece.astype(F32)
        moved = dot(piece, perm, NN)
        for p in range(3):
            tile = jnp.where(row == 3 * k + p, moved[0:1, 128 * p : 128 * p + 128], tile)
    one_ref[:, LANES:CARRY] = tile.astype(BF)
    for copy in range(out_ref.shape[0]):
        out_ref[copy] = one_ref[...]


def window_kernel(idx_ref, x_ref, cot_ref, out_ref):
    shards, rows, chans, lanes = out_ref.shape
    image = x_ref.shape[3]
    x = x_ref[idx_ref[3]].astype(F32)
    cot = cot_ref[idx_ref[3]].astype(F32)
    lane = lax.broadcasted_iota(jnp.int32, (chans, lanes), 1)
    room = jnp.zeros((chans, lanes - image), F32)
    for r in range(rows):
        from_x, from_cot = x[:, r, :], cot[:, r, :]
        if image < lanes:
            from_x = jnp.concatenate([from_x, room], axis=1)
            from_cot = jnp.concatenate([from_cot, room], axis=1)
        for p in range(shards):
            here = None
            for value, start in ((from_x, OWN * p - 32), (from_cot, OWN * p - 16 - XWIN)):
                shift = (-start) % lanes
                moved = pltpu.roll(value, shift, 1) if shift else value
                moved = jnp.where((lane + start >= 0) & (lane + start < image), moved, 0.0)
                here = moved if here is None else jnp.where(lane < XWIN, here, moved)
            out_ref[p, r] = here.astype(BF)


def assemble_kernel(slabs, rows, idx_ref, *refs):
    pieces, (x_ref, cot_ref) = refs[:slabs], refs[slabs:]
    lanes = XWIN + CWIN
    eye = (
        lax.broadcasted_iota(jnp.int32, (lanes, lanes), 0)
        == lax.broadcasted_iota(jnp.int32, (lanes, lanes), 1)
    ).astype(F32).astype(BF)

    def one(r, carry):
        for y in range(slabs):
            piece = pieces[y][:, pl.ds(r, 1)].astype(F32)
            piece = piece.reshape(HALF, lanes).astype(BF)
            flipped = dot(eye, piece, NT).astype(BF)
            place = lax.rem(idx_ref[1] + y, slabs) * rows + r
            x_ref[pl.ds(place, 1)] = flipped[:XWIN].reshape(1, XWIN, HALF)
            cot_ref[pl.ds(place, 1)] = flipped[XWIN:].reshape(1, CWIN, HALF)
        return carry

    lax.fori_loop(0, rows, one, 0)


def norm_phase(block, xo_ref, xt_ref, gain, nbuf, nk):
    d = DIL[block]
    first_in, width_in = X_WIN[block]
    first_out, width_out = X_WIN[block + 1]
    low = first_out - first_in
    own = 32 - first_in
    for edge in (0, PAD + ROWS):
        nbuf[edge : edge + PAD] = jnp.zeros((PAD, width_out, 3 * CHANS), BF)
        nk[edge : edge + PAD] = jnp.zeros((PAD, OWN, 3 * CHANS), BF)
    n = R_NORM

    def some(r):
        unit, _ = unit_of(widen(flat(xo_ref[pl.ds(r, n)]), flat(xt_ref[pl.ds(r, n)])))
        both = unit * gain
        for kx in range(3):
            shift = (-(kx - 1) * d) % (n * width_in)
            moved = pltpu.roll(both, shift, 0) if shift else both
            moved = moved.reshape(n, width_in, CHANS)
            lanes = slice(kx * CHANS, (kx + 1) * CHANS)
            nbuf[pl.ds(PAD + r, n), :, lanes] = moved[:, low : low + width_out].astype(BF)
            nk[pl.ds(PAD + r, n), :, lanes] = moved[:, own : own + OWN].astype(BF)

    row_loop(some, n)


def conv_phase(block, nbuf, w_ref, pre):
    d = DIL[block]
    width = X_WIN[block + 1][1]
    step = 32

    def one(i, carry):
        r0 = i * step
        acc = None
        for ky in range(3):
            left = nbuf[pl.ds(PAD + r0 + (ky - 1) * d, step)].reshape(step * width, 3 * CHANS)
            term = dot(left, w_ref[:, ky * 3 * CHANS : (ky + 1) * 3 * CHANS], NT)
            acc = term if acc is None else acc + term
        pre[pl.ds(r0, step)] = acc.reshape(step, width, HALF)
        return carry

    lax.fori_loop(0, ROWS // step, one, 0)


def forward_kernel(block, image, pieces, index, idx_ref, xo_ref, xt_ref, *rest):
    w_refs, rest = rest[:pieces], rest[pieces:]
    y_ref, d_ref, gain_ref, nk_far, *rest = rest
    whole = None
    if pieces > 1:
        whole_far, nk, nbuf, pre, sem, w_ref = rest
        lines = HALF // pieces
        for j in range(pieces):
            place = lax.rem(idx_ref[2] + j, pieces) * lines
            w_ref[pl.ds(pl.multiple_of(place, lines), lines)] = w_refs[j][...]
        whole = pltpu.make_async_copy(w_ref, whole_far, sem.at[1])
        whole.start()
    else:
        nk, nbuf, pre, sem, w_ref, tile_ref = rest
        source = w_refs[0] if index is None else w_refs[0].at[index]
        part = pltpu.make_async_copy(source.at[pl.ds(0, 16), pl.ds(LANES, 128)], tile_ref, sem.at[2])
        part.start()
        coming = pltpu.make_async_copy(source, w_ref, sem.at[1])
        coming.start()
        part.wait()
    first_in = X_WIN[block][0]
    first_out, width_out = X_WIN[block + 1]
    first_s, width_s = S_WIN[block]
    gain = read_gain(w_ref) if pieces > 1 else read_gain(tile_ref, 0)
    gain_ref[...] = gain
    norm_phase(block, xo_ref, xt_ref, gain, nbuf, nk)
    if pieces == 1:
        coming.wait()
    kept = pltpu.make_async_copy(nk, nk_far, sem.at[0])
    kept.start()
    conv_phase(block, nbuf, w_ref, pre)
    live = in_image(idx_ref[0], first_out, width_out, image)
    low, at = first_out - first_in, first_s - first_out
    n = R_EPI

    def some(r):
        act = pre[pl.ds(r, n)]
        tangent = gelu_inner(act)
        out = xo_ref[pl.ds(r, n)].astype(F32)[:, low : low + width_out] + 0.5 * act * (1.0 + tangent)
        y_ref[pl.ds(r, n)] = jnp.where(live, out, 0.0).astype(BF)
        d_ref[pl.ds(r, n)] = gelu_slope(act[:, at : at + width_s], tangent[:, at : at + width_s])

    row_loop(some, n)
    kept.wait()
    if whole is not None:
        whole.wait()


def scatter_s(block, s, r, n, sbuf, sown):
    first, width = S_WIN[block]
    rows = s.reshape(n, width, HALF)
    sown[pl.ds(r, n)] = rows[:, 32 - first : 32 - first + OWN].astype(BF)
    if sbuf is None:
        return
    d = DIL[block]
    first_q, width_q = S_WIN[block - 1]
    low = first_q - first
    gap = jnp.zeros((n * width, 256 - HALF), F32)
    wide = jnp.concatenate([s, gap], axis=1)
    for kx in range(3):
        shift = ((kx - 1) * d) % (n * width)
        moved = pltpu.roll(wide, shift, 0) if shift else wide
        moved = moved.reshape(n, width, 256)[:, low : low + width_q]
        sbuf[pl.ds(PAD + r, n), :, kx * 256 : (kx + 1) * 256] = moved.astype(BF)


def q_phase(block, sbuf, w_ref, wq, q_ref):
    d = DIL[block]
    width = S_WIN[block - 1][1]
    for ky in range(3):
        for kx in range(3):
            t = 3 * ky + kx
            wq[ky, kx * 256 : kx * 256 + HALF] = w_ref[:, t * CHANS : (t + 1) * CHANS]
            wq[ky, kx * 256 + HALF : (kx + 1) * 256] = jnp.zeros((256 - HALF, CHANS), BF)
    for edge in (0, PAD + ROWS):
        sbuf[edge : edge + PAD] = jnp.zeros((PAD, width, 768), BF)
    step = 512 // width

    def one(i, carry):
        r0 = i * step
        acc = None
        for ky in range(3):
            left = sbuf[pl.ds(PAD + r0 - (ky - 1) * d, step)].reshape(step * width, 768)
            term = dot(left, wq[ky], NN)
            acc = term if acc is None else acc + term
        q_ref[0, pl.ds(r0, step)] = acc[:, HALF:].reshape(step, width, HALF).astype(BF)
        q_ref[1, pl.ds(r0, step)] = acc[:, :HALF].reshape(step, width, HALF).astype(BF)
        return carry

    lax.fori_loop(0, ROWS // step, one, 0)


def weight_phase(block, dims, idx_ref, sown, nk, w_ref, gain, wg_ref):
    own_chans, share, lines = dims
    d = DIL[block]
    count = (HALF // own_chans) * lines
    bits = lines.bit_length() - 1
    line = lax.broadcasted_iota(jnp.int32, (count, HALF), 0)
    place = jnp.bitwise_and(line, lines - 1)
    want = jnp.right_shift(line, bits) * own_chans + share * idx_ref[1] + place
    pick = (lax.broadcasted_iota(jnp.int32, (count, HALF), 1) == want) & (place < share)
    pick = jnp.where(pick, 1.0, 0.0).astype(BF)
    left = dot(pick, sown[...].reshape(ROWS * OWN, HALF), NT).astype(BF)
    total = jnp.zeros((1, CHANS), F32)
    first = None
    for ky in range(3):
        lanes = slice(ky * 3 * CHANS, (ky + 1) * 3 * CHANS)
        start = PAD + (ky - 1) * d
        right = nk[start : start + ROWS].reshape(ROWS * OWN, 3 * CHANS)
        grads = dot(left, right, NN)
        wg_ref[:, lanes] = grads.astype(BF)
        part = jnp.sum(grads * dot(pick, w_ref[:, lanes], NN), axis=0, keepdims=True)
        for kx in range(3):
            total = total + part[:, kx * CHANS : (kx + 1) * CHANS]
        if ky == 0:
            first = grads[:, :CHANS]
    spot = jnp.bitwise_and(lax.broadcasted_iota(jnp.int32, (count, CHANS), 0), lines - 1)
    wg_ref[:, :CHANS] = jnp.where(spot == share, total / gain, first).astype(BF)


def turn_kernel(dims, index, idx_ref, xo_ref, xt_ref, cot_ref, w_far, q_ref, wg_ref, gain_ref,
                nbuf, nk, pre, sbuf, sown, wq, w_ref, tile_ref, sem):
    source = w_far.at[index]
    part = pltpu.make_async_copy(source.at[pl.ds(0, 16), pl.ds(LANES, 128)], tile_ref, sem.at[0])
    part.start()
    coming = pltpu.make_async_copy(source, w_ref, sem.at[1])
    coming.start()
    part.wait()
    gain = read_gain(tile_ref, 0)
    gain_ref[...] = gain
    norm_phase(3, xo_ref, xt_ref, gain, nbuf, nk)
    coming.wait()
    conv_phase(3, nbuf, w_ref, pre)
    n = R_TURN

    def some(r):
        act = flat(pre[pl.ds(r, n)])
        s = flat(cot_ref[pl.ds(r, n)]).astype(F32) * gelu_slope(act, gelu_inner(act))
        scatter_s(3, s, r, n, sbuf, sown)

    row_loop(some, n)
    q_phase(3, sbuf, w_ref, wq, q_ref)
    weight_phase(3, dims, idx_ref, sown, nk, w_ref, gain, wg_ref)


def backward_kernel(block, dims, image, first_g, index, idx_ref, qm_ref, qr_ref, xo_ref, xt_ref, g_ref,
                    gain_up_ref, d_ref, w_far, nk_far, gain_ref, *rest):
    if block:
        q_ref, gn_ref, wg_ref, w_ref, nk_ref, sem, sown, sbuf, wq = rest
    else:
        wg_ref, w_ref, nk_ref, sem, sown = rest
        q_ref = gn_ref = sbuf = wq = None
    w_far = w_far if index is None else w_far.at[index]
    weights_in = pltpu.make_async_copy(w_far, w_ref, sem.at[0])
    kept_in = pltpu.make_async_copy(nk_far, nk_ref, sem.at[1])
    weights_in.start()
    kept_in.start()
    first, width = S_WIN[block]
    at = first - X_WIN[block + 1][0]
    cut = first - first_g
    live = in_image(idx_ref[0], first, width, image)
    gain_up = gain_up_ref[...]
    n = R_BACK

    def some(r):
        rows = pl.ds(r, n)
        unit, rstd = unit_of(
            widen(flat(xo_ref[rows, at : at + width]), flat(xt_ref[rows, at : at + width]))
        )
        p = gain_up * jnp.concatenate(
            [
                flat(qm_ref[1, rows]).astype(F32) + flat(qr_ref[0, rows]).astype(F32),
                flat(qm_ref[0, rows]).astype(F32) + flat(qr_ref[1, rows]).astype(F32),
            ],
            axis=1,
        )
        change = p[:, :HALF] - chan_mean(p) - unit[:, :HALF] * chan_mean(p * unit)
        g = flat(g_ref[rows, cut : cut + width]).astype(F32) + rstd * change
        g = jnp.where(live, g.reshape(n, width, HALF), 0.0).astype(BF)
        if gn_ref is not None:
            gn_ref[rows] = g
        s = flat(g.astype(F32) * d_ref[rows])
        scatter_s(block, s, r, n, sbuf, sown)

    row_loop(some, n)
    weights_in.wait()
    if block:
        q_phase(block, sbuf, w_ref, wq, q_ref)
    kept_in.wait()
    weight_phase(block, dims, idx_ref, sown, nk_ref, w_ref, gain_ref[...], wg_ref)


def finish_kernel(dims, slabs, idx_ref, all_ref, perms_ref, out_ref):
    perm = perms_ref[idx_ref[4]]
    own_chans, share, lines = dims
    bits = lines.bit_length() - 1
    col = lax.broadcasted_iota(jnp.int32, (own_chans, slabs * lines), 1)
    place = jnp.bitwise_and(col, lines - 1)
    row = jnp.right_shift(col, bits) * share + place
    pick = (lax.broadcasted_iota(jnp.int32, (own_chans, slabs * lines), 0) == row) & (place < share)
    pick = jnp.where(pick, 1.0, 0.0).astype(BF)
    for t in range(TAPS):
        grads = dot(pick, all_ref[:, t * CHANS : (t + 1) * CHANS], NN).astype(BF)
        out_ref[t] = dot(grads, perm, NT)


def local(sizes, x_in, cot, w1, gain):
    nx, nz, ny, ns = sizes
    own_chans, rows = x_in.shape[1], x_in.shape[2]
    image = x_in.shape[3]
    shards = nx * nz
    share = own_chans // ny
    lines = 8
    while lines < share + 1:
        lines *= 2
    dims = (own_chans, share, lines)
    sec, ax, az = lax.axis_index("section"), lax.axis_index("x"), lax.axis_index("zh")
    core, slab = lax.axis_index("core"), lax.axis_index("slab")
    patch = ax * nz + az
    idx = jnp.stack([patch * OWN, slab, ax, sec, core]).astype(jnp.int32)

    def other(value):
        return lax.ppermute(value, "core", [(0, 1), (1, 0)])

    order = np.arange(CHANS).reshape(shards, 2, own_chans)
    orders = [np.concatenate([order[:, h].ravel(), order[:, 1 - h].ravel()]) for h in (0, 1)]
    perms = np.stack([np.eye(CHANS, dtype=np.float32)[:, o] for o in orders])
    perms = jnp.asarray(perms, BF)

    windows = call(
        window_kernel, shape((shards, rows, own_chans, XWIN + CWIN), BF), [], (idx, x_in, cot), (0,)
    )

    def from_chips(value, axis, size):
        moves = [[(i, (i - j) % size) for i in range(size)] for j in range(1, size)]
        return [value] + [lax.ppermute(value, axis, move) for move in moves]

    wide = call(
        prep_kernel,
        shape((ns * nz, own_chans, CARRY), BF),
        [pltpu.VMEM((own_chans, CARRY), BF)],
        (idx, w1[0], gain, perms),
        (0,),
    )
    wide = lax.all_to_all(wide, ("section", "zh"), 0, 0, tiled=True)
    wide = wide.reshape(ns, nz * own_chans, CARRY)


    first, second = from_chips(wide[0], "x", nx), from_chips(wide[1], "x", nx)

    windows, wide = lax.optimization_barrier((windows, wide))
    recv = lax.all_to_all(windows, ("x", "zh"), 0, 0, tiled=True)
    row_pieces = from_chips(recv, "slab", ny)
    row_pieces, first, second = lax.optimization_barrier((row_pieces, first, second))
    rest, _ = lax.optimization_barrier((wide[2:], second))
    pair = lax.all_gather(rest, "x", axis=1, tiled=True)
    weights, index = [first, second, [pair], [pair]], [None, None, 0, 1]
    x_own, cot_own = call(
        functools.partial(assemble_kernel, ny, rows),
        (shape((ROWS, XWIN, HALF), BF), shape((ROWS, CWIN, HALF), BF)),
        [],
        (idx, *row_pieces),
        (0,),
    )

    taps3 = 3 * CHANS
    nk_shape = (ROWS + 2 * PAD, OWN, taps3)
    gain_shape = shape((1, CHANS), F32)
    halves, slopes, shifted, gains = [(x_own, other(x_own))], [], [], []
    for b in range(ns - 1):
        width = X_WIN[b + 1][1]
        pieces = len(weights[b])
        many = pieces > 1
        whole_shape = shape((HALF, CARRY), BF)
        y, slope, gain_b, nk, *whole = call(
            functools.partial(forward_kernel, b, image, pieces, index[b]),
            (
                shape((ROWS, width, HALF), BF),
                shape((ROWS, S_WIN[b][1], HALF), F32),
                gain_shape,
                shape(nk_shape, BF),
            )
            + (whole_shape,) * many,
            [
                pltpu.VMEM(nk_shape, BF),
                pltpu.VMEM((ROWS + 2 * PAD, width, taps3), BF),
                pltpu.VMEM((ROWS, width, HALF), F32),
                pltpu.SemaphoreType.DMA((3,)),
                pltpu.VMEM((HALF, CARRY), BF),
            ]
            + [pltpu.VMEM((16, 128), BF)] * (not many),
            (idx, *halves[b], *weights[b]),
            (0,),
            () if many else (3,),
            (3, 4),
            0,
        )
        halves.append((y, other(y)))
        slopes.append(slope)
        shifted.append(nk)
        gains.append(gain_b)
        weights[b] = whole[0] if whole else weights[b][0]

    def back_scratch(b):
        width = S_WIN[b - 1][1]
        return [
            pltpu.VMEM((ROWS + 2 * PAD, width, 768), BF),
            pltpu.VMEM((ROWS, OWN, HALF), BF),
            pltpu.VMEM((3, 768, CHANS), BF),
        ]

    count = shards * lines
    wg_shape = shape((count, TAPS * CHANS), BF)
    width = X_WIN[4][1]
    sbuf_s, sown_s, wq_s = back_scratch(3)
    q, grads, gain_b = call(
        functools.partial(turn_kernel, dims, index[3]),
        (shape((2, ROWS, S_WIN[2][1], HALF), BF), wg_shape, gain_shape),
        [
            pltpu.VMEM((ROWS + 2 * PAD, width, taps3), BF),
            pltpu.VMEM(nk_shape, BF),
            pltpu.VMEM((ROWS, width, HALF), F32),
            sbuf_s,
            sown_s,
            wq_s,
            pltpu.VMEM((HALF, CARRY), BF),
            pltpu.VMEM((16, 128), BF),
            pltpu.SemaphoreType.DMA((2,)),
        ],
        (idx, *halves[3], cot_own, weights[3][0]),
        (0,),
        (4,),
        micros=12,
    )
    gains.append(gain_b)

    def reduced(*values):
        value = jnp.stack([v.reshape(nx, nz * lines, LANES) for v in values], axis=1)
        value = lax.all_to_all(value, "x", 0, 0, tiled=True)
        return jnp.sum(value.astype(F32), axis=0).astype(BF)

    weight_parts = [None] * 3 + [grads]
    g, first_g = cot_own, S_WIN[3][0]
    for b in (2, 1, 0):
        args = (
            idx, q, other(q), *halves[b + 1], g, gains[b + 1], slopes[b], weights[b], shifted[b], gains[b],
        )
        kernel = functools.partial(backward_kernel, b, dims, image, first_g, index[b])
        fetched = [
            pltpu.VMEM((HALF, CARRY), BF),
            pltpu.VMEM(nk_shape, BF),
            pltpu.SemaphoreType.DMA((2,)),
        ]
        if b:
            sbuf_s, sown_s, wq_s = back_scratch(b)
            q, g, grads = call(
                kernel,
                (
                    shape((2, ROWS, S_WIN[b - 1][1], HALF), BF),
                    shape((ROWS, S_WIN[b][1], HALF), BF),
                    wg_shape,
                ),
                fetched + [sown_s, sbuf_s, wq_s],
                args,
                (0,),
                (8, 9),
                micros=8,
            )
        else:
            own_s = pltpu.VMEM((ROWS, OWN, HALF), BF)
            (grads,) = call(kernel, (wg_shape,), fetched + [own_s], args, (0,), (8, 9))
        first_g = S_WIN[b][0]
        weight_parts[b] = grads
        if b == 2:
            late = [reduced(*weight_parts[2:])]
        else:
            late.insert(0, reduced(grads))

    parts = jnp.concatenate(late).reshape(ns * nz, lines, LANES)
    parts = lax.all_to_all(parts, ("section", "zh"), 0, 0, tiled=True)
    total = jnp.sum(parts.astype(F32), axis=0).astype(BF)
    every = lax.all_gather(total, "slab", axis=0, tiled=True)
    weight_grad = call(
        functools.partial(finish_kernel, dims, ny),
        shape((TAPS, own_chans, CHANS), F32),
        [],
        (idx, every, perms),
        (0,),
    )
    gain_rows = every.reshape(ny, lines, LANES)[:, share, :CHANS]
    gain_all = jnp.sum(gain_rows.astype(F32), axis=0)
    here = lax.dynamic_slice_in_dim(gain_all, patch * own_chans, own_chans)
    there = lax.dynamic_slice_in_dim(gain_all, HALF + patch * own_chans, own_chans)
    gain_grad = here + other(there)
    return weight_grad[None], gain_grad[None]


def solution(mesh):
    ns, chans, ny = mesh.shape["section"], mesh.shape["ch"], mesh.shape["slab"]
    nz = 2 if chans % 4 == 0 else 1
    nx = chans // (2 * nz)
    axes = ("section", "x", "zh", "core", "slab")
    fine = Mesh(mesh.devices.reshape(ns, nx, nz, 2, ny), axes)
    ch = ("x", "zh", "core")
    return jax.shard_map(
        functools.partial(local, (nx, nz, ny, ns)),
        mesh=fine,
        in_specs=(
            P(None, ch, "slab", None),
            P(None, ch, "slab", None),
            P("section", None, ch, None),
            P("section", None),
        ),
        out_specs=(P("section", None, ch, None), P("section", ch)),
        check_vma=False,
    )
```
